128 devices in a mesh: tile: 8 (over x, core), tm: 4 (over y), plane: 4 (over z).
Axes of the slice: x: 4, y: 4, z: 4, core: 2. Of those that a mesh axis runs over, the one named last changes fastest.
Arguments:
- movie: bfloat16 [8192, 128, 512], P(('tile', 'plane'), None, 'tm'), may hold values from -6 to 6
- footprint: bfloat16 [32768, 128], P(('tile', 'plane')), may hold values from 0 to 0.5
- entry_block: int32 [32768], P(('tile', 'plane')), may hold values from 0 to 255
- entry_owner: int32 [32768, 1], P(('tile', 'plane')), may hold values from 0 to 31; in each aligned block of 1024 rows (0 to 1023, 1024 to 2047, ...) at most 96 rows name the same one
- entry_slot: int32 [32768], P(('tile', 'plane')), may hold values from 0 to 255
- traces: float32 [8192, 512], P(('tile', 'plane'), 'tm'), may hold values from -6 to 6
- slow_root: float32 [8192], P(('tile', 'plane')), may hold values from 0.9 to 0.995
- fast_root: float32 [8192], P(('tile', 'plane')), may hold values from 0.2 to 0.7
Outputs:
- reconstruction: bfloat16 [8192, 128, 512], P(('tile', 'plane'), None, 'tm')
- calcium: float32 [8192, 512], P(('tile', 'plane'), 'tm')
The draws below stay inside these ranges and needn't reach their ends.
Inputs may be any that keep to these rules, and one draw needn't show every extreme that they name: `entry_owner`: among the 1024 footprint blocks of one device, at most 96 name one owner, a bound that some block reaches.
All inputs are finite; a program needn't handle non-finite values.
Results may differ from the reference program's by a relative error of at most 0.0038.
Values sent between devices are 32-bit elements; how exact they have to be, the bound alone decides.
A program may use at most 128 MiB of HBM per device.

```python
import math
import jax
import jax.numpy as jnp
import numpy as np
from jax import lax

VOX = 128
BLK_DEV = 256
ENT_DEV = 1024
K_DEV = 256
SWEEPS = 4
CAP = 96
BLOCKS = 8192
ENTRIES = 32768
NEURONS = 8192
FRAMES = 512
N_TILE = 8
N_PLANE = 4


def with_ends(drawn, stream_key, smallest, largest):
    longest = drawn.shape.index(max(drawn.shape))
    spots = []
    for shift in (0, 1):
        where = [jax.random.randint(jax.random.fold_in(stream_key, axis), (), 0, length) for axis, length in enumerate(drawn.shape)]
        where[longest] = (where[longest] + shift) % drawn.shape[longest]
        spots.append(tuple(where))
    return drawn.at[spots[0]].set(smallest).at[spots[1]].set(largest)


def shard_levels(key, shape, shards, low, largest):
    def one(dim, blocks):
        heights = jax.random.uniform(jax.random.fold_in(jax.random.fold_in(key, 6), dim), (blocks,), jnp.float32, low / len(shards), largest / len(shards))
        return jnp.repeat(jnp.exp(heights), shape[dim] // blocks).reshape((-1,) + (1,) * (len(shape) - dim - 1))

    gain = one(*shards[0])
    for cut in shards[1:]:
        gain = gain * one(*cut)
    return gain


def assign_block(key, own, number, rows, count, top, reach, slope):
    order = jax.random.permutation(key, count)
    heavy_load, usual = load_shares(count, rows * top, reach, slope, True), load_shares(count, rows * top, reach, slope, False)
    places = jnp.arange(count)

    def named(tallies, offset_by):
        used = int((tallies > 0).sum())
        fixed = max(1, used // 4)
        moved = fixed + (places - fixed + offset_by * (used - fixed)) % max(1, count - fixed)
        return jnp.zeros((count,), jnp.int32).at[order[jnp.where(places < fixed, places, moved)]].set(jnp.asarray(tallies, jnp.int32))

    tallies = jnp.where(number % 4 == 0, named(heavy_load, number // 4), named(usual, number - number // 4 - 1))
    mixed = jax.random.permutation(jax.random.fold_in(own, 3), count)
    donor, sink = mixed[0:count // 2 * 2:2], mixed[1:count // 2 * 2:2]
    room = jnp.minimum(tallies[donor] - 1, reach - tallies[sink]) // 2
    room = jnp.where((donor == order[0]) | (sink == order[0]) | (tallies[sink] == 0), 0, jnp.maximum(room, 0))
    moved = jax.random.randint(jax.random.fold_in(own, 4), (count // 2,), 0, 1 << 20) % (room + 1)
    tallies = tallies.at[donor].add(-moved).at[sink].add(moved)
    items = jnp.searchsorted(jnp.cumsum(tallies), jnp.arange(rows * top), side="right").astype(jnp.int32)
    grid = items.reshape(top, rows).T
    grid = grid[jax.random.permutation(jax.random.fold_in(own, 1), rows)]
    offset_by = jax.random.randint(jax.random.fold_in(own, 2), (rows, 1), 0, top)
    return jnp.take_along_axis(grid, (jnp.arange(top)[None, :] + offset_by) % top, axis=1)


def load_shares(count, total, bound, lean, full):
    loads = [(1 << 20) // math.isqrt(standing ** lean) + 1 for standing in range(1, count + 1)]
    largest = bound if full else min(bound, max(-(-total // count), total * loads[0] // sum(loads)))
    least = 1 if total - largest >= count - 1 else 0
    counts, surplus = [largest] + [least] * (count - 1), total - largest - least * (count - 1)
    while surplus > 0:
        candidates = [i for i in range(1, count) if counts[i] < largest] or [i for i in range(1, count) if counts[i] < bound]
        mass, remaining = sum([loads[i] for i in candidates]), surplus
        for i in candidates:
            addition = min(bound - counts[i], max(1, remaining * loads[i] // mass), surplus)
            counts[i] = counts[i] + addition
            surplus = surplus - addition
    return np.array(counts)


def bell_draw(key, shape, deviation, bound, shards=(), held_as=jnp.bfloat16):
    loudness = shard_levels(key, shape, shards, -0.22, 0.18) if shards else 1.0
    drawn = jax.random.normal(key, shape, jnp.float32) * deviation * loudness
    return jnp.minimum(jnp.maximum(drawn, -bound), bound).astype(held_as)


def setup_inputs(seed: int = 0) -> dict:
    key_list = jax.random.split(jax.random.key(seed), 9)
    movie = bell_draw(key_list[0], (BLOCKS, VOX, FRAMES), 1.0, 6.0, ((0, 32), (2, 4)))
    footprint = jnp.clip(0.5 * jax.random.uniform(key_list[1], (ENTRIES, VOX), jnp.float32) ** shard_levels(key_list[1], (ENTRIES, VOX), ((0, 32),), -0.2, 0.2), 0.0, 0.5).astype(jnp.bfloat16)
    entry_block = with_ends(jax.random.randint(key_list[2], (ENTRIES,), 0, BLK_DEV), jax.random.fold_in(key_list[2], 1), 0, BLK_DEV - 1).astype(jnp.int32)
    entry_owner_keys = jax.random.split(jax.random.fold_in(key_list[3], 1), ENTRIES // ENT_DEV)
    entry_owner_turns = jax.random.permutation(jax.random.fold_in(key_list[3], 3), ENTRIES // ENT_DEV)
    entry_owner = jax.vmap(lambda own, number: assign_block(jax.random.fold_in(key_list[3], 2), own, number, ENT_DEV, N_TILE * N_PLANE, 1, CAP, 2))(entry_owner_keys, entry_owner_turns).reshape((ENTRIES, 1))
    entry_slot = with_ends(jax.random.randint(key_list[4], (ENTRIES,), 0, K_DEV), jax.random.fold_in(key_list[4], 1), 0, K_DEV - 1).astype(jnp.int32)
    traces = bell_draw(key_list[5], (NEURONS, FRAMES), 1.0, 6.0, ((0, 32), (1, 4)), jnp.float32)
    slow_root = jnp.clip(0.9 + 0.09500003 * jax.random.uniform(key_list[6], (NEURONS,), jnp.float32) ** shard_levels(key_list[6], (NEURONS,), ((0, 32),), -0.2, 0.2), 0.9, 0.995)
    fast_root = jnp.clip(0.2 + 0.5 * jax.random.uniform(key_list[7], (NEURONS,), jnp.float32) ** shard_levels(key_list[7], (NEURONS,), ((0, 32),), -0.2, 0.2), 0.2, 0.7)
    return dict(movie=movie, footprint=footprint, entry_block=entry_block, entry_owner=entry_owner, entry_slot=entry_slot, traces=traces, slow_root=slow_root, fast_root=fast_root)


def reference(movie, footprint, entry_block, entry_owner, entry_slot, traces, slow_root, fast_root):
    owners = N_TILE * N_PLANE
    neuron = entry_owner[:, 0] * K_DEV + entry_slot
    foot_values = footprint.astype(jnp.float32)

    def device_terms(device):
        blocks = lax.dynamic_slice_in_dim(movie, device * BLK_DEV, BLK_DEV, 0)
        values = lax.dynamic_slice_in_dim(foot_values, device * ENT_DEV, ENT_DEV, 0)
        local_ids = lax.dynamic_slice_in_dim(entry_block, device * ENT_DEV, ENT_DEV, 0)
        picked = jnp.take(blocks, local_ids, axis=0).astype(jnp.float32)
        return jnp.einsum('ev,evf->ef', values, picked)

    projected = lax.map(device_terms, jnp.arange(owners, dtype=jnp.int32)).reshape(ENTRIES, FRAMES)
    summed = jax.ops.segment_sum(projected, neuron, num_segments=NEURONS)
    energy = jax.ops.segment_sum(jnp.sum(foot_values * foot_values, axis=1), neuron, num_segments=NEURONS)
    target = (summed + traces) / (energy[:, None] + 1.0)
    lag_one = slow_root + fast_root
    lag_two = -slow_root * fast_root

    def filtered(spikes):
        def advance(state, column):
            value = column + lag_one * state[0] + lag_two * state[1]
            return (value, state[0]), value
        zeros = jnp.zeros((NEURONS,), jnp.float32)
        _, values = lax.scan(advance, (zeros, zeros), spikes.T)
        return values.T

    estimate = target
    for sweep_index in range(SWEEPS):
        padded = jnp.pad(estimate, ((0, 0), (2, 0)))
        spikes = jnp.maximum(estimate - lag_one[:, None] * padded[:, 1:-1] - lag_two[:, None] * padded[:, :-2], 0.0)
        calcium = filtered(spikes)
        if sweep_index + 1 < SWEEPS:
            estimate = 0.5 * (target + calcium)

    calcium_rounded = calcium.astype(jnp.bfloat16).astype(jnp.float32)

    def device_blocks(device):
        values = lax.dynamic_slice_in_dim(foot_values, device * ENT_DEV, ENT_DEV, 0)
        local_ids = lax.dynamic_slice_in_dim(entry_block, device * ENT_DEV, ENT_DEV, 0)
        owned = lax.dynamic_slice_in_dim(neuron, device * ENT_DEV, ENT_DEV, 0)
        rows_of = jnp.take(calcium_rounded, owned, axis=0)
        outer_terms = values[:, :, None] * rows_of[:, None, :]
        return jax.ops.segment_sum(outer_terms, local_ids, num_segments=BLK_DEV)

    rebuilt = lax.map(device_blocks, jnp.arange(owners, dtype=jnp.int32)).reshape(BLOCKS, VOX, FRAMES)
    return rebuilt.astype(jnp.bfloat16), calcium
```

```python
import jax
import jax.numpy as jnp
from jax import lax
from jax.experimental import pallas as pl
from jax.experimental.pallas import tpu as pltpu
from jax.sharding import PartitionSpec as P

SWEEPS = 4
CAP = 96
OWN = 256
ENT = 1024
VOX = 128
FR = 128
BLK = 256
MSG = 4 * CAP
ROWS = MSG + 8
SUB = OWN // 4
PIECE = SUB + 8
MESH = pl.DeviceIdType.MESH
F32 = jnp.float32
BF16 = jnp.bfloat16
VMEM = pl.BlockSpec(memory_space=pltpu.VMEM)
SMEM = pl.BlockSpec(memory_space=pltpu.SMEM)
NT = (((1,), (1,)), ((), ()))
TN = (((0,), (0,)), ((), ()))


def iota(shape, axis):
    return lax.broadcasted_iota(jnp.int32, shape, axis)


def split(value):
    high = value.astype(BF16)
    return high, (value - high.astype(F32)).astype(BF16)


def gather_kernel(
    movie_hbm, foot, block_s, block, owner, slot,
    send, pos_out, rank_out, foot_sorted, block_sorted, starts,
    movie, pos_s, sem,
):
    load = pltpu.make_async_copy(movie_hbm, movie, sem.at[0])
    load.start()
    send[...] = jnp.zeros_like(send)
    blk, own, slt = block[...], owner[...], slot[...]
    entry = iota((8, 128), 0) * 128 + iota((8, 128), 1)
    key = (blk * ENT + entry).astype(F32)
    ownf = own.astype(F32)
    key_col, own_col = key.T, ownf.T
    before = iota((128, 128), 0) < iota((128, 128), 1)
    owner_rank, block_rank = [], []
    for row in range(8):
        key_row, own_row = key[row : row + 1, :], ownf[row : row + 1, :]
        count_o = jnp.zeros((128, 128), F32)
        count_k = jnp.zeros((128, 128), F32)
        for col in range(8):
            count_k += jnp.where(key_col[:, col : col + 1] < key_row, 1.0, 0.0)
            if col <= row:
                same = own_col[:, col : col + 1] == own_row
                if col == row:
                    same = same & before
                count_o += jnp.where(same, 1.0, 0.0)
        owner_rank.append(jnp.sum(count_o, axis=0, keepdims=True))
        block_rank.append(jnp.sum(count_k, axis=0, keepdims=True))
    rank = jnp.concatenate(owner_rank, axis=0).astype(jnp.int32)
    order = jnp.concatenate(block_rank, axis=0).astype(jnp.int32)
    core, far, near = (own >> 2) & 1, own >> 3, own & 3
    message = jnp.where(core == 0, far, 4 + near)
    member = jnp.where(core == 0, near, far)
    pos = message * ROWS + member * CAP + rank
    pos_out[...] = pos
    rank_out[...] = order
    to_smem = pltpu.make_async_copy(pos_out, pos_s, sem.at[1])
    to_smem.start()

    foot_values = foot[...].astype(F32)
    sq_high, sq_low = split(foot_values * foot_values)
    ones = jnp.ones((8, 128), BF16)
    energy = lax.dot_general(ones, sq_high, NT, preferred_element_type=F32) + lax.dot_general(
        ones, sq_low, NT, preferred_element_type=F32
    )
    place = member * 128 + rank
    meta = jnp.zeros((24, 512), F32)
    sorted_wide = jnp.zeros((ENT, 256), F32)
    blkf_col = blk.astype(F32).T
    less = jnp.zeros((128, 128), F32)
    lane8 = (iota((128, 128), 1) * 8).astype(F32)
    for row in range(8):
        lanes = slice(row * 128, row * 128 + 128)
        chosen = message[row : row + 1, :] == iota((8, 128), 0)
        en_high, en_low = split(energy[:, lanes])
        slots = (slt[row : row + 1, :] + 1).astype(F32)
        values = jnp.concatenate(
            [
                jnp.where(chosen, slots, 0.0),
                jnp.where(chosen, en_high.astype(F32), 0.0),
                jnp.where(chosen, en_low.astype(F32), 0.0),
            ],
            axis=0,
        ).astype(BF16)
        places = jnp.where(place[row : row + 1, :] == iota((512, 128), 0), 1.0, 0.0).astype(BF16)
        meta += lax.dot_general(values, places, NT, preferred_element_type=F32)
        permute = jnp.where(order[row : row + 1, :] == iota((ENT, 128), 0), 1.0, 0.0).astype(BF16)
        column = blkf_col[:, row : row + 1]
        wide = jnp.concatenate(
            [foot[lanes, :], jnp.broadcast_to(column, (128, 128)).astype(BF16)], axis=1
        )
        sorted_wide += jnp.dot(permute, wide, preferred_element_type=F32)
        less += jnp.where(column < lane8, 1.0, 0.0)
    foot_sorted[...] = sorted_wide[:, :128].astype(BF16)
    block_sorted[...] = sorted_wide[:, 128:]
    starts[...] = jnp.broadcast_to(jnp.sum(less, axis=0, keepdims=True), (8, 128)).astype(jnp.int32)
    for m in range(8):
        for i in range(4):
            lanes = slice(i * 128, i * 128 + 128)
            base = m * ROWS + MSG
            send[base + i : base + i + 1, :] = meta[m : m + 1, lanes]
            send[base + 4 + i : base + 5 + i, :] = (
                meta[8 + m : 9 + m, lanes] + meta[16 + m : 17 + m, lanes]
            )
    to_smem.wait()
    load.wait()
    diagonal = iota((16, 128), 0)

    @pl.loop(0, ENT // 16)
    def _(group):
        first = group * 16
        values = foot[pl.ds(pl.multiple_of(first, 16), 16), :].astype(F32)
        left = jnp.concatenate(
            [jnp.where(diagonal == i, values, 0.0) for i in range(16)], axis=1
        ).astype(BF16)
        right = jnp.concatenate([movie[block_s[first + i]] for i in range(16)], axis=0)
        out = jnp.dot(left, right, preferred_element_type=F32)
        for i in range(16):
            send[pl.ds(pos_s[group // 8, lax.rem(group, 8) * 16 + i], 1), :] = out[i : i + 1, :]


def gather(movie, footprint, entry_block, entry_owner, entry_slot):
    shape = jax.ShapeDtypeStruct
    return pl.pallas_call(
        gather_kernel,
        out_shape=(
            shape((8 * ROWS, FR), F32),
            shape((8, 128), jnp.int32),
            shape((8, 128), jnp.int32),
            shape((ENT, VOX), BF16),
            shape((ENT, 128), F32),
            shape((8, 128), jnp.int32),
        ),
        in_specs=[pl.BlockSpec(memory_space=pl.ANY), VMEM, SMEM, VMEM, VMEM, VMEM],
        out_specs=(VMEM,) * 6,
        scratch_shapes=[
            pltpu.VMEM((BLK, VOX, FR), BF16),
            pltpu.SMEM((8, 128), jnp.int32),
            pltpu.SemaphoreType.DMA((2,)),
        ],
        compiler_params=pltpu.CompilerParams(vmem_limit_bytes=48 << 20),
        name="project",
    )(
        movie, footprint, entry_block, entry_block.reshape(8, 128),
        entry_owner.reshape(8, 128), entry_slot.reshape(8, 128),
    )


def pick(rows, sub):
    chosen = jnp.where(sub // 2 == 0, rows[0:1, :], rows[1:2, :])
    lane = iota((SUB, 128), 1) - lax.rem(sub, 2) * SUB
    return jnp.sum(jnp.where(lane == iota((SUB, 128), 0), chosen, 0.0), axis=1, keepdims=True)


def delayed(parts, steps):
    if steps >= 128:
        hop = steps // 128
        return [None] * hop + parts[: len(parts) - hop]
    lane = iota((SUB, 128), 1)
    rolled = [pltpu.roll(part, steps, 1) for part in parts]
    out = [jnp.where(lane < steps, 0.0, rolled[0])]
    for index in range(1, len(parts)):
        out.append(jnp.where(lane < steps, rolled[index - 1], rolled[index]))
    return out


def first_order(parts, powers):
    for level, power in enumerate(powers):
        moved = delayed(parts, 1 << level)
        parts = [
            part if late is None else part + power * late for part, late in zip(parts, moved)
        ]
    return parts


def sweeps(target, slow, fast):
    lag_one, lag_two = slow + fast, -slow * fast
    slow_powers, fast_powers = [slow], [fast]
    for _ in range(8):
        slow_powers.append(slow_powers[-1] * slow_powers[-1])
        fast_powers.append(fast_powers[-1] * fast_powers[-1])
    slow_share = slow / (slow - fast)
    fast_share = fast / (slow - fast)
    estimate = target
    for sweep in range(SWEEPS):
        one, two = delayed(estimate, 1), delayed(estimate, 2)
        spikes = [
            jnp.maximum(now - lag_one * a - lag_two * b, 0.0)
            for now, a, b in zip(estimate, one, two)
        ]
        slow_part = first_order(spikes, slow_powers)
        fast_part = first_order(spikes, fast_powers)
        calcium = [slow_share * a - fast_share * b for a, b in zip(slow_part, fast_part)]
        if sweep + 1 < SWEEPS:
            estimate = [0.5 * (a + b) for a, b in zip(target, calcium)]
    return calcium


def exchange_kernel(
    send, traces, slow, fast, back, calcium,
    got, hot, part, parts, piece, whole, reply, answer,
    s1, r1, s2, r2, s3, r3, s4, r4, local,
):
    tile, y, z = lax.axis_index("tile"), lax.axis_index("tm"), lax.axis_index("plane")
    x, c = tile // 2, lax.rem(tile, 2)
    d = 1 - c
    p = x * d + z * c
    q = z * d + x * c

    def turn(value, by):
        return lax.rem(value + by, 4)

    def mine(pos, core):
        return (d * (2 * pos + core) + c * (2 * x + core), y, d * z + c * pos)

    def other(pos):
        return (c * 2 * pos + d * (2 * x + 1), y, c * z + d * pos)

    def column(pos, frame):
        return (d * 2 * x + c * (2 * pos + 1), frame, d * pos + c * z)

    far = [(dq, dy) for dq in range(4) for dy in range(4) if (dq, dy) != (0, 0)]
    far = sorted(far, key=lambda pair: -(min(pair[0], 4 - pair[0]) + min(pair[1], 4 - pair[1])))
    reach = (2, 1, 3)

    barrier = pltpu.get_barrier_semaphore()
    met = [mine(turn(p, by), c) for by in reach]
    met += [mine(turn(p, by), d) for by in (2, 1, 3, 0)]
    met += [other(turn(q, by)) for by in reach]
    met += [column(turn(q, dq), turn(y, dy)) for dq, dy in far]
    for device in met:
        pl.semaphore_signal(barrier, inc=1, device_id=device, device_id_type=MESH)
    for source in range(8):
        got[source, ROWS:, :] = jnp.zeros((24, FR), F32)
    part[...] = jnp.zeros_like(part)
    for sub in range(4):
        part[q, sub, :SUB, :] = traces[sub * SUB : (sub + 1) * SUB, :]
    pl.semaphore_wait(barrier, len(met))

    def remote(source, target, sends, arrives, device):
        return pltpu.make_async_remote_copy(
            src_ref=source, dst_ref=target, send_sem=sends, recv_sem=arrives,
            device_id=device, device_id_type=MESH,
        )

    def message(index):
        return send.at[pl.ds(pl.multiple_of(index * ROWS, 8), ROWS), :]

    def landing(index):
        return got.at[index, pl.ds(0, ROWS), :]

    started = []
    own = pltpu.make_async_copy(message(c * 4 + p), landing(p * 2 + c), local.at[0])
    own.start()
    for by in reach:
        index = c * 4 + turn(p, by)
        started.append(
            remote(message(index), landing(p * 2 + c), s1.at[index], r1.at[p * 2 + c], mine(turn(p, by), c))
        )
        started[-1].start()
        index = d * 4 + turn(q, by)
        started.append(
            remote(message(index), landing(q * 2 + c), s1.at[index], r1.at[q * 2 + c], other(turn(q, by)))
        )
        started[-1].start()
    index = d * 4 + q
    started.append(remote(message(index), landing(q * 2 + c), s1.at[index], r1.at[q * 2 + c], other(q)))
    started[-1].start()

    slots_iota = (iota((OWN, 128), 0) + 1).astype(F32)
    weight = [jnp.zeros((OWN, 128), F32) for _ in range(4)]
    own.wait()
    sources = [(0, 0), (0, 1), (1, 0), (1, 1), (3, 0), (3, 1), (2, 0), (2, 1)]
    for by, flip in sources:
        source = turn(p, by) * 2 + (d if flip else c)
        if (by, flip) != (0, 0):
            remote(
                message(0), landing(source), s1.at[0], r1.at[source], mine(turn(p, by), c)
            ).wait_recv()
        for i in range(4):
            slots = got[source, MSG + i : MSG + i + 1, :]
            energies = got[source, MSG + 4 + i : MSG + 5 + i, :]
            match = slots_iota == slots
            chosen = jnp.where(match, 1.0, 0.0).astype(BF16)
            hot[source, i] = chosen
            weight[i] = weight[i] + jnp.where(match, energies, 0.0)
            high, low = split(got[source, i * CAP : i * CAP + 128, :])
            total = jnp.dot(
                jnp.concatenate([chosen, chosen], axis=1),
                jnp.concatenate([high, low], axis=0),
                preferred_element_type=F32,
            )
            for sub in range(4):
                part[i, sub, :SUB, :] += total[sub * SUB : (sub + 1) * SUB, :]
    ones = jnp.ones((8, 128), BF16)
    top = iota((8, 128), 0) == 0
    for i in range(4):
        high, low = split(weight[i])
        energy = lax.dot_general(ones, high, NT, preferred_element_type=F32) + lax.dot_general(
            ones, low, NT, preferred_element_type=F32
        )
        tile_rows = jnp.where(top, energy[:, :128], energy[:, 128:])
        for sub in range(4):
            part[i, sub, SUB:, :] = tile_rows

    for dq, dy in far:
        tq, ty = turn(q, dq), turn(y, dy)
        started.append(
            remote(part.at[tq, ty], parts.at[q, y], s2.at[tq * 4 + ty], r2.at[q * 4 + y], column(tq, ty))
        )
        started[-1].start()
    own = pltpu.make_async_copy(part.at[q, y], parts.at[q, y], local.at[1])
    own.start()
    own.wait()
    for dq, dy in far:
        fq, fy = turn(q, dq), turn(y, dy)
        remote(part.at[0, 0], parts.at[fq, fy], s2.at[0], r2.at[fq * 4 + fy], column(fq, fy)).wait_recv()
    energy = parts[0, 0, SUB : SUB + 2, :]
    for other_q in range(1, 4):
        energy = energy + parts[other_q, 0, SUB : SUB + 2, :]
    scale = pick(energy, y) + 1.0
    target = []
    for frame in range(4):
        total = parts[0, frame, :SUB, :]
        for other_q in range(1, 4):
            total = total + parts[other_q, frame, :SUB, :]
        target.append(total / scale)
    traced = sweeps(target, pick(slow[...], y), pick(fast[...], y))
    for frame in range(4):
        piece[frame] = traced[frame]

    for dq, dy in far:
        tq, ty = turn(q, dq), turn(y, dy)
        started.append(
            remote(piece.at[ty], whole.at[q, y], s3.at[tq * 4 + ty], r3.at[q * 4 + y], column(tq, ty))
        )
        started[-1].start()
    own = pltpu.make_async_copy(piece.at[y], whole.at[q, y], local.at[2])
    own.start()
    own.wait()
    for dq, dy in far:
        fq, fy = turn(q, dq), turn(y, dy)
        remote(piece.at[0], whole.at[fq, fy], s3.at[0], r3.at[fq * 4 + fy], column(fq, fy)).wait_recv()
    for sub in range(4):
        calcium[sub * SUB : (sub + 1) * SUB, :] = whole[q, sub]
    rows = [whole[i].reshape(OWN, FR).astype(BF16) for i in range(4)]

    for by, flip in sources[::-1]:
        core = d if flip else c
        source = turn(p, by) * 2 + core
        for i in range(4):
            got_rows = lax.dot_general(hot[source, i], rows[i], TN, preferred_element_type=F32)
            reply[source, i * CAP : (i + 1) * CAP, :] = got_rows[:CAP, :]
        if (by, flip) == (0, 0):
            own = pltpu.make_async_copy(reply.at[source], answer.at[c * 4 + p], local.at[3])
            own.start()
        else:
            started.append(
                remote(
                    reply.at[source], answer.at[c * 4 + p], s4.at[source], r4.at[c * 4 + p],
                    mine(turn(p, by), core),
                )
            )
            started[-1].start()
    own.wait()
    back[pl.ds(pl.multiple_of((c * 4 + p) * ROWS, 8), MSG), :] = answer[c * 4 + p]
    for by in (0, 1, 3, 2):
        for core, pos in ((d, turn(q, by)), (c, turn(p, by))):
            if by == 0 and core is c:
                continue
            index = core * 4 + pos
            remote(reply.at[0], answer.at[index], s4.at[0], r4.at[index], other(q)).wait_recv()
            back[pl.ds(pl.multiple_of(index * ROWS, 8), MSG), :] = answer[index]
    for copy in started:
        copy.wait_send()


def exchange(send, traces, slow_root, fast_root):
    dma = pltpu.SemaphoreType.DMA
    return pl.pallas_call(
        exchange_kernel,
        out_shape=(
            jax.ShapeDtypeStruct((8 * ROWS, FR), F32),
            jax.ShapeDtypeStruct((OWN, FR), F32),
        ),
        in_specs=[VMEM] * 4,
        out_specs=(VMEM, VMEM),
        scratch_shapes=[
            pltpu.VMEM((8, MSG + 32, FR), F32),
            pltpu.VMEM((8, 4, OWN, 128), BF16),
            pltpu.VMEM((4, 4, PIECE, FR), F32),
            pltpu.VMEM((4, 4, PIECE, FR), F32),
            pltpu.VMEM((4, SUB, FR), F32),
            pltpu.VMEM((4, 4, SUB, FR), F32),
            pltpu.VMEM((8, MSG, FR), F32),
            pltpu.VMEM((8, MSG, FR), F32),
            dma((8,)), dma((8,)), dma((16,)), dma((16,)),
            dma((16,)), dma((16,)), dma((8,)), dma((8,)), dma((4,)),
        ],
        compiler_params=pltpu.CompilerParams(
            collective_id=1, has_side_effects=True, vmem_limit_bytes=48 << 20
        ),
        name="exchange",
    )(send, traces, slow_root.reshape(2, 128), fast_root.reshape(2, 128))


def rebuild_kernel(pos, order, starts, back, foot, block, calcium, out, calcium_out, rows, total):
    step = pl.program_id(0)

    @pl.when(step == 0)
    def _():
        calcium_out[...] = calcium[...]

        @pl.loop(0, ENT // 16)
        def _(group):
            line, lane = group // 8, lax.rem(group, 8) * 16
            for i in range(16):
                rows[pl.ds(order[line, lane + i], 1), :] = back[pl.ds(pos[line, lane + i], 1), :]

    begin, end = starts[0, step], starts[0, step + 1]
    first = jnp.minimum(begin // 128, ENT // 128 - 1)
    last = jnp.maximum(first, (end - 1) // 128)

    def product(window):
        span = pl.ds(pl.multiple_of(window * 128, 128), 128)
        values, which = rows[span, :], block[span, :]
        masked = jnp.concatenate(
            [
                jnp.where(which == (step * 8 + n).astype(F32), values, 0.0).astype(BF16)
                for n in range(8)
            ],
            axis=1,
        )
        return lax.dot_general(foot[span, :], masked, TN, preferred_element_type=F32)

    def store(result):
        for n in range(8):
            out[n] = result[:, n * 128 : (n + 1) * 128].astype(BF16)

    @pl.when(first == last)
    def _():
        store(product(first))

    @pl.when(first != last)
    def _():
        total[...] = product(first)

        @pl.loop(first + 1, last + 1)
        def _(window):
            total[...] += product(window)

        store(total[...])


def rebuild(pos, order, starts, back, foot, block, calcium):
    grid = BLK // 8
    whole = lambda shape: pl.BlockSpec(shape, lambda i: (0, 0))
    return pl.pallas_call(
        rebuild_kernel,
        grid=(grid,),
        out_shape=(
            jax.ShapeDtypeStruct((BLK, VOX, FR), BF16),
            jax.ShapeDtypeStruct((OWN, FR), F32),
        ),
        in_specs=[SMEM, SMEM, SMEM, whole((8 * ROWS, FR)), whole((ENT, VOX)), whole((ENT, 128)), whole((OWN, FR))],
        out_specs=(pl.BlockSpec((8, VOX, FR), lambda i: (i, 0, 0)), whole((OWN, FR))),
        scratch_shapes=[pltpu.VMEM((ENT, FR), F32), pltpu.VMEM((VOX, 8 * FR), F32)],
        compiler_params=pltpu.CompilerParams(vmem_limit_bytes=32 << 20),
        name="rebuild",
    )(pos, order, starts, back, foot, block, calcium)


def shards(movie, footprint, entry_block, entry_owner, entry_slot, traces, slow_root, fast_root):
    send, pos, order, foot, block, starts = gather(
        movie, footprint, entry_block, entry_owner, entry_slot
    )
    back, calcium = exchange(send, traces, slow_root, fast_root)
    return rebuild(pos, order, starts, back, foot, block, calcium)


def solution(mesh):
    owners = ("tile", "plane")
    placed = (
        P(owners, None, "tm"),
        P(owners, None),
        P(owners),
        P(owners, None),
        P(owners),
        P(owners, "tm"),
        P(owners),
        P(owners),
    )
    return jax.shard_map(
        shards,
        mesh=mesh,
        in_specs=placed,
        out_specs=(P(owners, None, "tm"), P(owners, "tm")),
        check_vma=False,
    )
```

```python
import jax
import jax.numpy as jnp
from jax import lax
from jax.experimental import pallas as pl
from jax.experimental.pallas import tpu as pltpu
from jax.sharding import PartitionSpec as P

SWEEPS = 4
CAP = 96
OWN = 256
ENT = 1024
VOX = 128
FR = 128
BLK = 256
MSG = 4 * CAP
ROWS = MSG + 8
SUB = OWN // 4
PIECE = SUB + 8
WINDOW = 64
PART = 64
MESH = pl.DeviceIdType.MESH
F32 = jnp.float32
BF16 = jnp.bfloat16
VMEM = pl.BlockSpec(memory_space=pltpu.VMEM)
SMEM = pl.BlockSpec(memory_space=pltpu.SMEM)
NT = (((1,), (1,)), ((), ()))
TN = (((0,), (0,)), ((), ()))


def iota(shape, axis):
    return lax.broadcasted_iota(jnp.int32, shape, axis)


def split(value):
    high = value.astype(BF16)
    return high, (value - high.astype(F32)).astype(BF16)


def gather_kernel(
    movie_hbm, foot_hbm, block_hbm, owner_hbm, slot_hbm,
    send, pos_out, rank_out, starts_out, foot_sorted, block_sorted,
    movie, foot, index, projected, pos_s, rank_s, starts_s, sem, movie_sem,
):
    small = [
        pltpu.make_async_copy(source, target, sem.at[number])
        for number, (source, target) in enumerate(
            [(block_hbm, index.at[0]), (owner_hbm, index.at[1]), (slot_hbm, index.at[2]), (foot_hbm, foot)]
        )
    ]
    for copy in small:
        copy.start()

    def movie_part(number):
        span = pl.ds(number * PART, PART)
        return pltpu.make_async_copy(movie_hbm.at[span], movie.at[span], movie_sem.at[number])

    for number in range(BLK // PART):
        movie_part(number).start()
    send[...] = jnp.zeros_like(send)
    projected[...] = jnp.zeros_like(projected)
    foot_sorted[ENT:, :] = jnp.zeros((WINDOW, VOX), F32)
    block_sorted[ENT:, :] = jnp.full((WINDOW, 128), -1.0, F32)
    for copy in small:
        copy.wait()
    blk, own, slt = index[0], index[1], index[2]
    entry = iota((8, 128), 0) * 128 + iota((8, 128), 1)
    key = (blk * ENT + entry).astype(F32)
    ownf = own.astype(F32)
    key_col, own_col, blk_col = key.T, ownf.T, blk.astype(F32).T
    before = iota((128, 128), 0) < iota((128, 128), 1)
    lane8 = (iota((128, 128), 1) * 8).astype(F32)
    owner_rank, block_rank = [], []
    less = jnp.zeros((128, 128), F32)
    for row in range(8):
        key_row, own_row = key[row : row + 1, :], ownf[row : row + 1, :]
        count_o = jnp.zeros((128, 128), F32)
        count_k = jnp.zeros((128, 128), F32)
        for col in range(8):
            count_k += jnp.where(key_col[:, col : col + 1] < key_row, 1.0, 0.0)
            if col <= row:
                same = own_col[:, col : col + 1] == own_row
                if col == row:
                    same = same & before
                count_o += jnp.where(same, 1.0, 0.0)
        owner_rank.append(jnp.sum(count_o, axis=0, keepdims=True))
        block_rank.append(jnp.sum(count_k, axis=0, keepdims=True))
        less += jnp.where(blk_col[:, row : row + 1] < lane8, 1.0, 0.0)
    rank = jnp.concatenate(owner_rank, axis=0).astype(jnp.int32)
    order = jnp.concatenate(block_rank, axis=0).astype(jnp.int32)
    core, far, near = (own >> 2) & 1, own >> 3, own & 3
    message = jnp.where(core == 0, far, 4 + near)
    member = jnp.where(core == 0, near, far)
    pos_out[...] = message * ROWS + member * CAP + rank
    rank_out[...] = order
    starts_out[...] = jnp.broadcast_to(jnp.sum(less, axis=0, keepdims=True), (8, 128)).astype(
        jnp.int32
    )
    to_smem = [
        pltpu.make_async_copy(source, target, sem.at[4 + number])
        for number, (source, target) in enumerate(
            [(pos_out, pos_s), (rank_out, rank_s), (starts_out, starts_s)]
        )
    ]
    for copy in to_smem:
        copy.start()

    foot_values = foot[...].astype(F32)
    sq_high, sq_low = split(foot_values * foot_values)
    ones = jnp.ones((8, 128), BF16)
    energy = lax.dot_general(ones, sq_high, NT, preferred_element_type=F32) + lax.dot_general(
        ones, sq_low, NT, preferred_element_type=F32
    )
    place = member * 128 + rank
    meta = jnp.zeros((24, 512), F32)
    sorted_wide = jnp.zeros((ENT, 256), F32)
    for row in range(8):
        lanes = slice(row * 128, row * 128 + 128)
        chosen = message[row : row + 1, :] == iota((8, 128), 0)
        en_high, en_low = split(energy[:, lanes])
        slots = (slt[row : row + 1, :] + 1).astype(F32)
        values = jnp.concatenate(
            [
                jnp.where(chosen, slots, 0.0),
                jnp.where(chosen, en_high.astype(F32), 0.0),
                jnp.where(chosen, en_low.astype(F32), 0.0),
            ],
            axis=0,
        ).astype(BF16)
        places = jnp.where(place[row : row + 1, :] == iota((512, 128), 0), 1.0, 0.0).astype(BF16)
        meta += lax.dot_general(values, places, NT, preferred_element_type=F32)
        permute = jnp.where(order[row : row + 1, :] == iota((ENT, 128), 0), 1.0, 0.0).astype(BF16)
        wide = jnp.concatenate(
            [
                foot[lanes, :],
                jnp.broadcast_to(blk_col[:, row : row + 1], (128, 128)).astype(BF16),
            ],
            axis=1,
        )
        sorted_wide += jnp.dot(permute, wide, preferred_element_type=F32)
    foot_sorted[:ENT, :] = sorted_wide[:, :128]
    block_sorted[:ENT, :] = sorted_wide[:, 128:]
    for m in range(8):
        for i in range(4):
            lanes = slice(i * 128, i * 128 + 128)
            base = m * ROWS + MSG
            send[base + i : base + i + 1, :] = meta[m : m + 1, lanes]
            send[base + 4 + i : base + 5 + i, :] = (
                meta[8 + m : 9 + m, lanes] + meta[16 + m : 17 + m, lanes]
            )
    for copy in to_smem:
        copy.wait()

    def product(chunk, first):
        span = pl.ds(pl.multiple_of(first, 8), WINDOW)
        values, which = foot_sorted[span, :], block_sorted[span, :]
        left = jnp.concatenate(
            [
                jnp.where(which == (chunk * 8 + n).astype(F32), values, 0.0).astype(BF16)
                for n in range(8)
            ],
            axis=1,
        )
        right = movie[pl.ds(chunk * 8, 8)].reshape(8 * VOX, FR)
        projected[span, :] += jnp.dot(left, right, preferred_element_type=F32)

    @pl.loop(0, BLK // PART)
    def _(group):
        movie_part(group).wait()
        windows(starts_s, group, product)

    @pl.loop(0, 8)
    def _(line):
        for lane in range(128):
            send[pl.ds(pos_s[line, lane], 1), :] = projected[pl.ds(rank_s[line, lane], 1), :]


def windows(starts, group, product):
    count = PART // 8
    fits = None
    for k in range(count):
        chunk = group * count + k
        begin = (starts[0, chunk] // 8) * 8
        inside = starts[0, chunk + 1] - begin <= WINDOW
        fits = inside if fits is None else fits & inside

    @pl.when(fits)
    def _():
        for k in range(count):
            chunk = group * count + k
            product(chunk, (starts[0, chunk] // 8) * 8)

    @pl.when(jnp.logical_not(fits))
    def _():
        @pl.loop(0, count)
        def _(k):
            chunk = group * count + k
            begin = (starts[0, chunk] // 8) * 8
            number = jnp.maximum(1, (starts[0, chunk + 1] - begin + WINDOW - 1) // WINDOW)

            @pl.loop(0, number)
            def _(step):
                product(chunk, begin + step * WINDOW)


def gather(movie, footprint, entry_block, entry_owner, entry_slot):
    shape = jax.ShapeDtypeStruct
    any_place = pl.BlockSpec(memory_space=pl.ANY)
    index = shape((8, 128), jnp.int32)
    return pl.pallas_call(
        gather_kernel,
        out_shape=(
            shape((8 * ROWS, FR), F32),
            index,
            index,
            index,
            shape((ENT + WINDOW, VOX), F32),
            shape((ENT + WINDOW, 128), F32),
        ),
        in_specs=[any_place] * 5,
        out_specs=(VMEM,) * 6,
        scratch_shapes=[
            pltpu.VMEM((BLK, VOX, FR), BF16),
            pltpu.VMEM((ENT, VOX), BF16),
            pltpu.VMEM((3, 8, 128), jnp.int32),
            pltpu.VMEM((ENT + WINDOW, FR), F32),
            pltpu.SMEM((8, 128), jnp.int32),
            pltpu.SMEM((8, 128), jnp.int32),
            pltpu.SMEM((8, 128), jnp.int32),
            pltpu.SemaphoreType.DMA((7,)),
            pltpu.SemaphoreType.DMA((BLK // PART,)),
        ],
        compiler_params=pltpu.CompilerParams(vmem_limit_bytes=56 << 20),
        name="project",
    )(
        movie, footprint, entry_block.reshape(8, 128),
        entry_owner.reshape(8, 128), entry_slot.reshape(8, 128),
    )


def pick(rows, sub):
    chosen = jnp.where(sub // 2 == 0, rows[0:1, :], rows[1:2, :])
    lane = iota((SUB, 128), 1) - lax.rem(sub, 2) * SUB
    return jnp.sum(jnp.where(lane == iota((SUB, 128), 0), chosen, 0.0), axis=1, keepdims=True)


def delayed(parts, steps):
    if steps >= 128:
        hop = steps // 128
        return [None] * hop + parts[: len(parts) - hop]
    lane = iota((SUB, 128), 1)
    rolled = [pltpu.roll(part, steps, 1) for part in parts]
    out = [jnp.where(lane < steps, 0.0, rolled[0])]
    for index in range(1, len(parts)):
        out.append(jnp.where(lane < steps, rolled[index - 1], rolled[index]))
    return out


def first_order(parts, powers):
    for level, power in enumerate(powers):
        moved = delayed(parts, 1 << level)
        parts = [
            part if late is None else part + power * late for part, late in zip(parts, moved)
        ]
    return parts


def sweeps(target, slow, fast):
    lag_one, lag_two = slow + fast, -slow * fast
    slow_powers, fast_powers = [slow], [fast]
    for _ in range(8):
        slow_powers.append(slow_powers[-1] * slow_powers[-1])
        fast_powers.append(fast_powers[-1] * fast_powers[-1])
    slow_share = slow / (slow - fast)
    fast_share = fast / (slow - fast)
    estimate = target
    for sweep in range(SWEEPS):
        one, two = delayed(estimate, 1), delayed(estimate, 2)
        spikes = [
            jnp.maximum(now - lag_one * a - lag_two * b, 0.0)
            for now, a, b in zip(estimate, one, two)
        ]
        slow_part = first_order(spikes, slow_powers)
        fast_part = first_order(spikes, fast_powers)
        calcium = [slow_share * a - fast_share * b for a, b in zip(slow_part, fast_part)]
        if sweep + 1 < SWEEPS:
            estimate = [0.5 * (a + b) for a, b in zip(target, calcium)]
    return calcium


def exchange_kernel(
    send, traces, slow, fast, back, calcium,
    got, hot, part, parts, piece, whole, reply, answer,
    s1, r1, s2, r2, s3, r3, s4, r4, local,
):
    tile, y, z = lax.axis_index("tile"), lax.axis_index("tm"), lax.axis_index("plane")
    x, c = tile // 2, lax.rem(tile, 2)
    d = 1 - c
    p = x * d + z * c
    q = z * d + x * c

    def turn(value, by):
        return lax.rem(value + by, 4)

    def mine(pos, core):
        return (d * (2 * pos + core) + c * (2 * x + core), y, d * z + c * pos)

    def other(pos):
        return (c * 2 * pos + d * (2 * x + 1), y, c * z + d * pos)

    def column(pos, frame):
        return (d * 2 * x + c * (2 * pos + 1), frame, d * pos + c * z)

    far = [(dq, dy) for dq in range(4) for dy in range(4) if (dq, dy) != (0, 0)]
    far = sorted(far, key=lambda pair: -(min(pair[0], 4 - pair[0]) + min(pair[1], 4 - pair[1])))
    reach = (2, 1, 3)

    barrier = pltpu.get_barrier_semaphore()
    met = [mine(turn(p, by), c) for by in reach]
    met += [mine(turn(p, by), d) for by in (2, 1, 3, 0)]
    met += [other(turn(q, by)) for by in reach]
    met += [column(turn(q, dq), turn(y, dy)) for dq, dy in far]
    for device in met:
        pl.semaphore_signal(barrier, inc=1, device_id=device, device_id_type=MESH)
    for source in range(8):
        got[source, ROWS:, :] = jnp.zeros((24, FR), F32)
    part[...] = jnp.zeros_like(part)
    for sub in range(4):
        part[q, sub, :SUB, :] = traces[sub * SUB : (sub + 1) * SUB, :]
    pl.semaphore_wait(barrier, len(met))

    def remote(source, target, sends, arrives, device):
        return pltpu.make_async_remote_copy(
            src_ref=source, dst_ref=target, send_sem=sends, recv_sem=arrives,
            device_id=device, device_id_type=MESH,
        )

    def message(index):
        return send.at[pl.ds(pl.multiple_of(index * ROWS, 8), ROWS), :]

    def landing(index):
        return got.at[index, pl.ds(0, ROWS), :]

    started = []
    own = pltpu.make_async_copy(message(c * 4 + p), landing(p * 2 + c), local.at[0])
    own.start()
    for by in reach:
        index = c * 4 + turn(p, by)
        started.append(
            remote(message(index), landing(p * 2 + c), s1.at[index], r1.at[p * 2 + c], mine(turn(p, by), c))
        )
        started[-1].start()
        index = d * 4 + turn(q, by)
        started.append(
            remote(message(index), landing(q * 2 + c), s1.at[index], r1.at[q * 2 + c], other(turn(q, by)))
        )
        started[-1].start()
    index = d * 4 + q
    started.append(remote(message(index), landing(q * 2 + c), s1.at[index], r1.at[q * 2 + c], other(q)))
    started[-1].start()

    slots_iota = (iota((OWN, 128), 0) + 1).astype(F32)
    weight = [jnp.zeros((OWN, 128), F32) for _ in range(4)]
    own.wait()
    sources = [(0, 0), (0, 1), (1, 0), (1, 1), (3, 0), (3, 1), (2, 0), (2, 1)]
    for by, flip in sources:
        source = turn(p, by) * 2 + (d if flip else c)
        if (by, flip) != (0, 0):
            remote(
                message(0), landing(source), s1.at[0], r1.at[source], mine(turn(p, by), c)
            ).wait_recv()
        for i in range(4):
            slots = got[source, MSG + i : MSG + i + 1, :]
            energies = got[source, MSG + 4 + i : MSG + 5 + i, :]
            match = slots_iota == slots
            chosen = jnp.where(match, 1.0, 0.0).astype(BF16)
            hot[source, i] = chosen
            weight[i] = weight[i] + jnp.where(match, energies, 0.0)
            high, low = split(got[source, i * CAP : i * CAP + 128, :])
            total = jnp.dot(
                jnp.concatenate([chosen, chosen], axis=1),
                jnp.concatenate([high, low], axis=0),
                preferred_element_type=F32,
            )
            for sub in range(4):
                part[i, sub, :SUB, :] += total[sub * SUB : (sub + 1) * SUB, :]
    ones = jnp.ones((8, 128), BF16)
    top = iota((8, 128), 0) == 0
    for i in range(4):
        high, low = split(weight[i])
        energy = lax.dot_general(ones, high, NT, preferred_element_type=F32) + lax.dot_general(
            ones, low, NT, preferred_element_type=F32
        )
        tile_rows = jnp.where(top, energy[:, :128], energy[:, 128:])
        for sub in range(4):
            part[i, sub, SUB:, :] = tile_rows

    for dq, dy in far:
        tq, ty = turn(q, dq), turn(y, dy)
        started.append(
            remote(part.at[tq, ty], parts.at[q, y], s2.at[tq * 4 + ty], r2.at[q * 4 + y], column(tq, ty))
        )
        started[-1].start()
    own = pltpu.make_async_copy(part.at[q, y], parts.at[q, y], local.at[1])
    own.start()
    own.wait()
    for dq, dy in far:
        fq, fy = turn(q, dq), turn(y, dy)
        remote(part.at[0, 0], parts.at[fq, fy], s2.at[0], r2.at[fq * 4 + fy], column(fq, fy)).wait_recv()
    energy = parts[0, 0, SUB : SUB + 2, :]
    for other_q in range(1, 4):
        energy = energy + parts[other_q, 0, SUB : SUB + 2, :]
    scale = pick(energy, y) + 1.0
    target = []
    for frame in range(4):
        total = parts[0, frame, :SUB, :]
        for other_q in range(1, 4):
            total = total + parts[other_q, frame, :SUB, :]
        target.append(total / scale)
    traced = sweeps(target, pick(slow[...], y), pick(fast[...], y))
    for frame in range(4):
        piece[frame] = traced[frame]

    for dq, dy in far:
        tq, ty = turn(q, dq), turn(y, dy)
        started.append(
            remote(piece.at[ty], whole.at[q, y], s3.at[tq * 4 + ty], r3.at[q * 4 + y], column(tq, ty))
        )
        started[-1].start()
    own = pltpu.make_async_copy(piece.at[y], whole.at[q, y], local.at[2])
    own.start()
    own.wait()
    for dq, dy in far:
        fq, fy = turn(q, dq), turn(y, dy)
        remote(piece.at[0], whole.at[fq, fy], s3.at[0], r3.at[fq * 4 + fy], column(fq, fy)).wait_recv()
    for sub in range(4):
        calcium[sub * SUB : (sub + 1) * SUB, :] = whole[q, sub]
    rows = [whole[i].reshape(OWN, FR).astype(BF16) for i in range(4)]

    for by, flip in sources[::-1]:
        core = d if flip else c
        source = turn(p, by) * 2 + core
        for i in range(4):
            got_rows = lax.dot_general(hot[source, i], rows[i], TN, preferred_element_type=F32)
            reply[source, i * CAP : (i + 1) * CAP, :] = got_rows[:CAP, :]
        if (by, flip) == (0, 0):
            own = pltpu.make_async_copy(reply.at[source], answer.at[c * 4 + p], local.at[3])
            own.start()
        else:
            started.append(
                remote(
                    reply.at[source], answer.at[c * 4 + p], s4.at[source], r4.at[c * 4 + p],
                    mine(turn(p, by), core),
                )
            )
            started[-1].start()
    own.wait()
    back[pl.ds(pl.multiple_of((c * 4 + p) * ROWS, 8), MSG), :] = answer[c * 4 + p]
    for by in (0, 1, 3, 2):
        for core, pos in ((d, turn(q, by)), (c, turn(p, by))):
            if by == 0 and core is c:
                continue
            index = core * 4 + pos
            remote(reply.at[0], answer.at[index], s4.at[0], r4.at[index], other(q)).wait_recv()
            back[pl.ds(pl.multiple_of(index * ROWS, 8), MSG), :] = answer[index]
    for copy in started:
        copy.wait_send()


def exchange(send, traces, slow_root, fast_root):
    dma = pltpu.SemaphoreType.DMA
    return pl.pallas_call(
        exchange_kernel,
        out_shape=(
            jax.ShapeDtypeStruct((8 * ROWS, FR), F32),
            jax.ShapeDtypeStruct((OWN, FR), F32),
        ),
        in_specs=[VMEM] * 4,
        out_specs=(VMEM, VMEM),
        scratch_shapes=[
            pltpu.VMEM((8, MSG + 32, FR), F32),
            pltpu.VMEM((8, 4, OWN, 128), BF16),
            pltpu.VMEM((4, 4, PIECE, FR), F32),
            pltpu.VMEM((4, 4, PIECE, FR), F32),
            pltpu.VMEM((4, SUB, FR), F32),
            pltpu.VMEM((4, 4, SUB, FR), F32),
            pltpu.VMEM((8, MSG, FR), F32),
            pltpu.VMEM((8, MSG, FR), F32),
            dma((8,)), dma((8,)), dma((16,)), dma((16,)),
            dma((16,)), dma((16,)), dma((8,)), dma((8,)), dma((4,)),
        ],
        compiler_params=pltpu.CompilerParams(
            collective_id=1, has_side_effects=True, vmem_limit_bytes=48 << 20
        ),
        name="exchange",
    )(send, traces, slow_root.reshape(2, 128), fast_root.reshape(2, 128))


def rebuild_kernel(
    pos, order, starts, back, foot, block, calcium, out_hbm, calcium_out, rows, out, total, sem
):
    calcium_out[...] = calcium[...]
    rows[ENT:, :] = jnp.zeros((WINDOW, FR), F32)

    @pl.loop(0, 8)
    def _(line):
        for lane in range(128):
            rows[pl.ds(order[line, lane], 1), :] = back[pl.ds(pos[line, lane], 1), :]

    def product(chunk, first):
        span = pl.ds(pl.multiple_of(first, 8), WINDOW)
        values, which = rows[span, :], block[span, :]
        masked = jnp.concatenate(
            [
                jnp.where(which == (chunk * 8 + n).astype(F32), values, 0.0).astype(BF16)
                for n in range(8)
            ],
            axis=1,
        )
        left = foot[span, :].astype(BF16)
        return lax.dot_general(left, masked, TN, preferred_element_type=F32)

    def out_part(number):
        span = pl.ds(number * PART, PART)
        return pltpu.make_async_copy(out.at[span], out_hbm.at[span], sem.at[number])

    def store(chunk, result):
        for n in range(8):
            out[chunk * 8 + n] = result[:, n * FR : (n + 1) * FR].astype(BF16)

    count = PART // 8

    @pl.loop(0, BLK // PART)
    def _(group):
        fits = None
        for k in range(count):
            chunk = group * count + k
            inside = starts[0, chunk + 1] - (starts[0, chunk] // 8) * 8 <= WINDOW
            fits = inside if fits is None else fits & inside

        @pl.when(fits)
        def _():
            for k in range(count):
                chunk = group * count + k
                store(chunk, product(chunk, (starts[0, chunk] // 8) * 8))

        @pl.when(jnp.logical_not(fits))
        def _():
            @pl.loop(0, count)
            def _(k):
                chunk = group * count + k
                begin = (starts[0, chunk] // 8) * 8
                number = jnp.maximum(1, (starts[0, chunk + 1] - begin + WINDOW - 1) // WINDOW)
                total[...] = product(chunk, begin)

                @pl.loop(1, number)
                def _(step):
                    total[...] += product(chunk, begin + step * WINDOW)

                store(chunk, total[...])

        out_part(group).start()

    @pl.loop(0, BLK // PART)
    def _(group):
        out_part(group).wait()


def rebuild(pos, order, starts, back, foot, block, calcium):
    return pl.pallas_call(
        rebuild_kernel,
        out_shape=(
            jax.ShapeDtypeStruct((BLK, VOX, FR), BF16),
            jax.ShapeDtypeStruct((OWN, FR), F32),
        ),
        in_specs=[SMEM] * 3 + [VMEM] * 4,
        out_specs=(pl.BlockSpec(memory_space=pl.ANY), VMEM),
        scratch_shapes=[
            pltpu.VMEM((ENT + WINDOW, FR), F32),
            pltpu.VMEM((BLK, VOX, FR), BF16),
            pltpu.VMEM((VOX, 8 * FR), F32),
            pltpu.SemaphoreType.DMA((BLK // PART,)),
        ],
        compiler_params=pltpu.CompilerParams(vmem_limit_bytes=48 << 20),
        name="rebuild",
    )(pos, order, starts, back, foot, block, calcium)


def shards(movie, footprint, entry_block, entry_owner, entry_slot, traces, slow_root, fast_root):
    send, pos, order, starts, foot, block = gather(
        movie, footprint, entry_block, entry_owner, entry_slot
    )
    back, calcium = exchange(send, traces, slow_root, fast_root)
    return rebuild(pos, order, starts, back, foot, block, calcium)


def solution(mesh):
    owners = ("tile", "plane")
    placed = (
        P(owners, None, "tm"),
        P(owners, None),
        P(owners),
        P(owners, None),
        P(owners),
        P(owners, "tm"),
        P(owners),
        P(owners),
    )
    return jax.shard_map(
        shards,
        mesh=mesh,
        in_specs=placed,
        out_specs=(P(owners, None, "tm"), P(owners, "tm")),
        check_vma=False,
    )
```

```python
import jax
import jax.numpy as jnp
from jax import lax
from jax.experimental import pallas as pl
from jax.experimental.pallas import tpu as pltpu
from jax.sharding import PartitionSpec as P

SWEEPS = 4
TURNS = (2, 1, 3, 0)
CAP = 96
OWN = 256
ENT = 1024
VOX = 128
FR = 128
BLK = 256
MSG = 4 * CAP
ROWS = MSG + 8
SUB = OWN // 4
PIECE = SUB + 8
WINDOW = 64
PART = 64
MESH = pl.DeviceIdType.MESH
F32 = jnp.float32
BF16 = jnp.bfloat16
VMEM = pl.BlockSpec(memory_space=pltpu.VMEM)
NT = (((1,), (1,)), ((), ()))
TN = (((0,), (0,)), ((), ()))


def iota(shape, axis):
    return lax.broadcasted_iota(jnp.int32, shape, axis)


def split(value):
    high = value.astype(BF16)
    return high, (value - high.astype(F32)).astype(BF16)


def gather_kernel(
    movie_hbm, foot_hbm, block_hbm, owner_hbm, slot_hbm,
    send, numbers, foot_sorted, block_sorted,
    movie, foot, index, projected, numbers_s, sem, movie_sem,
):
    small = [
        pltpu.make_async_copy(source, target, sem.at[number])
        for number, (source, target) in enumerate(
            [(block_hbm, index.at[0]), (owner_hbm, index.at[1]), (slot_hbm, index.at[2]), (foot_hbm, foot)]
        )
    ]
    for copy in small:
        copy.start()

    def movie_part(number):
        span = pl.ds(number * PART, PART)
        return pltpu.make_async_copy(movie_hbm.at[span], movie.at[span], movie_sem.at[number])

    for number in range(BLK // PART):
        movie_part(number).start()
    send[...] = jnp.zeros_like(send)
    projected[...] = jnp.zeros_like(projected)
    foot_sorted[ENT:, :] = jnp.zeros((WINDOW, VOX), F32)
    block_sorted[ENT:, :] = jnp.full((WINDOW, 128), -1.0, F32)
    for copy in small[:3]:
        copy.wait()
    blk, own, slt = index[0], index[1], index[2]
    entry = iota((8, 128), 0) * 128 + iota((8, 128), 1)
    key = (blk * ENT + entry).astype(F32)
    ownf = own.astype(F32)
    key_col, own_col, blk_col = key.T, ownf.T, blk.astype(F32).T
    before = iota((128, 128), 0) < iota((128, 128), 1)
    lane8 = (iota((128, 128), 1) * 8).astype(F32)
    owner_rank, block_rank = [], []
    less = jnp.zeros((128, 128), F32)
    for row in range(8):
        key_row, own_row = key[row : row + 1, :], ownf[row : row + 1, :]
        count_o = jnp.zeros((128, 128), F32)
        count_k = jnp.zeros((128, 128), F32)
        for col in range(8):
            count_k += jnp.where(key_col[:, col : col + 1] < key_row, 1.0, 0.0)
            if col <= row:
                same = own_col[:, col : col + 1] == own_row
                if col == row:
                    same = same & before
                count_o += jnp.where(same, 1.0, 0.0)
        owner_rank.append(jnp.sum(count_o, axis=0, keepdims=True))
        block_rank.append(jnp.sum(count_k, axis=0, keepdims=True))
        less += jnp.where(blk_col[:, row : row + 1] < lane8, 1.0, 0.0)
    rank = jnp.concatenate(owner_rank, axis=0).astype(jnp.int32)
    order = jnp.concatenate(block_rank, axis=0).astype(jnp.int32)
    core, far, near = (own >> 2) & 1, own >> 3, own & 3
    message = jnp.where(core == 0, far, 4 + near)
    member = jnp.where(core == 0, near, far)
    tile, z = lax.axis_index("tile"), lax.axis_index("plane")
    turned = (member - jnp.where(core == 0, z, tile // 2) + 4) & 3
    section = jnp.where(turned == 0, 3, jnp.where(turned == 2, 0, jnp.where(turned == 1, 1, 2)))
    numbers[0] = message * ROWS + 8 + section * CAP + rank
    numbers[1] = order
    numbers[2] = jnp.broadcast_to(jnp.sum(less, axis=0, keepdims=True), (8, 128)).astype(jnp.int32)
    to_smem = pltpu.make_async_copy(numbers, numbers_s, sem.at[4])
    to_smem.start()

    small[3].wait()
    foot_values = foot[...].astype(F32)
    sq_high, sq_low = split(foot_values * foot_values)
    ones = jnp.ones((8, 128), BF16)
    energy = lax.dot_general(ones, sq_high, NT, preferred_element_type=F32) + lax.dot_general(
        ones, sq_low, NT, preferred_element_type=F32
    )
    place = section * 128 + rank
    meta = jnp.zeros((24, 512), F32)
    sorted_wide = jnp.zeros((ENT, 256), F32)
    for row in range(8):
        lanes = slice(row * 128, row * 128 + 128)
        chosen = message[row : row + 1, :] == iota((8, 128), 0)
        en_high, en_low = split(energy[:, lanes])
        slots = (slt[row : row + 1, :] + 1).astype(F32)
        values = jnp.concatenate(
            [
                jnp.where(chosen, slots, 0.0),
                jnp.where(chosen, en_high.astype(F32), 0.0),
                jnp.where(chosen, en_low.astype(F32), 0.0),
            ],
            axis=0,
        ).astype(BF16)
        places = jnp.where(place[row : row + 1, :] == iota((512, 128), 0), 1.0, 0.0).astype(BF16)
        meta += lax.dot_general(values, places, NT, preferred_element_type=F32)
        permute = jnp.where(order[row : row + 1, :] == iota((ENT, 128), 0), 1.0, 0.0).astype(BF16)
        wide = jnp.concatenate(
            [
                foot[lanes, :],
                jnp.broadcast_to(blk_col[:, row : row + 1], (128, 128)).astype(BF16),
            ],
            axis=1,
        )
        sorted_wide += jnp.dot(permute, wide, preferred_element_type=F32)
    foot_sorted[:ENT, :] = sorted_wide[:, :128]
    block_sorted[:ENT, :] = sorted_wide[:, 128:]
    for m in range(8):
        for i in range(4):
            lanes = slice(i * 128, i * 128 + 128)
            base = m * ROWS
            send[base + i : base + i + 1, :] = meta[m : m + 1, lanes]
            send[base + 4 + i : base + 5 + i, :] = (
                meta[8 + m : 9 + m, lanes] + meta[16 + m : 17 + m, lanes]
            )
    to_smem.wait()

    def product(chunk, first):
        span = pl.ds(pl.multiple_of(first, 8), WINDOW)
        values, which = foot_sorted[span, :], block_sorted[span, :]
        left = jnp.concatenate(
            [
                jnp.where(which == (chunk * 8 + n).astype(F32), values, 0.0).astype(BF16)
                for n in range(8)
            ],
            axis=1,
        )
        right = movie[pl.ds(chunk * 8, 8)].reshape(8 * VOX, FR)
        projected[span, :] += jnp.dot(left, right, preferred_element_type=F32)

    @pl.loop(0, BLK // PART)
    def _(group):
        movie_part(group).wait()
        windows(numbers_s, group, product)

    @pl.loop(0, 8)
    def _(line):
        for lane in range(128):
            send[pl.ds(numbers_s[0, line, lane], 1), :] = projected[
                pl.ds(numbers_s[1, line, lane], 1), :
            ]


def windows(numbers, group, product):
    count = PART // 8
    fits = None
    for k in range(count):
        chunk = group * count + k
        begin = (numbers[2, 0, chunk] // 8) * 8
        inside = numbers[2, 0, chunk + 1] - begin <= WINDOW
        fits = inside if fits is None else fits & inside

    @pl.when(fits)
    def _():
        for k in range(count):
            chunk = group * count + k
            product(chunk, (numbers[2, 0, chunk] // 8) * 8)

    @pl.when(jnp.logical_not(fits))
    def _():
        @pl.loop(0, count)
        def _(k):
            chunk = group * count + k
            begin = (numbers[2, 0, chunk] // 8) * 8
            number = jnp.maximum(1, (numbers[2, 0, chunk + 1] - begin + WINDOW - 1) // WINDOW)

            @pl.loop(0, number)
            def _(step):
                product(chunk, begin + step * WINDOW)


def gather(movie, footprint, entry_block, entry_owner, entry_slot):
    shape = jax.ShapeDtypeStruct
    in_place = pl.BlockSpec(memory_space=pltpu.HBM)
    return pl.pallas_call(
        gather_kernel,
        out_shape=(
            shape((8 * ROWS, FR), F32),
            shape((3, 8, 128), jnp.int32),
            shape((ENT + WINDOW, VOX), F32),
            shape((ENT + WINDOW, 128), F32),
        ),
        in_specs=[in_place] * 5,
        out_specs=(VMEM,) * 4,
        scratch_shapes=[
            pltpu.VMEM((BLK, VOX, FR), BF16),
            pltpu.VMEM((ENT, VOX), BF16),
            pltpu.VMEM((3, 8, 128), jnp.int32),
            pltpu.VMEM((ENT + WINDOW, FR), F32),
            pltpu.SMEM((3, 8, 128), jnp.int32),
            pltpu.SemaphoreType.DMA((5,)),
            pltpu.SemaphoreType.DMA((BLK // PART,)),
        ],
        compiler_params=pltpu.CompilerParams(vmem_limit_bytes=48 << 20),
        name="project",
    )(
        *(
            pltpu.with_memory_space_constraint(array, pltpu.HBM)
            for array in (
                movie, footprint, entry_block.reshape(8, 128),
                entry_owner.reshape(8, 128), entry_slot.reshape(8, 128),
            )
        )
    )


def pick(rows, sub):
    chosen = jnp.where(sub // 2 == 0, rows[0:1, :], rows[1:2, :])
    lane = iota((SUB, 128), 1) - lax.rem(sub, 2) * SUB
    return jnp.sum(jnp.where(lane == iota((SUB, 128), 0), chosen, 0.0), axis=1, keepdims=True)


def delayed(parts, steps):
    if steps >= 128:
        hop = steps // 128
        return [None] * hop + parts[: len(parts) - hop]
    lane = iota((SUB, 128), 1)
    rolled = [pltpu.roll(part, steps, 1) for part in parts]
    out = [jnp.where(lane < steps, 0.0, rolled[0])]
    for index in range(1, len(parts)):
        out.append(jnp.where(lane < steps, rolled[index - 1], rolled[index]))
    return out


def first_order(parts, powers):
    for level, power in enumerate(powers):
        moved = delayed(parts, 1 << level)
        parts = [
            part if late is None else part + power * late for part, late in zip(parts, moved)
        ]
    return parts


def sweeps(target, slow, fast):
    lag_one, lag_two = slow + fast, -slow * fast
    slow_powers, fast_powers = [slow], [fast]
    for _ in range(8):
        slow_powers.append(slow_powers[-1] * slow_powers[-1])
        fast_powers.append(fast_powers[-1] * fast_powers[-1])
    slow_share = slow / (slow - fast)
    fast_share = fast / (slow - fast)
    estimate = target
    for sweep in range(SWEEPS):
        one, two = delayed(estimate, 1), delayed(estimate, 2)
        spikes = [
            jnp.maximum(now - lag_one * a - lag_two * b, 0.0)
            for now, a, b in zip(estimate, one, two)
        ]
        slow_part = first_order(spikes, slow_powers)
        fast_part = first_order(spikes, fast_powers)
        calcium = [slow_share * a - fast_share * b for a, b in zip(slow_part, fast_part)]
        if sweep + 1 < SWEEPS:
            estimate = [0.5 * (a + b) for a, b in zip(target, calcium)]
    return calcium


def exchange_kernel(
    send, traces, slow, fast, back, calcium,
    got, hot, part, parts, piece, whole, reply,
    s1, r1, s2, r2, s3, r3, s4, r4, local,
):
    tile, y, z = lax.axis_index("tile"), lax.axis_index("tm"), lax.axis_index("plane")
    x, c = tile // 2, lax.rem(tile, 2)
    d = 1 - c
    p = x * d + z * c
    q = z * d + x * c

    def turn(value, by):
        return lax.rem(value + by, 4)

    def mine(pos, core):
        return (d * (2 * pos + core) + c * (2 * x + core), y, d * z + c * pos)

    def other(pos):
        return (c * 2 * pos + d * (2 * x + 1), y, c * z + d * pos)

    def column(pos, frame):
        return (d * 2 * x + c * (2 * pos + 1), frame, d * pos + c * z)

    reach = TURNS[:3]
    barrier = pltpu.get_barrier_semaphore()
    met = [mine(turn(p, by), c) for by in reach]
    met += [mine(turn(p, by), d) for by in TURNS]
    met += [other(turn(q, by)) for by in reach]
    met += [column(turn(q, dq), turn(y, dy)) for dq in TURNS for dy in TURNS if dq or dy]
    for device in met:
        pl.semaphore_signal(barrier, inc=1, device_id=device, device_id_type=MESH)
    pl.semaphore_wait(barrier, len(met))

    def remote(source, target, sends, arrives, device):
        return pltpu.make_async_remote_copy(
            src_ref=source, dst_ref=target, send_sem=sends, recv_sem=arrives,
            device_id=device, device_id_type=MESH,
        )

    def rows_of(section):
        return (0, 8 + CAP) if section == 0 else (8 + CAP * section, CAP)

    def message(index, section):
        first, count = rows_of(section)
        return send.at[pl.ds(pl.multiple_of(index * ROWS + first, 8), count), :]

    def landing(index, section):
        first, count = rows_of(section)
        return got.at[index, pl.ds(first, count), :]

    started = []

    def start(copy):
        copy.start()
        started.append(copy)

    own = pltpu.make_async_copy(
        send.at[pl.ds(pl.multiple_of((c * 4 + p) * ROWS, 8), ROWS), :], got.at[p * 2 + c], local.at[0]
    )
    own.start()
    for section in range(4):
        for by in TURNS:
            if by:
                index = c * 4 + turn(p, by)
                start(
                    remote(
                        message(index, section), landing(p * 2 + c, section),
                        s1.at[index * 4 + section], r1.at[(p * 2 + c) * 4 + section],
                        mine(turn(p, by), c),
                    )
                )
            index = d * 4 + turn(q, by)
            start(
                remote(
                    message(index, section), landing(q * 2 + c, section),
                    s1.at[index * 4 + section], r1.at[(q * 2 + c) * 4 + section],
                    other(turn(q, by)),
                )
            )

    slots_iota = (iota((OWN, 128), 0) + 1).astype(F32)
    ones = jnp.ones((8, 128), BF16)
    blank = jnp.zeros((128 - CAP, FR), BF16)
    top = iota((8, 128), 0) == 0
    sources = [(0, 0), (0, 1), (1, 0), (1, 1), (3, 0), (3, 1), (2, 0), (2, 1)]
    own.wait()
    for section in range(4):
        total = jnp.zeros((OWN, FR), F32)
        weight = jnp.zeros((OWN, 128), F32)
        first = 8 + CAP * section
        for by, flip in sources:
            source = turn(p, by) * 2 + (d if flip else c)
            if by or flip:
                remote(
                    message(0, section), landing(source, section), s1.at[0],
                    r1.at[source * 4 + section], mine(turn(p, by), c),
                ).wait_recv()
            match = slots_iota == got[source, section : section + 1, :]
            chosen = jnp.where(match, 1.0, 0.0).astype(BF16)
            hot[source, section] = chosen
            weight = weight + jnp.where(match, got[source, 4 + section : 5 + section, :], 0.0)
            high, low = split(got[source, first : first + CAP, :])
            total = total + jnp.dot(
                jnp.concatenate([chosen, chosen], axis=1),
                jnp.concatenate([high, blank, low, blank], axis=0),
                preferred_element_type=F32,
            )
        if section == 3:
            total = total + traces[...]
        high, low = split(weight)
        energy = lax.dot_general(ones, high, NT, preferred_element_type=F32) + lax.dot_general(
            ones, low, NT, preferred_element_type=F32
        )
        energy = jnp.where(top, energy[:, :128], energy[:, 128:])
        for sub in range(4):
            part[section, sub, :SUB, :] = total[sub * SUB : (sub + 1) * SUB, :]
            part[section, sub, SUB:, :] = energy
        tq = turn(q, TURNS[section])
        for dy in TURNS:
            ty = turn(y, dy)
            if section == 3 and dy == 0:
                own = pltpu.make_async_copy(part.at[section, y], parts.at[q, y], local.at[1])
                own.start()
            else:
                start(
                    remote(
                        part.at[section, ty], parts.at[q, y], s2.at[section * 4 + dy],
                        r2.at[q * 4 + y], column(tq, ty),
                    )
                )
    own.wait()
    for dq in TURNS:
        for dy in TURNS:
            if dq or dy:
                fq, fy = turn(q, dq), turn(y, dy)
                remote(
                    part.at[0, 0], parts.at[fq, fy], s2.at[0], r2.at[fq * 4 + fy], column(fq, fy)
                ).wait_recv()
    energy = parts[0, 0, SUB : SUB + 2, :]
    for other_q in range(1, 4):
        energy = energy + parts[other_q, 0, SUB : SUB + 2, :]
    scale = pick(energy, y) + 1.0
    target = []
    for frame in range(4):
        total = parts[0, frame, :SUB, :]
        for other_q in range(1, 4):
            total = total + parts[other_q, frame, :SUB, :]
        target.append(total / scale)
    traced = sweeps(target, pick(slow[...], y), pick(fast[...], y))
    for frame in range(4):
        piece[frame] = traced[frame]

    for section in (3, 1, 2, 0):
        tq = turn(q, TURNS[section])
        for dy in TURNS:
            ty = turn(y, dy)
            if section == 3 and dy == 0:
                own = pltpu.make_async_copy(piece.at[y], whole.at[q, y], local.at[2])
                own.start()
            else:
                start(
                    remote(
                        piece.at[ty], whole.at[q, y], s3.at[section * 4 + dy], r3.at[q * 4 + y],
                        column(tq, ty),
                    )
                )
    own.wait()

    def answer(index, section):
        return back.at[pl.ds(pl.multiple_of(index * ROWS + 8 + CAP * section, 8), CAP), :]

    for section in (3, 1, 2, 0):
        fq = turn(q, TURNS[section])
        for dy in TURNS:
            if section != 3 or dy:
                fy = turn(y, dy)
                remote(
                    piece.at[0], whole.at[fq, fy], s3.at[0], r3.at[fq * 4 + fy], column(fq, fy)
                ).wait_recv()
        if section == 3:
            for sub in range(4):
                calcium[sub * SUB : (sub + 1) * SUB, :] = whole[q, sub]
        rows = whole[fq].reshape(OWN, FR).astype(BF16)
        for order, (by, flip) in enumerate(sources[::-1]):
            core = d if flip else c
            source = turn(p, by) * 2 + core
            picked = lax.dot_general(hot[source, section], rows, TN, preferred_element_type=F32)
            reply[source, section] = picked[:CAP, :]
            if by or flip:
                start(
                    remote(
                        reply.at[source, section], answer(c * 4 + p, section),
                        s4.at[order * 4 + section], r4.at[(c * 4 + p) * 4 + section],
                        mine(turn(p, by), core),
                    )
                )
            else:
                own = pltpu.make_async_copy(
                    reply.at[source, section], answer(c * 4 + p, section), local.at[3 + section]
                )
                own.start()
                started.append(own)
    for section in (3, 1, 2, 0):
        for by in TURNS[::-1]:
            for core, pos in ((d, turn(q, by)), (c, turn(p, by))):
                if by == 0 and core is c:
                    continue
                index = core * 4 + pos
                remote(
                    reply.at[0, 0], answer(index, section), s4.at[0], r4.at[index * 4 + section],
                    other(q),
                ).wait_recv()
    for copy in started:
        if copy.is_remote:
            copy.wait_send()
        else:
            copy.wait()


def exchange(send, traces, slow_root, fast_root):
    dma = pltpu.SemaphoreType.DMA
    return pl.pallas_call(
        exchange_kernel,
        out_shape=(
            jax.ShapeDtypeStruct((8 * ROWS, FR), F32),
            jax.ShapeDtypeStruct((OWN, FR), F32),
        ),
        in_specs=[VMEM] * 4,
        out_specs=(VMEM, VMEM),
        scratch_shapes=[
            pltpu.VMEM((8, ROWS, FR), F32),
            pltpu.VMEM((8, 4, OWN, 128), BF16),
            pltpu.VMEM((4, 4, PIECE, FR), F32),
            pltpu.VMEM((4, 4, PIECE, FR), F32),
            pltpu.VMEM((4, SUB, FR), F32),
            pltpu.VMEM((4, 4, SUB, FR), F32),
            pltpu.VMEM((8, 4, CAP, FR), F32),
            dma((32,)), dma((32,)), dma((16,)), dma((16,)),
            dma((16,)), dma((16,)), dma((32,)), dma((32,)), dma((7,)),
        ],
        compiler_params=pltpu.CompilerParams(
            collective_id=1, has_side_effects=True, vmem_limit_bytes=48 << 20
        ),
        name="exchange",
    )(send, traces, slow_root.reshape(2, 128), fast_root.reshape(2, 128))


def rebuild_kernel(
    numbers_v, back, foot, block, calcium, out_hbm, calcium_out, numbers, rows, out, total, sem
):
    to_smem = pltpu.make_async_copy(numbers_v, numbers, sem.at[BLK // PART])
    to_smem.start()
    calcium_out[...] = calcium[...]
    rows[ENT:, :] = jnp.zeros((WINDOW, FR), F32)
    to_smem.wait()

    @pl.loop(0, 8)
    def _(line):
        for lane in range(128):
            rows[pl.ds(numbers[1, line, lane], 1), :] = back[
                pl.ds(numbers[0, line, lane], 1), :
            ]

    def product(chunk, first):
        span = pl.ds(pl.multiple_of(first, 8), WINDOW)
        values, which = rows[span, :], block[span, :]
        masked = jnp.concatenate(
            [
                jnp.where(which == (chunk * 8 + n).astype(F32), values, 0.0).astype(BF16)
                for n in range(8)
            ],
            axis=1,
        )
        left = foot[span, :].astype(BF16)
        return lax.dot_general(left, masked, TN, preferred_element_type=F32)

    def out_part(number):
        span = pl.ds(number * PART, PART)
        return pltpu.make_async_copy(out.at[span], out_hbm.at[span], sem.at[number])

    def store(chunk, result):
        for n in range(8):
            out[chunk * 8 + n] = result[:, n * FR : (n + 1) * FR].astype(BF16)

    count = PART // 8

    @pl.loop(0, BLK // PART)
    def _(group):
        fits = None
        for k in range(count):
            chunk = group * count + k
            inside = numbers[2, 0, chunk + 1] - (numbers[2, 0, chunk] // 8) * 8 <= WINDOW
            fits = inside if fits is None else fits & inside

        @pl.when(fits)
        def _():
            for k in range(count):
                chunk = group * count + k
                store(chunk, product(chunk, (numbers[2, 0, chunk] // 8) * 8))

        @pl.when(jnp.logical_not(fits))
        def _():
            @pl.loop(0, count)
            def _(k):
                chunk = group * count + k
                begin = (numbers[2, 0, chunk] // 8) * 8
                number = jnp.maximum(1, (numbers[2, 0, chunk + 1] - begin + WINDOW - 1) // WINDOW)
                total[...] = product(chunk, begin)

                @pl.loop(1, number)
                def _(step):
                    total[...] += product(chunk, begin + step * WINDOW)

                store(chunk, total[...])

        out_part(group).start()

    @pl.loop(0, BLK // PART)
    def _(group):
        out_part(group).wait()


def rebuild(numbers, back, foot, block, calcium):
    return pl.pallas_call(
        rebuild_kernel,
        out_shape=(
            jax.ShapeDtypeStruct((BLK, VOX, FR), BF16),
            jax.ShapeDtypeStruct((OWN, FR), F32),
        ),
        in_specs=[VMEM] * 5,
        out_specs=(pl.BlockSpec(memory_space=pl.ANY), VMEM),
        scratch_shapes=[
            pltpu.SMEM((3, 8, 128), jnp.int32),
            pltpu.VMEM((ENT + WINDOW, FR), F32),
            pltpu.VMEM((BLK, VOX, FR), BF16),
            pltpu.VMEM((VOX, 8 * FR), F32),
            pltpu.SemaphoreType.DMA((BLK // PART + 1,)),
        ],
        compiler_params=pltpu.CompilerParams(vmem_limit_bytes=48 << 20),
        name="rebuild",
    )(numbers, back, foot, block, calcium)


def shards(movie, footprint, entry_block, entry_owner, entry_slot, traces, slow_root, fast_root):
    send, numbers, foot, block = gather(
        movie, footprint, entry_block, entry_owner, entry_slot
    )
    back, calcium = exchange(send, traces, slow_root, fast_root)
    return rebuild(numbers, back, foot, block, calcium)


def solution(mesh):
    owners = ("tile", "plane")
    placed = (
        P(owners, None, "tm"),
        P(owners, None),
        P(owners),
        P(owners, None),
        P(owners),
        P(owners, "tm"),
        P(owners),
        P(owners),
    )
    return jax.shard_map(
        shards,
        mesh=mesh,
        in_specs=placed,
        out_specs=(P(owners, None, "tm"), P(owners, "tm")),
        check_vma=False,
    )
```

```python
import jax
import jax.numpy as jnp
from jax import lax
from jax.experimental import pallas as pl
from jax.experimental.pallas import tpu as pltpu
from jax.sharding import PartitionSpec as P

SWEEPS = 4
TURNS = (2, 1, 3, 0)
CAP = 96
OWN = 256
ENT = 1024
VOX = 128
FR = 128
BLK = 256
MSG = 4 * CAP
ROWS = MSG + 8
SUB = OWN // 4
PIECE = SUB + 8
WINDOW = 64
PART = 64
MESH = pl.DeviceIdType.MESH
F32 = jnp.float32
BF16 = jnp.bfloat16
VMEM = pl.BlockSpec(memory_space=pltpu.VMEM)
NT = (((1,), (1,)), ((), ()))
TN = (((0,), (0,)), ((), ()))


def iota(shape, axis):
    return lax.broadcasted_iota(jnp.int32, shape, axis)


def split(value):
    high = value.astype(BF16)
    return high, (value - high.astype(F32)).astype(BF16)


def gather_kernel(
    movie_hbm, foot_hbm, block_hbm, owner_hbm, slot_hbm,
    projected, labels, inverse, numbers, foot_sorted, block_sorted,
    movie, foot, index, numbers_s, sem, movie_sem,
):
    small = [
        pltpu.make_async_copy(source, target, sem.at[number])
        for number, (source, target) in enumerate(
            [(block_hbm, index.at[0]), (owner_hbm, index.at[1]), (slot_hbm, index.at[2]), (foot_hbm, foot)]
        )
    ]
    for copy in small:
        copy.start()

    def movie_part(number):
        span = pl.ds(number * PART, PART)
        return pltpu.make_async_copy(movie_hbm.at[span], movie.at[span], movie_sem.at[number])

    for number in range(BLK // PART):
        movie_part(number).start()
    projected[...] = jnp.zeros_like(projected)
    foot_sorted[ENT:, :] = jnp.zeros((WINDOW, VOX), F32)
    block_sorted[ENT:, :] = jnp.full((WINDOW, 128), -1.0, F32)
    for copy in small[:3]:
        copy.wait()
    blk, own, slt = index[0], index[1], index[2]
    entry = iota((8, 128), 0) * 128 + iota((8, 128), 1)
    key = (blk * ENT + entry).astype(F32)
    ownf = own.astype(F32)
    key_col, own_col, blk_col = key.T, ownf.T, blk.astype(F32).T
    before = iota((128, 128), 0) < iota((128, 128), 1)
    lane8 = (iota((128, 128), 1) * 8).astype(F32)
    owner_rank, block_rank = [], []
    less = jnp.zeros((128, 128), F32)
    for row in range(8):
        key_row, own_row = key[row : row + 1, :], ownf[row : row + 1, :]
        count_o = jnp.zeros((128, 128), F32)
        count_k = jnp.zeros((128, 128), F32)
        for col in range(8):
            count_k += jnp.where(key_col[:, col : col + 1] < key_row, 1.0, 0.0)
            if col <= row:
                same = own_col[:, col : col + 1] == own_row
                if col == row:
                    same = same & before
                count_o += jnp.where(same, 1.0, 0.0)
        owner_rank.append(jnp.sum(count_o, axis=0, keepdims=True))
        block_rank.append(jnp.sum(count_k, axis=0, keepdims=True))
        less += jnp.where(blk_col[:, row : row + 1] < lane8, 1.0, 0.0)
    rank = jnp.concatenate(owner_rank, axis=0).astype(jnp.int32)
    order = jnp.concatenate(block_rank, axis=0).astype(jnp.int32)
    core, far, near = (own >> 2) & 1, own >> 3, own & 3
    message = jnp.where(core == 0, far, 4 + near)
    member = jnp.where(core == 0, near, far)
    tile, z = lax.axis_index("tile"), lax.axis_index("plane")
    turned = (member - jnp.where(core == 0, z, tile // 2) + 4) & 3
    section = jnp.where(turned == 0, 3, jnp.where(turned == 2, 0, jnp.where(turned == 1, 1, 2)))
    numbers[0] = message * ROWS + 8 + section * CAP + rank
    numbers[1] = order
    numbers[2] = jnp.broadcast_to(jnp.sum(less, axis=0, keepdims=True), (8, 128)).astype(jnp.int32)
    to_smem = pltpu.make_async_copy(numbers, numbers_s, sem.at[4])
    to_smem.start()

    small[3].wait()
    foot_values = foot[...].astype(F32)
    sq_high, sq_low = split(foot_values * foot_values)
    ones = jnp.ones((8, 128), BF16)
    energy = lax.dot_general(ones, sq_high, NT, preferred_element_type=F32) + lax.dot_general(
        ones, sq_low, NT, preferred_element_type=F32
    )
    place = section * 128 + rank
    meta = jnp.zeros((40, 512), F32)
    sorted_wide = jnp.zeros((ENT, 256), F32)
    for row in range(8):
        lanes = slice(row * 128, row * 128 + 128)
        chosen = message[row : row + 1, :] == iota((8, 128), 0)
        en_high, en_low = split(energy[:, lanes])
        slots = (slt[row : row + 1, :] + 1).astype(F32)
        sorted_at = order[row : row + 1, :] + 1
        values = jnp.concatenate(
            [
                jnp.where(chosen, slots, 0.0),
                jnp.where(chosen, en_high.astype(F32), 0.0),
                jnp.where(chosen, en_low.astype(F32), 0.0),
                jnp.where(chosen, (sorted_at >> 5).astype(F32), 0.0),
                jnp.where(chosen, (sorted_at & 31).astype(F32), 0.0),
            ],
            axis=0,
        ).astype(BF16)
        places = jnp.where(place[row : row + 1, :] == iota((512, 128), 0), 1.0, 0.0).astype(BF16)
        meta += lax.dot_general(values, places, NT, preferred_element_type=F32)
        permute = jnp.where(order[row : row + 1, :] == iota((ENT, 128), 0), 1.0, 0.0).astype(BF16)
        wide = jnp.concatenate(
            [
                foot[lanes, :],
                jnp.broadcast_to(blk_col[:, row : row + 1], (128, 128)).astype(BF16),
            ],
            axis=1,
        )
        sorted_wide += jnp.dot(permute, wide, preferred_element_type=F32)
    foot_sorted[:ENT, :] = sorted_wide[:, :128]
    block_sorted[:ENT, :] = sorted_wide[:, 128:]
    place_of = (meta[24:32, :] * 32.0 + meta[32:40, :]).astype(jnp.int32)
    place_of = jnp.where(place_of == 0, ENT, place_of - 1)
    weights = meta[8:16, :] + meta[16:24, :]
    for i in range(4):
        lanes = slice(i * 128, i * 128 + 128)
        inverse[i] = place_of[:, lanes]
        labels[:, i, :] = meta[:8, lanes]
        labels[:, 4 + i, :] = weights[:, lanes]
    to_smem.wait()

    def product(chunk, first):
        span = pl.ds(pl.multiple_of(first, 8), WINDOW)
        values, which = foot_sorted[span, :], block_sorted[span, :]
        left = jnp.concatenate(
            [
                jnp.where(which == (chunk * 8 + n).astype(F32), values, 0.0).astype(BF16)
                for n in range(8)
            ],
            axis=1,
        )
        right = movie[pl.ds(chunk * 8, 8)].reshape(8 * VOX, FR)
        projected[span, :] += jnp.dot(left, right, preferred_element_type=F32)

    @pl.loop(0, BLK // PART)
    def _(group):
        movie_part(group).wait()
        windows(numbers_s, group, product)


def windows(numbers, group, product):
    count = PART // 8
    fits = None
    for k in range(count):
        chunk = group * count + k
        begin = (numbers[2, 0, chunk] // 8) * 8
        inside = numbers[2, 0, chunk + 1] - begin <= WINDOW
        fits = inside if fits is None else fits & inside

    @pl.when(fits)
    def _():
        for k in range(count):
            chunk = group * count + k
            product(chunk, (numbers[2, 0, chunk] // 8) * 8)

    @pl.when(jnp.logical_not(fits))
    def _():
        @pl.loop(0, count)
        def _(k):
            chunk = group * count + k
            begin = (numbers[2, 0, chunk] // 8) * 8
            number = jnp.maximum(1, (numbers[2, 0, chunk + 1] - begin + WINDOW - 1) // WINDOW)

            @pl.loop(0, number)
            def _(step):
                product(chunk, begin + step * WINDOW)


def gather(movie, footprint, entry_block, entry_owner, entry_slot):
    shape = jax.ShapeDtypeStruct
    in_place = pl.BlockSpec(memory_space=pltpu.HBM)
    return pl.pallas_call(
        gather_kernel,
        out_shape=(
            shape((ENT + WINDOW, FR), F32),
            shape((8, 8, 128), F32),
            shape((4, 8, 128), jnp.int32),
            shape((3, 8, 128), jnp.int32),
            shape((ENT + WINDOW, VOX), F32),
            shape((ENT + WINDOW, 128), F32),
        ),
        in_specs=[in_place] * 5,
        out_specs=(VMEM,) * 6,
        scratch_shapes=[
            pltpu.VMEM((BLK, VOX, FR), BF16),
            pltpu.VMEM((ENT, VOX), BF16),
            pltpu.VMEM((3, 8, 128), jnp.int32),
            pltpu.SMEM((3, 8, 128), jnp.int32),
            pltpu.SemaphoreType.DMA((5,)),
            pltpu.SemaphoreType.DMA((BLK // PART,)),
        ],
        compiler_params=pltpu.CompilerParams(vmem_limit_bytes=48 << 20),
        name="project",
    )(
        *(
            pltpu.with_memory_space_constraint(array, pltpu.HBM)
            for array in (
                movie, footprint, entry_block.reshape(8, 128),
                entry_owner.reshape(8, 128), entry_slot.reshape(8, 128),
            )
        )
    )


def pick(rows, sub):
    chosen = jnp.where(sub // 2 == 0, rows[0:1, :], rows[1:2, :])
    lane = iota((SUB, 128), 1) - lax.rem(sub, 2) * SUB
    return jnp.sum(jnp.where(lane == iota((SUB, 128), 0), chosen, 0.0), axis=1, keepdims=True)


def delayed(parts, steps):
    if steps >= 128:
        hop = steps // 128
        return [None] * hop + parts[: len(parts) - hop]
    lane = iota((SUB, 128), 1)
    rolled = [pltpu.roll(part, steps, 1) for part in parts]
    out = [jnp.where(lane < steps, 0.0, rolled[0])]
    for index in range(1, len(parts)):
        out.append(jnp.where(lane < steps, rolled[index - 1], rolled[index]))
    return out


def first_order(parts, powers):
    for level, power in enumerate(powers):
        moved = delayed(parts, 1 << level)
        parts = [
            part if late is None else part + power * late for part, late in zip(parts, moved)
        ]
    return parts


def sweeps(target, slow, fast):
    lag_one, lag_two = slow + fast, -slow * fast
    slow_powers, fast_powers = [slow], [fast]
    for _ in range(8):
        slow_powers.append(slow_powers[-1] * slow_powers[-1])
        fast_powers.append(fast_powers[-1] * fast_powers[-1])
    slow_share = slow / (slow - fast)
    fast_share = fast / (slow - fast)
    estimate = target
    for sweep in range(SWEEPS):
        one, two = delayed(estimate, 1), delayed(estimate, 2)
        spikes = [
            jnp.maximum(now - lag_one * a - lag_two * b, 0.0)
            for now, a, b in zip(estimate, one, two)
        ]
        slow_part = first_order(spikes, slow_powers)
        fast_part = first_order(spikes, fast_powers)
        calcium = [slow_share * a - fast_share * b for a, b in zip(slow_part, fast_part)]
        if sweep + 1 < SWEEPS:
            estimate = [0.5 * (a + b) for a, b in zip(target, calcium)]
    return calcium


def exchange_kernel(
    projected, labels, inverse_v, traces, slow, fast, back, calcium,
    inverse, send, got, hot, part, parts, piece, whole, reply,
    s1, r1, s2, r2, s3, r3, s4, r4, local,
):
    tile, y, z = lax.axis_index("tile"), lax.axis_index("tm"), lax.axis_index("plane")
    x, c = tile // 2, lax.rem(tile, 2)
    d = 1 - c
    p = x * d + z * c
    q = z * d + x * c

    def turn(value, by):
        return lax.rem(value + by, 4)

    def mine(pos, core):
        return (d * (2 * pos + core) + c * (2 * x + core), y, d * z + c * pos)

    def other(pos):
        return (c * 2 * pos + d * (2 * x + 1), y, c * z + d * pos)

    def column(pos, frame):
        return (d * 2 * x + c * (2 * pos + 1), frame, d * pos + c * z)

    to_smem = pltpu.make_async_copy(inverse_v, inverse, local.at[0])
    to_smem.start()
    reach = TURNS[:3]
    barrier = pltpu.get_barrier_semaphore()
    met = [mine(turn(p, by), c) for by in reach]
    met += [mine(turn(p, by), d) for by in TURNS]
    met += [other(turn(q, by)) for by in reach]
    met += [column(turn(q, dq), turn(y, dy)) for dq in TURNS for dy in TURNS if dq or dy]
    for device in met:
        pl.semaphore_signal(barrier, inc=1, device_id=device, device_id_type=MESH)
    for index in range(8):
        send[index * ROWS : index * ROWS + 8, :] = labels[index]

    def place(section):
        @pl.loop(0, 8)
        def _(index):
            first = pl.multiple_of(index * ROWS + 8 + CAP * section, 8)
            for block in range(0, CAP, 8):
                rows = [
                    projected[pl.ds(inverse[section, index, block + row], 1), :] for row in range(8)
                ]
                send[pl.ds(first + block, 8), :] = jnp.concatenate(rows, axis=0)

    to_smem.wait()
    place(0)
    pl.semaphore_wait(barrier, len(met))

    def remote(source, target, sends, arrives, device):
        return pltpu.make_async_remote_copy(
            src_ref=source, dst_ref=target, send_sem=sends, recv_sem=arrives,
            device_id=device, device_id_type=MESH,
        )

    def rows_of(section):
        return (0, 8 + CAP) if section == 0 else (8 + CAP * section, CAP)

    def message(index, section):
        first, count = rows_of(section)
        return send.at[pl.ds(pl.multiple_of(index * ROWS + first, 8), count), :]

    def landing(index, section):
        first, count = rows_of(section)
        return got.at[index, pl.ds(first, count), :]

    started = []

    def start(copy):
        copy.start()
        started.append(copy)

    def send_section(section):
        for by in TURNS:
            if by:
                index = c * 4 + turn(p, by)
                start(
                    remote(
                        message(index, section), landing(p * 2 + c, section),
                        s1.at[index * 4 + section], r1.at[(p * 2 + c) * 4 + section],
                        mine(turn(p, by), c),
                    )
                )
            index = d * 4 + turn(q, by)
            start(
                remote(
                    message(index, section), landing(q * 2 + c, section),
                    s1.at[index * 4 + section], r1.at[(q * 2 + c) * 4 + section],
                    other(turn(q, by)),
                )
            )

    for section in range(4):
        if section:
            place(section)
        send_section(section)

    slots_iota = (iota((OWN, 128), 0) + 1).astype(F32)
    ones = jnp.ones((8, 128), BF16)
    blank = jnp.zeros((128 - CAP, FR), BF16)
    top = iota((8, 128), 0) == 0
    sources = [(0, 0), (0, 1), (1, 0), (1, 1), (3, 0), (3, 1), (2, 0), (2, 1)]
    for section in range(4):
        weight = jnp.zeros((OWN, 128), F32)
        lefts, rights = [], []
        first = 8 + CAP * section
        for by, flip in sources[1:]:
            source = turn(p, by) * 2 + (d if flip else c)
            remote(
                message(0, section), landing(source, section), s1.at[0],
                r1.at[source * 4 + section], mine(turn(p, by), c),
            ).wait_recv()
        for place_in, (by, flip) in enumerate(sources):
            if by or flip:
                source = turn(p, by) * 2 + (d if flip else c)
                slots = got[source, section : section + 1, :]
                energies = got[source, 4 + section : 5 + section, :]
                values = got[source, first : first + CAP, :]
            else:
                base = (c * 4 + p) * ROWS
                slots = labels[c * 4 + p, section : section + 1, :]
                energies = labels[c * 4 + p, 4 + section : 5 + section, :]
                values = send[pl.ds(pl.multiple_of(base + first, 8), CAP), :]
            match = slots_iota == slots
            chosen = jnp.where(match, 1.0, 0.0)
            hot[section, place_in * CAP : (place_in + 1) * CAP, :] = chosen.T[:CAP, :].astype(BF16)
            weight = weight + jnp.where(match, energies, 0.0)
            high, low = split(values)
            chosen = chosen.astype(BF16)
            lefts += [chosen, chosen]
            rights += [high, blank, low, blank]
        total = jnp.dot(
            jnp.concatenate(lefts, axis=1),
            jnp.concatenate(rights, axis=0),
            preferred_element_type=F32,
        )
        if section == 3:
            total = total + traces[...]
        high, low = split(weight)
        energy = lax.dot_general(ones, high, NT, preferred_element_type=F32) + lax.dot_general(
            ones, low, NT, preferred_element_type=F32
        )
        energy = jnp.where(top, energy[:, :128], energy[:, 128:])
        for sub in range(4):
            part[section, sub, :SUB, :] = total[sub * SUB : (sub + 1) * SUB, :]
            part[section, sub, SUB:, :] = energy
        tq = turn(q, TURNS[section])
        for dy in TURNS:
            ty = turn(y, dy)
            if section == 3 and dy == 0:
                own = pltpu.make_async_copy(part.at[section, y], parts.at[q, y], local.at[1])
                own.start()
            else:
                count = SUB if dy else PIECE
                start(
                    remote(
                        part.at[section, ty, pl.ds(0, count)], parts.at[q, y, pl.ds(0, count)],
                        s2.at[section * 4 + dy], r2.at[q * 4 + y], column(tq, ty),
                    )
                )
    own.wait()
    for dq in TURNS:
        for dy in TURNS:
            if dq or dy:
                fq, fy = turn(q, dq), turn(y, dy)
                count = SUB if dy else PIECE
                remote(
                    part.at[0, 0, pl.ds(0, count)], parts.at[fq, fy, pl.ds(0, count)], s2.at[0],
                    r2.at[fq * 4 + fy], column(fq, fy),
                ).wait_recv()
    energy = parts[0, y, SUB : SUB + 2, :]
    for other_q in range(1, 4):
        energy = energy + parts[other_q, y, SUB : SUB + 2, :]
    scale = pick(energy, y) + 1.0
    target = []
    for frame in range(4):
        total = parts[0, frame, :SUB, :]
        for other_q in range(1, 4):
            total = total + parts[other_q, frame, :SUB, :]
        target.append(total / scale)
    traced = sweeps(target, pick(slow[...], y), pick(fast[...], y))
    for frame in range(4):
        piece[frame] = traced[frame]

    for section in (3, 1, 2, 0):
        tq = turn(q, TURNS[section])
        for dy in TURNS:
            ty = turn(y, dy)
            if section == 3 and dy == 0:
                own = pltpu.make_async_copy(piece.at[y], whole.at[q, y], local.at[2])
                own.start()
            else:
                start(
                    remote(
                        piece.at[ty], whole.at[q, y], s3.at[section * 4 + dy], r3.at[q * 4 + y],
                        column(tq, ty),
                    )
                )
    own.wait()

    def answer(index, section):
        return back.at[pl.ds(pl.multiple_of(index * ROWS + 8 + CAP * section, 8), CAP), :]

    for section in (3, 1, 2, 0):
        fq = turn(q, TURNS[section])
        for dy in TURNS:
            if section != 3 or dy:
                fy = turn(y, dy)
                remote(
                    piece.at[0], whole.at[fq, fy], s3.at[0], r3.at[fq * 4 + fy], column(fq, fy)
                ).wait_recv()
        if section == 3:
            for sub in range(4):
                calcium[sub * SUB : (sub + 1) * SUB, :] = whole[q, sub]
        rows = whole[fq].reshape(OWN, FR).astype(BF16)
        reply[section] = jnp.dot(hot[section], rows, preferred_element_type=F32)
        for order in range(7, -1, -1):
            by, flip = sources[order]
            core = d if flip else c
            if by or flip:
                start(
                    remote(
                        reply.at[section, pl.ds(order * CAP, CAP)], answer(c * 4 + p, section),
                        s4.at[order * 4 + section], r4.at[(c * 4 + p) * 4 + section],
                        mine(turn(p, by), core),
                    )
                )
            else:
                own = pltpu.make_async_copy(
                    reply.at[section, pl.ds(order * CAP, CAP)], answer(c * 4 + p, section),
                    local.at[3 + section],
                )
                own.start()
                started.append(own)
    for section in (3, 1, 2, 0):
        for by in TURNS[::-1]:
            for core, pos in ((d, turn(q, by)), (c, turn(p, by))):
                if by == 0 and core is c:
                    continue
                index = core * 4 + pos
                remote(
                    reply.at[0, pl.ds(0, CAP)], answer(index, section), s4.at[0], r4.at[index * 4 + section],
                    other(q),
                ).wait_recv()
    for copy in started:
        if copy.is_remote:
            copy.wait_send()
        else:
            copy.wait()


def exchange(projected, labels, inverse, traces, slow_root, fast_root):
    dma = pltpu.SemaphoreType.DMA
    return pl.pallas_call(
        exchange_kernel,
        out_shape=(
            jax.ShapeDtypeStruct((8 * ROWS, FR), F32),
            jax.ShapeDtypeStruct((OWN, FR), F32),
        ),
        in_specs=[VMEM] * 6,
        out_specs=(VMEM, VMEM),
        scratch_shapes=[
            pltpu.SMEM((4, 8, 128), jnp.int32),
            pltpu.VMEM((8 * ROWS, FR), F32),
            pltpu.VMEM((8, ROWS, FR), F32),
            pltpu.VMEM((4, 8 * CAP, OWN), BF16),
            pltpu.VMEM((4, 4, PIECE, FR), F32),
            pltpu.VMEM((4, 4, PIECE, FR), F32),
            pltpu.VMEM((4, SUB, FR), F32),
            pltpu.VMEM((4, 4, SUB, FR), F32),
            pltpu.VMEM((4, 8 * CAP, FR), F32),
            dma((32,)), dma((32,)), dma((16,)), dma((16,)),
            dma((16,)), dma((16,)), dma((32,)), dma((32,)), dma((7,)),
        ],
        compiler_params=pltpu.CompilerParams(
            collective_id=1, has_side_effects=True, vmem_limit_bytes=48 << 20
        ),
        name="exchange",
    )(projected, labels, inverse, traces, slow_root.reshape(2, 128), fast_root.reshape(2, 128))


def rebuild_kernel(
    numbers_v, back, foot, block, calcium, out_hbm, calcium_out, numbers, rows, out, total, sem
):
    to_smem = pltpu.make_async_copy(numbers_v, numbers, sem.at[BLK // PART])
    to_smem.start()
    calcium_out[...] = calcium[...]
    rows[ENT:, :] = jnp.zeros((WINDOW, FR), F32)
    to_smem.wait()

    @pl.loop(0, 8)
    def _(line):
        for lane in range(128):
            rows[pl.ds(numbers[1, line, lane], 1), :] = back[
                pl.ds(numbers[0, line, lane], 1), :
            ]

    def product(chunk, first):
        span = pl.ds(pl.multiple_of(first, 8), WINDOW)
        values, which = rows[span, :], block[span, :]
        masked = jnp.concatenate(
            [
                jnp.where(which == (chunk * 8 + n).astype(F32), values, 0.0).astype(BF16)
                for n in range(8)
            ],
            axis=1,
        )
        left = foot[span, :].astype(BF16)
        return lax.dot_general(left, masked, TN, preferred_element_type=F32)

    def out_part(number):
        span = pl.ds(number * PART, PART)
        return pltpu.make_async_copy(out.at[span], out_hbm.at[span], sem.at[number])

    def store(chunk, result):
        for n in range(8):
            out[chunk * 8 + n] = result[:, n * FR : (n + 1) * FR].astype(BF16)

    count = PART // 8

    @pl.loop(0, BLK // PART)
    def _(group):
        fits = None
        for k in range(count):
            chunk = group * count + k
            inside = numbers[2, 0, chunk + 1] - (numbers[2, 0, chunk] // 8) * 8 <= WINDOW
            fits = inside if fits is None else fits & inside

        @pl.when(fits)
        def _():
            for k in range(count):
                chunk = group * count + k
                store(chunk, product(chunk, (numbers[2, 0, chunk] // 8) * 8))

        @pl.when(jnp.logical_not(fits))
        def _():
            @pl.loop(0, count)
            def _(k):
                chunk = group * count + k
                begin = (numbers[2, 0, chunk] // 8) * 8
                number = jnp.maximum(1, (numbers[2, 0, chunk + 1] - begin + WINDOW - 1) // WINDOW)
                total[...] = product(chunk, begin)

                @pl.loop(1, number)
                def _(step):
                    total[...] += product(chunk, begin + step * WINDOW)

                store(chunk, total[...])

        out_part(group).start()

    @pl.loop(0, BLK // PART)
    def _(group):
        out_part(group).wait()


def rebuild(numbers, back, foot, block, calcium):
    return pl.pallas_call(
        rebuild_kernel,
        out_shape=(
            jax.ShapeDtypeStruct((BLK, VOX, FR), BF16),
            jax.ShapeDtypeStruct((OWN, FR), F32),
        ),
        in_specs=[VMEM] * 5,
        out_specs=(pl.BlockSpec(memory_space=pl.ANY), VMEM),
        scratch_shapes=[
            pltpu.SMEM((3, 8, 128), jnp.int32),
            pltpu.VMEM((ENT + WINDOW, FR), F32),
            pltpu.VMEM((BLK, VOX, FR), BF16),
            pltpu.VMEM((VOX, 8 * FR), F32),
            pltpu.SemaphoreType.DMA((BLK // PART + 1,)),
        ],
        compiler_params=pltpu.CompilerParams(vmem_limit_bytes=48 << 20),
        name="rebuild",
    )(numbers, back, foot, block, calcium)


def shards(movie, footprint, entry_block, entry_owner, entry_slot, traces, slow_root, fast_root):
    projected, labels, inverse, numbers, foot, block = gather(
        movie, footprint, entry_block, entry_owner, entry_slot
    )
    back, calcium = exchange(projected, labels, inverse, traces, slow_root, fast_root)
    return rebuild(numbers, back, foot, block, calcium)


def solution(mesh):
    owners = ("tile", "plane")
    placed = (
        P(owners, None, "tm"),
        P(owners, None),
        P(owners),
        P(owners, None),
        P(owners),
        P(owners, "tm"),
        P(owners),
        P(owners),
    )
    return jax.shard_map(
        shards,
        mesh=mesh,
        in_specs=placed,
        out_specs=(P(owners, None, "tm"), P(owners, "tm")),
        check_vma=False,
    )
```

```python
import jax
import jax.numpy as jnp
from jax import lax
from jax.experimental import pallas as pl
from jax.experimental.pallas import tpu as pltpu
from jax.sharding import PartitionSpec as P

SWEEPS = 4
TURNS = (2, 1, 3, 0)
CAP = 96
OWN = 256
ENT = 1024
VOX = 128
FR = 128
BLK = 256
MSG = 4 * CAP
ROWS = MSG + 8
SUB = OWN // 4
PIECE = SUB + 8
WINDOW = 64
PART = 32
MESH = pl.DeviceIdType.MESH
F32 = jnp.float32
BF16 = jnp.bfloat16
VMEM = pl.BlockSpec(memory_space=pltpu.VMEM)
NT = (((1,), (1,)), ((), ()))
TN = (((0,), (0,)), ((), ()))


def iota(shape, axis):
    return lax.broadcasted_iota(jnp.int32, shape, axis)


def split(value):
    high = value.astype(BF16)
    return high, (value - high.astype(F32)).astype(BF16)


def gather_kernel(
    movie_hbm, foot_hbm, block_hbm, owner_hbm, slot_hbm,
    projected, labels, inverse, numbers, foot_sorted, block_sorted,
    movie, foot, index, numbers_s, sem,
):
    small = [
        pltpu.make_async_copy(source, target, sem.at[number])
        for number, (source, target) in enumerate(
            [(block_hbm, index.at[0]), (owner_hbm, index.at[1]), (slot_hbm, index.at[2]), (foot_hbm, foot)]
        )
    ]
    for copy in small:
        copy.start()

    load = pltpu.make_async_copy(movie_hbm, movie, sem.at[5])
    load.start()
    projected[...] = jnp.zeros_like(projected)
    foot_sorted[ENT:, :] = jnp.zeros((WINDOW, VOX), F32)
    block_sorted[ENT:, :] = jnp.full((WINDOW, 128), -1.0, F32)
    for copy in small[:3]:
        copy.wait()
    blk, own, slt = index[0], index[1], index[2]
    entry = iota((8, 128), 0) * 128 + iota((8, 128), 1)
    key = (blk * ENT + entry).astype(F32)
    ownf = own.astype(F32)
    key_col, own_col, blk_col = key.T, ownf.T, blk.astype(F32).T
    before = iota((128, 128), 0) < iota((128, 128), 1)
    lane8 = (iota((128, 128), 1) * 8).astype(F32)
    owner_rank, block_rank = [], []
    less = jnp.zeros((128, 128), F32)
    for row in range(8):
        key_row, own_row = key[row : row + 1, :], ownf[row : row + 1, :]
        count_o = jnp.zeros((128, 128), F32)
        count_k = jnp.zeros((128, 128), F32)
        for col in range(8):
            count_k += jnp.where(key_col[:, col : col + 1] < key_row, 1.0, 0.0)
            if col <= row:
                same = own_col[:, col : col + 1] == own_row
                if col == row:
                    same = same & before
                count_o += jnp.where(same, 1.0, 0.0)
        owner_rank.append(jnp.sum(count_o, axis=0, keepdims=True))
        block_rank.append(jnp.sum(count_k, axis=0, keepdims=True))
        less += jnp.where(blk_col[:, row : row + 1] < lane8, 1.0, 0.0)
    rank = jnp.concatenate(owner_rank, axis=0).astype(jnp.int32)
    order = jnp.concatenate(block_rank, axis=0).astype(jnp.int32)
    core, far, near = (own >> 2) & 1, own >> 3, own & 3
    message = jnp.where(core == 0, far, 4 + near)
    member = jnp.where(core == 0, near, far)
    tile, z = lax.axis_index("tile"), lax.axis_index("plane")
    turned = (member - jnp.where(core == 0, z, tile // 2) + 4) & 3
    section = jnp.where(turned == 0, 3, jnp.where(turned == 2, 0, jnp.where(turned == 1, 1, 2)))
    numbers[0] = message * ROWS + 8 + section * CAP + rank
    numbers[1] = order
    begins = jnp.broadcast_to(jnp.sum(less, axis=0, keepdims=True), (8, 128)).astype(jnp.int32)
    beyond = pltpu.roll(begins, 127, 1) - (begins >> 3) * 8 > WINDOW
    lane = iota((8, 128), 1)
    misfits = jnp.sum(
        jnp.where(beyond & (lane < BLK // 8), 1.0, 0.0), axis=1, keepdims=True
    ).astype(jnp.int32)
    numbers[2] = jnp.where(lane == 127, misfits, begins)
    to_smem = pltpu.make_async_copy(numbers, numbers_s, sem.at[4])
    to_smem.start()

    small[3].wait()
    foot_values = foot[...].astype(F32)
    sq_high, sq_low = split(foot_values * foot_values)
    ones = jnp.ones((8, 128), BF16)
    energy = lax.dot_general(ones, sq_high, NT, preferred_element_type=F32) + lax.dot_general(
        ones, sq_low, NT, preferred_element_type=F32
    )
    place = section * 128 + rank
    meta = jnp.zeros((40, 512), F32)
    sorted_wide = jnp.zeros((ENT, 256), F32)
    for row in range(8):
        lanes = slice(row * 128, row * 128 + 128)
        chosen = message[row : row + 1, :] == iota((8, 128), 0)
        en_high, en_low = split(energy[:, lanes])
        slots = (slt[row : row + 1, :] + 1).astype(F32)
        sorted_at = order[row : row + 1, :] + 1
        values = jnp.concatenate(
            [
                jnp.where(chosen, slots, 0.0),
                jnp.where(chosen, en_high.astype(F32), 0.0),
                jnp.where(chosen, en_low.astype(F32), 0.0),
                jnp.where(chosen, (sorted_at >> 5).astype(F32), 0.0),
                jnp.where(chosen, (sorted_at & 31).astype(F32), 0.0),
            ],
            axis=0,
        ).astype(BF16)
        places = jnp.where(place[row : row + 1, :] == iota((512, 128), 0), 1.0, 0.0).astype(BF16)
        meta += lax.dot_general(values, places, NT, preferred_element_type=F32)
        permute = jnp.where(order[row : row + 1, :] == iota((ENT, 128), 0), 1.0, 0.0).astype(BF16)
        wide = jnp.concatenate(
            [
                foot[lanes, :],
                jnp.broadcast_to(blk_col[:, row : row + 1], (128, 128)).astype(BF16),
            ],
            axis=1,
        )
        sorted_wide += jnp.dot(permute, wide, preferred_element_type=F32)
    foot_sorted[:ENT, :] = sorted_wide[:, :128]
    block_sorted[:ENT, :] = sorted_wide[:, 128:]
    place_of = (meta[24:32, :] * 32.0 + meta[32:40, :]).astype(jnp.int32)
    place_of = jnp.where(place_of == 0, ENT, place_of - 1)
    weights = meta[8:16, :] + meta[16:24, :]
    for i in range(4):
        lanes = slice(i * 128, i * 128 + 128)
        inverse[i] = place_of[:, lanes]
        labels[:, i, :] = meta[:8, lanes]
        labels[:, 4 + i, :] = weights[:, lanes]
    to_smem.wait()

    def product(chunk, begin, steps):
        right = movie[pl.ds(chunk * 8, 8)].reshape(8 * VOX, FR)

        def add(step):
            span = pl.ds(pl.multiple_of(begin + step * WINDOW, 8), WINDOW)
            values, which = foot_sorted[span, :], block_sorted[span, :]
            left = jnp.concatenate(
                [
                    jnp.where(which == jnp.asarray(chunk * 8 + n, F32), values, 0.0).astype(BF16)
                    for n in range(8)
                ],
                axis=1,
            )
            projected[span, :] += jnp.dot(left, right, preferred_element_type=F32)

        if isinstance(steps, int):
            add(0)
        else:
            pl.loop(0, steps)(add)

    load.wait()
    windows(numbers_s, product, lambda group: None)


def windows(numbers, product, after):
    count = PART // 8
    misfits = numbers[2, 0, 127]

    @pl.when(misfits == 0)
    def _():
        for group in range(BLK // PART):
            for chunk in range(group * count, (group + 1) * count):
                product(chunk, (numbers[2, 0, chunk] // 8) * 8, 1)
            after(group)

    @pl.when(misfits != 0)
    def _():
        @pl.loop(0, BLK // PART)
        def _(group):

            @pl.loop(group * count, (group + 1) * count)
            def _(chunk):
                begin = (numbers[2, 0, chunk] // 8) * 8
                steps = (numbers[2, 0, chunk + 1] - begin + WINDOW - 1) // WINDOW
                product(chunk, begin, jnp.maximum(1, steps))

            after(group)


def gather(movie, footprint, entry_block, entry_owner, entry_slot):
    shape = jax.ShapeDtypeStruct
    in_place = pl.BlockSpec(memory_space=pltpu.HBM)
    return pl.pallas_call(
        gather_kernel,
        out_shape=(
            shape((ENT + WINDOW, FR), F32),
            shape((8, 8, 128), F32),
            shape((4, 8, 128), jnp.int32),
            shape((3, 8, 128), jnp.int32),
            shape((ENT + WINDOW, VOX), F32),
            shape((ENT + WINDOW, 128), F32),
        ),
        in_specs=[in_place] * 5,
        out_specs=(VMEM,) * 6,
        scratch_shapes=[
            pltpu.VMEM((BLK, VOX, FR), BF16),
            pltpu.VMEM((ENT, VOX), BF16),
            pltpu.VMEM((3, 8, 128), jnp.int32),
            pltpu.SMEM((3, 8, 128), jnp.int32),
            pltpu.SemaphoreType.DMA((6,)),
        ],
        compiler_params=pltpu.CompilerParams(vmem_limit_bytes=48 << 20),
        name="project",
    )(
        *(
            pltpu.with_memory_space_constraint(array, pltpu.HBM)
            for array in (
                movie, footprint, entry_block.reshape(8, 128),
                entry_owner.reshape(8, 128), entry_slot.reshape(8, 128),
            )
        )
    )


def pick(rows, sub):
    chosen = jnp.where(sub // 2 == 0, rows[0:1, :], rows[1:2, :])
    lane = iota((SUB, 128), 1) - lax.rem(sub, 2) * SUB
    column = jnp.sum(jnp.where(lane == iota((SUB, 128), 0), chosen, 0.0), axis=1, keepdims=True)
    return jnp.broadcast_to(column, (SUB, 128))


def delayed(parts, steps):
    if steps >= 128:
        hop = steps // 128
        return [None] * hop + parts[: len(parts) - hop]
    lane = iota((SUB, 128), 1)
    rolled = [pltpu.roll(part, steps, 1) for part in parts]
    out = [jnp.where(lane < steps, 0.0, rolled[0])]
    for index in range(1, len(parts)):
        out.append(jnp.where(lane < steps, rolled[index - 1], rolled[index]))
    return out


def first_order(parts, powers):
    for level, power in enumerate(powers):
        moved = delayed(parts, 1 << level)
        parts = [
            part if late is None else part + power * late for part, late in zip(parts, moved)
        ]
    return parts


def sweeps(target, slow, fast):
    lag_one, lag_two = slow + fast, -slow * fast
    slow_powers, fast_powers = [slow], [fast]
    for _ in range(8):
        slow_powers.append(slow_powers[-1] * slow_powers[-1])
        fast_powers.append(fast_powers[-1] * fast_powers[-1])
    slow_share = slow / (slow - fast)
    fast_share = fast / (slow - fast)
    estimate = target
    for sweep in range(SWEEPS):
        one, two = delayed(estimate, 1), delayed(estimate, 2)
        spikes = [
            jnp.maximum(now - lag_one * a - lag_two * b, 0.0)
            for now, a, b in zip(estimate, one, two)
        ]
        slow_part = first_order(spikes, slow_powers)
        fast_part = first_order(spikes, fast_powers)
        calcium = [slow_share * a - fast_share * b for a, b in zip(slow_part, fast_part)]
        if sweep + 1 < SWEEPS:
            estimate = [0.5 * (a + b) for a, b in zip(target, calcium)]
    return calcium


def exchange_kernel(
    projected, labels, inverse_v, traces, slow, fast, back, calcium,
    inverse, send, got, hot, part, parts, piece, whole, reply,
    s1, r1, s2, r2, s3, r3, s4, r4, local,
):
    tile, y, z = lax.axis_index("tile"), lax.axis_index("tm"), lax.axis_index("plane")
    x, c = tile // 2, lax.rem(tile, 2)
    d = 1 - c
    p = x * d + z * c
    q = z * d + x * c

    def turn(value, by):
        return lax.rem(value + by, 4)

    def mine(pos, core):
        return (d * (2 * pos + core) + c * (2 * x + core), y, d * z + c * pos)

    def other(pos):
        return (c * 2 * pos + d * (2 * x + 1), y, c * z + d * pos)

    def column(pos, frame):
        return (d * 2 * x + c * (2 * pos + 1), frame, d * pos + c * z)

    to_smem = pltpu.make_async_copy(inverse_v, inverse, local.at[0])
    to_smem.start()
    reach = TURNS[:3]
    barrier = pltpu.get_barrier_semaphore()
    met = [mine(turn(p, by), c) for by in reach]
    met += [mine(turn(p, by), d) for by in TURNS]
    met += [other(turn(q, by)) for by in reach]
    met += [column(turn(q, dq), turn(y, dy)) for dq in TURNS for dy in TURNS if dq or dy]
    for device in met:
        pl.semaphore_signal(barrier, inc=1, device_id=device, device_id_type=MESH)
    for index in range(8):
        send[index * ROWS : index * ROWS + 8, :] = labels[index]

    def place(section):
        @pl.loop(0, 8)
        def _(index):
            first = pl.multiple_of(index * ROWS + 8 + CAP * section, 8)
            for block in range(0, CAP, 8):
                rows = [
                    projected[pl.ds(inverse[section, index, block + row], 1), :] for row in range(8)
                ]
                send[pl.ds(first + block, 8), :] = jnp.concatenate(rows, axis=0)

    to_smem.wait()
    place(0)
    pl.semaphore_wait(barrier, len(met))

    def remote(source, target, sends, arrives, device):
        return pltpu.make_async_remote_copy(
            src_ref=source, dst_ref=target, send_sem=sends, recv_sem=arrives,
            device_id=device, device_id_type=MESH,
        )

    def rows_of(section):
        return (0, 8 + CAP) if section == 0 else (8 + CAP * section, CAP)

    def message(index, section):
        first, count = rows_of(section)
        return send.at[pl.ds(pl.multiple_of(index * ROWS + first, 8), count), :]

    def landing(index, section):
        first, count = rows_of(section)
        return got.at[index, pl.ds(first, count), :]

    started = []

    def start(copy):
        copy.start()
        started.append(copy)

    def send_section(section):
        for by in TURNS:
            if by:
                index = c * 4 + turn(p, by)
                start(
                    remote(
                        message(index, section), landing(p * 2 + c, section),
                        s1.at[index * 4 + section], r1.at[(p * 2 + c) * 4 + section],
                        mine(turn(p, by), c),
                    )
                )
            index = d * 4 + turn(q, by)
            start(
                remote(
                    message(index, section), landing(q * 2 + c, section),
                    s1.at[index * 4 + section], r1.at[(q * 2 + c) * 4 + section],
                    other(turn(q, by)),
                )
            )

    for section in range(4):
        if section:
            place(section)
        if section >= 2:
            for copy in started[(section - 2) * 7 : (section - 1) * 7]:
                copy.wait_send()
        send_section(section)

    slots_iota = (iota((OWN, 128), 0) + 1).astype(F32)
    ones = jnp.ones((8, 128), BF16)
    blank = jnp.zeros((128 - CAP, FR), BF16)
    top = iota((8, 128), 0) == 0
    sources = [(0, 0), (0, 1), (1, 0), (1, 1), (3, 0), (3, 1), (2, 0), (2, 1)]
    for section in range(4):
        weight = jnp.zeros((OWN, 128), F32)
        lefts, rights = [], []
        first = 8 + CAP * section
        for by, flip in sources[1:]:
            source = turn(p, by) * 2 + (d if flip else c)
            remote(
                message(0, section), landing(source, section), s1.at[0],
                r1.at[source * 4 + section], mine(turn(p, by), c),
            ).wait_recv()
        for place_in, (by, flip) in enumerate(sources):
            if by or flip:
                source = turn(p, by) * 2 + (d if flip else c)
                slots = got[source, section : section + 1, :]
                energies = got[source, 4 + section : 5 + section, :]
                values = got[source, first : first + CAP, :]
            else:
                base = (c * 4 + p) * ROWS
                slots = labels[c * 4 + p, section : section + 1, :]
                energies = labels[c * 4 + p, 4 + section : 5 + section, :]
                values = send[pl.ds(pl.multiple_of(base + first, 8), CAP), :]
            match = slots_iota == slots
            chosen = jnp.where(match, 1.0, 0.0)
            hot[section, place_in * CAP : (place_in + 1) * CAP, :] = chosen.T[:CAP, :].astype(BF16)
            weight = weight + jnp.where(match, energies, 0.0)
            high, low = split(values)
            chosen = chosen.astype(BF16)
            lefts += [chosen, chosen]
            rights += [high, blank, low, blank]
        total = jnp.dot(
            jnp.concatenate(lefts, axis=1),
            jnp.concatenate(rights, axis=0),
            preferred_element_type=F32,
        )
        if section == 3:
            total = total + traces[...]
        high, low = split(weight)
        energy = lax.dot_general(ones, high, NT, preferred_element_type=F32) + lax.dot_general(
            ones, low, NT, preferred_element_type=F32
        )
        energy = jnp.where(top, energy[:, :128], energy[:, 128:])
        for sub in range(4):
            part[section, sub, :SUB, :] = total[sub * SUB : (sub + 1) * SUB, :]
            part[section, sub, SUB:, :] = energy
        tq = turn(q, TURNS[section])
        for dy in TURNS:
            ty = turn(y, dy)
            if section == 3 and dy == 0:
                own = pltpu.make_async_copy(part.at[section, y], parts.at[q, y], local.at[1])
                own.start()
            else:
                count = SUB if dy else PIECE
                start(
                    remote(
                        part.at[section, ty, pl.ds(0, count)], parts.at[q, y, pl.ds(0, count)],
                        s2.at[section * 4 + dy], r2.at[q * 4 + y], column(tq, ty),
                    )
                )
    own.wait()
    for dq in TURNS:
        for dy in TURNS:
            if dq or dy:
                fq, fy = turn(q, dq), turn(y, dy)
                count = SUB if dy else PIECE
                remote(
                    part.at[0, 0, pl.ds(0, count)], parts.at[fq, fy, pl.ds(0, count)], s2.at[0],
                    r2.at[fq * 4 + fy], column(fq, fy),
                ).wait_recv()
    energy = parts[0, y, SUB : SUB + 2, :]
    for other_q in range(1, 4):
        energy = energy + parts[other_q, y, SUB : SUB + 2, :]
    scale = 1.0 / (pick(energy, y) + 1.0)
    target = []
    for frame in range(4):
        total = parts[0, frame, :SUB, :]
        for other_q in range(1, 4):
            total = total + parts[other_q, frame, :SUB, :]
        target.append(total * scale)
    traced = sweeps(target, pick(slow[...], y), pick(fast[...], y))
    for frame in range(4):
        piece[frame] = traced[frame]

    for section in (3, 1, 2, 0):
        tq = turn(q, TURNS[section])
        for dy in TURNS:
            ty = turn(y, dy)
            if section == 3 and dy == 0:
                own = pltpu.make_async_copy(piece.at[y], whole.at[q, y], local.at[2])
                own.start()
            else:
                start(
                    remote(
                        piece.at[ty], whole.at[q, y], s3.at[section * 4 + dy], r3.at[q * 4 + y],
                        column(tq, ty),
                    )
                )
    own.wait()

    def answer(index, section):
        return back.at[pl.ds(pl.multiple_of(index * ROWS + 8 + CAP * section, 8), CAP), :]

    for section in (3, 1, 2, 0):
        fq = turn(q, TURNS[section])
        for dy in TURNS:
            if section != 3 or dy:
                fy = turn(y, dy)
                remote(
                    piece.at[0], whole.at[fq, fy], s3.at[0], r3.at[fq * 4 + fy], column(fq, fy)
                ).wait_recv()
        if section == 3:
            for sub in range(4):
                calcium[sub * SUB : (sub + 1) * SUB, :] = whole[q, sub]
        rows = whole[fq].reshape(OWN, FR).astype(BF16)
        reply[section] = jnp.dot(hot[section], rows, preferred_element_type=F32)
        for order in range(7, -1, -1):
            by, flip = sources[order]
            core = d if flip else c
            if by or flip:
                start(
                    remote(
                        reply.at[section, pl.ds(order * CAP, CAP)], answer(c * 4 + p, section),
                        s4.at[order * 4 + section], r4.at[(c * 4 + p) * 4 + section],
                        mine(turn(p, by), core),
                    )
                )
            else:
                own = pltpu.make_async_copy(
                    reply.at[section, pl.ds(order * CAP, CAP)], answer(c * 4 + p, section),
                    local.at[3 + section],
                )
                own.start()
                started.append(own)
    for section in (3, 1, 2, 0):
        for by in TURNS[::-1]:
            for core, pos in ((d, turn(q, by)), (c, turn(p, by))):
                if by == 0 and core is c:
                    continue
                index = core * 4 + pos
                remote(
                    reply.at[0, pl.ds(0, CAP)], answer(index, section), s4.at[0], r4.at[index * 4 + section],
                    other(q),
                ).wait_recv()
    for copy in started[14:]:
        if copy.is_remote:
            copy.wait_send()
        else:
            copy.wait()


def exchange(projected, labels, inverse, traces, slow_root, fast_root):
    dma = pltpu.SemaphoreType.DMA
    return pl.pallas_call(
        exchange_kernel,
        out_shape=(
            jax.ShapeDtypeStruct((8 * ROWS, FR), F32),
            jax.ShapeDtypeStruct((OWN, FR), F32),
        ),
        in_specs=[VMEM] * 6,
        out_specs=(VMEM, VMEM),
        scratch_shapes=[
            pltpu.SMEM((4, 8, 128), jnp.int32),
            pltpu.VMEM((8 * ROWS, FR), F32),
            pltpu.VMEM((8, ROWS, FR), F32),
            pltpu.VMEM((4, 8 * CAP, OWN), BF16),
            pltpu.VMEM((4, 4, PIECE, FR), F32),
            pltpu.VMEM((4, 4, PIECE, FR), F32),
            pltpu.VMEM((4, SUB, FR), F32),
            pltpu.VMEM((4, 4, SUB, FR), F32),
            pltpu.VMEM((4, 8 * CAP, FR), F32),
            dma((32,)), dma((32,)), dma((16,)), dma((16,)),
            dma((16,)), dma((16,)), dma((32,)), dma((32,)), dma((7,)),
        ],
        compiler_params=pltpu.CompilerParams(
            collective_id=1, has_side_effects=True, vmem_limit_bytes=48 << 20
        ),
        name="exchange",
    )(projected, labels, inverse, traces, slow_root.reshape(2, 128), fast_root.reshape(2, 128))


def rebuild_kernel(
    numbers_v, back, foot, block, calcium, out_hbm, calcium_out, numbers, rows, out, total, sem
):
    to_smem = pltpu.make_async_copy(numbers_v, numbers, sem.at[BLK // PART])
    to_smem.start()
    calcium_out[...] = calcium[...]
    rows[ENT:, :] = jnp.zeros((WINDOW, FR), F32)
    to_smem.wait()

    @pl.loop(0, 8)
    def _(line):
        for lane in range(128):
            rows[pl.ds(numbers[1, line, lane], 1), :] = back[
                pl.ds(numbers[0, line, lane], 1), :
            ]

    def term(chunk, first):
        span = pl.ds(pl.multiple_of(first, 8), WINDOW)
        values, which = rows[span, :], block[span, :]
        masked = jnp.concatenate(
            [
                jnp.where(which == jnp.asarray(chunk * 8 + n, F32), values, 0.0).astype(BF16)
                for n in range(8)
            ],
            axis=1,
        )
        left = foot[span, :].astype(BF16)
        return lax.dot_general(left, masked, TN, preferred_element_type=F32)

    def out_part(number):
        span = pl.ds(number * PART, PART)
        return pltpu.make_async_copy(out.at[span], out_hbm.at[span], sem.at[number])

    def product(chunk, begin, steps):
        result = term(chunk, begin)
        if not isinstance(steps, int):
            total[...] = result

            @pl.loop(1, steps)
            def _(step):
                total[...] += term(chunk, begin + step * WINDOW)

            result = total[...]
        for n in range(8):
            out[chunk * 8 + n] = result[:, n * FR : (n + 1) * FR].astype(BF16)

    windows(numbers, product, lambda group: out_part(group).start())

    @pl.loop(0, BLK // PART)
    def _(group):
        out_part(group).wait()


def rebuild(numbers, back, foot, block, calcium):
    return pl.pallas_call(
        rebuild_kernel,
        out_shape=(
            jax.ShapeDtypeStruct((BLK, VOX, FR), BF16),
            jax.ShapeDtypeStruct((OWN, FR), F32),
        ),
        in_specs=[VMEM] * 5,
        out_specs=(pl.BlockSpec(memory_space=pl.ANY), VMEM),
        scratch_shapes=[
            pltpu.SMEM((3, 8, 128), jnp.int32),
            pltpu.VMEM((ENT + WINDOW, FR), F32),
            pltpu.VMEM((BLK, VOX, FR), BF16),
            pltpu.VMEM((VOX, 8 * FR), F32),
            pltpu.SemaphoreType.DMA((BLK // PART + 1,)),
        ],
        compiler_params=pltpu.CompilerParams(vmem_limit_bytes=48 << 20),
        name="rebuild",
    )(numbers, back, foot, block, calcium)


def shards(movie, footprint, entry_block, entry_owner, entry_slot, traces, slow_root, fast_root):
    projected, labels, inverse, numbers, foot, block = gather(
        movie, footprint, entry_block, entry_owner, entry_slot
    )
    back, calcium = exchange(projected, labels, inverse, traces, slow_root, fast_root)
    return rebuild(numbers, back, foot, block, calcium)


def solution(mesh):
    owners = ("tile", "plane")
    placed = (
        P(owners, None, "tm"),
        P(owners, None),
        P(owners),
        P(owners, None),
        P(owners),
        P(owners, "tm"),
        P(owners),
        P(owners),
    )
    return jax.shard_map(
        shards,
        mesh=mesh,
        in_specs=placed,
        out_specs=(P(owners, None, "tm"), P(owners, "tm")),
        check_vma=False,
    )
```

```python
import jax
import jax.numpy as jnp
from jax import lax
from jax.experimental import pallas as pl
from jax.experimental.pallas import tpu as pltpu
from jax.sharding import PartitionSpec as P

SWEEPS = 4
TURNS = (2, 1, 3, 0)
CAP = 96
OWN = 256
ENT = 1024
VOX = 128
FR = 128
BLK = 256
MSG = 4 * CAP
ROWS = MSG + 8
SUB = OWN // 4
PIECE = SUB + 8
WINDOW = 64
PART = 32
STAGES = (352, 640, 896, 1024)
MESH = pl.DeviceIdType.MESH
F32 = jnp.float32
BF16 = jnp.bfloat16
VMEM = pl.BlockSpec(memory_space=pltpu.VMEM)
NT = (((1,), (1,)), ((), ()))
TN = (((0,), (0,)), ((), ()))


def iota(shape, axis):
    return lax.broadcasted_iota(jnp.int32, shape, axis)


def split(value):
    high = value.astype(BF16)
    return high, (value - high.astype(F32)).astype(BF16)


def gather_kernel(
    movie_hbm, foot_hbm, block_hbm, owner_hbm, slot_hbm,
    projected, labels, inverse, begins_out, places_out, foot_sorted, block_sorted,
    movie, foot, index, begins_s, sem,
):
    small = [
        pltpu.make_async_copy(source, target, sem.at[number])
        for number, (source, target) in enumerate(
            [(block_hbm, index.at[0]), (owner_hbm, index.at[1]), (slot_hbm, index.at[2]), (foot_hbm, foot)]
        )
    ]
    for copy in small:
        copy.start()

    load = pltpu.make_async_copy(movie_hbm, movie, sem.at[5])
    load.start()
    projected[...] = jnp.zeros_like(projected)
    foot_sorted[ENT:, :] = jnp.zeros((WINDOW, VOX), F32)
    block_sorted[ENT:, :] = jnp.full((WINDOW, 128), -1.0, F32)
    for copy in small[:3]:
        copy.wait()
    blk, own, slt = index[0], index[1], index[2]
    entry = iota((8, 128), 0) * 128 + iota((8, 128), 1)
    key = (blk * ENT + entry).astype(F32)
    ownf = own.astype(F32)
    key_col, own_col, blk_col = key.T, ownf.T, blk.astype(F32).T
    before = iota((128, 128), 0) < iota((128, 128), 1)
    lane8 = (iota((128, 128), 1) * 8).astype(F32)
    owner_rank, block_rank = [], []
    less = jnp.zeros((128, 128), F32)
    for row in range(8):
        key_row, own_row = key[row : row + 1, :], ownf[row : row + 1, :]
        count_o = jnp.zeros((128, 128), F32)
        count_k = jnp.zeros((128, 128), F32)
        for col in range(8):
            count_k += jnp.where(key_col[:, col : col + 1] < key_row, 1.0, 0.0)
            if col <= row:
                same = own_col[:, col : col + 1] == own_row
                if col == row:
                    same = same & before
                count_o += jnp.where(same, 1.0, 0.0)
        owner_rank.append(jnp.sum(count_o, axis=0, keepdims=True))
        block_rank.append(jnp.sum(count_k, axis=0, keepdims=True))
        less += jnp.where(blk_col[:, row : row + 1] < lane8, 1.0, 0.0)
    rank = jnp.concatenate(owner_rank, axis=0).astype(jnp.int32)
    order = jnp.concatenate(block_rank, axis=0).astype(jnp.int32)
    core, far, near = (own >> 2) & 1, own >> 3, own & 3
    message = jnp.where(core == 0, far, 4 + near)
    member = jnp.where(core == 0, near, far)
    tile, z = lax.axis_index("tile"), lax.axis_index("plane")
    turned = (member - jnp.where(core == 0, z, tile // 2) + 4) & 3
    section = jnp.where(turned == 0, 3, jnp.where(turned == 2, 0, jnp.where(turned == 1, 1, 2)))
    pos = message * ROWS + 8 + section * CAP + rank
    begins = jnp.broadcast_to(jnp.sum(less, axis=0, keepdims=True), (8, 128)).astype(jnp.int32)
    beyond = pltpu.roll(begins, 127, 1) - (begins >> 3) * 8 > WINDOW
    lane = iota((8, 128), 1)
    beyond = beyond & (lane < BLK // 8)
    for chunk, rows in zip((7, 15, 23), STAGES):
        beyond = beyond | ((lane == chunk) & ((begins >> 3) * 8 + WINDOW > rows))
    misfits = jnp.sum(jnp.where(beyond, 1.0, 0.0), axis=1, keepdims=True).astype(jnp.int32)
    begins_out[...] = jnp.where(lane == 127, misfits, begins)
    to_smem = pltpu.make_async_copy(begins_out, begins_s, sem.at[4])
    to_smem.start()

    small[3].wait()
    foot_values = foot[...].astype(F32)
    sq_high, sq_low = split(foot_values * foot_values)
    ones = jnp.ones((8, 128), BF16)
    energy = lax.dot_general(ones, sq_high, NT, preferred_element_type=F32) + lax.dot_general(
        ones, sq_low, NT, preferred_element_type=F32
    )
    place = section * 128 + rank
    meta = jnp.zeros((40, 512), F32)
    sorted_wide = jnp.zeros((ENT, 256), F32)
    sorted_pos = jnp.zeros((16, ENT), F32)
    for row in range(8):
        lanes = slice(row * 128, row * 128 + 128)
        chosen = message[row : row + 1, :] == iota((8, 128), 0)
        en_high, en_low = split(energy[:, lanes])
        slots = (slt[row : row + 1, :] + 1).astype(F32)
        sorted_at = order[row : row + 1, :] + 1
        values = jnp.concatenate(
            [
                jnp.where(chosen, slots, 0.0),
                jnp.where(chosen, en_high.astype(F32), 0.0),
                jnp.where(chosen, en_low.astype(F32), 0.0),
                jnp.where(chosen, (sorted_at >> 5).astype(F32), 0.0),
                jnp.where(chosen, (sorted_at & 31).astype(F32), 0.0),
            ],
            axis=0,
        ).astype(BF16)
        places = jnp.where(place[row : row + 1, :] == iota((512, 128), 0), 1.0, 0.0).astype(BF16)
        meta += lax.dot_general(values, places, NT, preferred_element_type=F32)
        permute = jnp.where(order[row : row + 1, :] == iota((ENT, 128), 0), 1.0, 0.0).astype(BF16)
        halves = [
            jnp.broadcast_to(part[row : row + 1, :], (8, 128)).astype(F32)
            for part in (pos >> 5, pos & 31)
        ]
        sorted_pos += lax.dot_general(
            jnp.concatenate(halves, axis=0).astype(BF16), permute, NT, preferred_element_type=F32
        )
        wide = jnp.concatenate(
            [
                foot[lanes, :],
                jnp.broadcast_to(blk_col[:, row : row + 1], (128, 128)).astype(BF16),
            ],
            axis=1,
        )
        sorted_wide += jnp.dot(permute, wide, preferred_element_type=F32)
    sorted_pos = (sorted_pos[:8, :] * 32.0 + sorted_pos[8:, :]).astype(jnp.int32)
    for row in range(8):
        places_out[row : row + 1, :] = sorted_pos[:1, row * 128 : (row + 1) * 128]
    foot_sorted[:ENT, :] = sorted_wide[:, :128]
    block_sorted[:ENT, :] = sorted_wide[:, 128:]
    place_of = (meta[24:32, :] * 32.0 + meta[32:40, :]).astype(jnp.int32)
    place_of = jnp.where(place_of == 0, ENT, place_of - 1)
    weights = meta[8:16, :] + meta[16:24, :]
    for i in range(4):
        lanes = slice(i * 128, i * 128 + 128)
        inverse[i] = place_of[:, lanes]
        labels[:, i, :] = meta[:8, lanes]
        labels[:, 4 + i, :] = weights[:, lanes]
    to_smem.wait()

    def product(chunk, begin, steps):
        right = movie[pl.ds(chunk * 8, 8)].reshape(8 * VOX, FR)

        def add(step):
            span = pl.ds(pl.multiple_of(begin + step * WINDOW, 8), WINDOW)
            values, which = foot_sorted[span, :], block_sorted[span, :]
            left = jnp.concatenate(
                [
                    jnp.where(which == jnp.asarray(chunk * 8 + n, F32), values, 0.0).astype(BF16)
                    for n in range(8)
                ],
                axis=1,
            )
            projected[span, :] += jnp.dot(left, right, preferred_element_type=F32)

        if isinstance(steps, int):
            add(0)
        else:
            pl.loop(0, steps)(add)

    load.wait()
    windows(begins_s, product)


def windows(begins, product, ahead=None, after=None):
    count = PART // 8
    misfits = begins[0, 127]

    @pl.when(misfits == 0)
    def _():
        for group in range(BLK // PART):
            if ahead is not None:
                ahead(group)
            for chunk in range(group * count, (group + 1) * count):
                product(chunk, (begins[0, chunk] // 8) * 8, 1)
            if after is not None:
                after(group)

    @pl.when(misfits != 0)
    def _():
        if ahead is not None:
            ahead(None)

        @pl.loop(0, BLK // PART)
        def _(group):
            @pl.loop(group * count, (group + 1) * count)
            def _(chunk):
                begin = (begins[0, chunk] // 8) * 8
                steps = (begins[0, chunk + 1] - begin + WINDOW - 1) // WINDOW
                product(chunk, begin, jnp.maximum(1, steps))

            if after is not None:
                after(group)


def gather(movie, footprint, entry_block, entry_owner, entry_slot):
    shape = jax.ShapeDtypeStruct
    in_place = pl.BlockSpec(memory_space=pltpu.HBM)
    return pl.pallas_call(
        gather_kernel,
        out_shape=(
            shape((ENT + WINDOW, FR), F32),
            shape((8, 8, 128), F32),
            shape((4, 8, 128), jnp.int32),
            shape((8, 128), jnp.int32),
            shape((8, 128), jnp.int32),
            shape((ENT + WINDOW, VOX), F32),
            shape((ENT + WINDOW, 128), F32),
        ),
        in_specs=[in_place] * 5,
        out_specs=(VMEM,) * 7,
        scratch_shapes=[
            pltpu.VMEM((BLK, VOX, FR), BF16),
            pltpu.VMEM((ENT, VOX), BF16),
            pltpu.VMEM((3, 8, 128), jnp.int32),
            pltpu.SMEM((8, 128), jnp.int32),
            pltpu.SemaphoreType.DMA((6,)),
        ],
        compiler_params=pltpu.CompilerParams(vmem_limit_bytes=48 << 20),
        name="project",
    )(
        *(
            pltpu.with_memory_space_constraint(array, pltpu.HBM)
            for array in (
                movie, footprint, entry_block.reshape(8, 128),
                entry_owner.reshape(8, 128), entry_slot.reshape(8, 128),
            )
        )
    )


def pick(rows, sub):
    chosen = jnp.where(sub // 2 == 0, rows[0:1, :], rows[1:2, :])
    lane = iota((SUB, 128), 1) - lax.rem(sub, 2) * SUB
    column = jnp.sum(jnp.where(lane == iota((SUB, 128), 0), chosen, 0.0), axis=1, keepdims=True)
    return jnp.broadcast_to(column, (SUB, 128))


def delayed(parts, steps):
    if steps >= 128:
        hop = steps // 128
        return [None] * hop + parts[: len(parts) - hop]
    lane = iota((SUB, 128), 1)
    rolled = [pltpu.roll(part, steps, 1) for part in parts]
    out = [jnp.where(lane < steps, 0.0, rolled[0])]
    for index in range(1, len(parts)):
        out.append(jnp.where(lane < steps, rolled[index - 1], rolled[index]))
    return out


def first_order(parts, powers):
    for level, power in enumerate(powers):
        moved = delayed(parts, 1 << level)
        parts = [
            part if late is None else part + power * late for part, late in zip(parts, moved)
        ]
    return parts


def sweeps(target, slow, fast):
    lag_one, lag_two = slow + fast, -slow * fast
    slow_powers, fast_powers = [slow], [fast]
    for _ in range(8):
        slow_powers.append(slow_powers[-1] * slow_powers[-1])
        fast_powers.append(fast_powers[-1] * fast_powers[-1])
    slow_share = slow / (slow - fast)
    fast_share = fast / (slow - fast)
    estimate = target
    for sweep in range(SWEEPS):
        one, two = delayed(estimate, 1), delayed(estimate, 2)
        spikes = [
            jnp.maximum(now - lag_one * a - lag_two * b, 0.0)
            for now, a, b in zip(estimate, one, two)
        ]
        slow_part = first_order(spikes, slow_powers)
        fast_part = first_order(spikes, fast_powers)
        calcium = [slow_share * a - fast_share * b for a, b in zip(slow_part, fast_part)]
        if sweep + 1 < SWEEPS:
            estimate = [0.5 * (a + b) for a, b in zip(target, calcium)]
    return calcium


def exchange_kernel(
    projected, labels, inverse_v, traces, slow, fast, back, calcium,
    inverse, send, got, hot, part, parts, piece, whole, reply,
    s1, r1, s2, r2, s3, r3, s4, r4, local,
):
    tile, y, z = lax.axis_index("tile"), lax.axis_index("tm"), lax.axis_index("plane")
    x, c = tile // 2, lax.rem(tile, 2)
    d = 1 - c
    p = x * d + z * c
    q = z * d + x * c

    def turn(value, by):
        return lax.rem(value + by, 4)

    def mine(pos, core):
        return (d * (2 * pos + core) + c * (2 * x + core), y, d * z + c * pos)

    def other(pos):
        return (c * 2 * pos + d * (2 * x + 1), y, c * z + d * pos)

    def column(pos, frame):
        return (d * 2 * x + c * (2 * pos + 1), frame, d * pos + c * z)

    to_smem = pltpu.make_async_copy(inverse_v, inverse, local.at[0])
    to_smem.start()
    reach = TURNS[:3]
    barrier = pltpu.get_barrier_semaphore()
    met = [mine(turn(p, by), c) for by in reach]
    met += [mine(turn(p, by), d) for by in TURNS]
    met += [other(turn(q, by)) for by in reach]
    met += [column(turn(q, dq), turn(y, dy)) for dq in TURNS for dy in TURNS if dq or dy]
    for device in met:
        pl.semaphore_signal(barrier, inc=1, device_id=device, device_id_type=MESH)
    for index in range(8):
        send[index * ROWS : index * ROWS + 8, :] = labels[index]

    def place(section):
        @pl.loop(0, 8)
        def _(index):
            first = pl.multiple_of(index * ROWS + 8 + CAP * section, 8)
            for block in range(0, CAP, 8):
                rows = [
                    projected[pl.ds(inverse[section, index, block + row], 1), :] for row in range(8)
                ]
                send[pl.ds(first + block, 8), :] = jnp.concatenate(rows, axis=0)

    to_smem.wait()
    place(0)
    pl.semaphore_wait(barrier, len(met))

    def remote(source, target, sends, arrives, device):
        return pltpu.make_async_remote_copy(
            src_ref=source, dst_ref=target, send_sem=sends, recv_sem=arrives,
            device_id=device, device_id_type=MESH,
        )

    def rows_of(section):
        return (0, 8 + CAP) if section == 0 else (8 + CAP * section, CAP)

    def message(index, section):
        first, count = rows_of(section)
        return send.at[pl.ds(pl.multiple_of(index * ROWS + first, 8), count), :]

    def landing(index, section):
        first, count = rows_of(section)
        return got.at[index, pl.ds(first, count), :]

    started = []

    def start(copy):
        copy.start()
        started.append(copy)

    def send_section(section):
        for by in TURNS:
            if by:
                index = c * 4 + turn(p, by)
                start(
                    remote(
                        message(index, section), landing(p * 2 + c, section),
                        s1.at[index * 4 + section], r1.at[(p * 2 + c) * 4 + section],
                        mine(turn(p, by), c),
                    )
                )
            index = d * 4 + turn(q, by)
            start(
                remote(
                    message(index, section), landing(q * 2 + c, section),
                    s1.at[index * 4 + section], r1.at[(q * 2 + c) * 4 + section],
                    other(turn(q, by)),
                )
            )

    for section in range(4):
        if section:
            place(section)
        if section >= 2:
            for copy in started[(section - 2) * 7 : (section - 1) * 7]:
                copy.wait_send()
        send_section(section)

    slots_iota = (iota((OWN, 128), 0) + 1).astype(F32)
    ones = jnp.ones((8, 128), BF16)
    blank = jnp.zeros((128 - CAP, FR), BF16)
    top = iota((8, 128), 0) == 0
    sources = [(0, 0), (0, 1), (1, 0), (1, 1), (3, 0), (3, 1), (2, 0), (2, 1)]
    for section in range(4):
        weight = jnp.zeros((OWN, 128), F32)
        lefts, rights = [], []
        first = 8 + CAP * section
        for by, flip in sources[1:]:
            source = turn(p, by) * 2 + (d if flip else c)
            remote(
                message(0, section), landing(source, section), s1.at[0],
                r1.at[source * 4 + section], mine(turn(p, by), c),
            ).wait_recv()
        for place_in, (by, flip) in enumerate(sources):
            if by or flip:
                source = turn(p, by) * 2 + (d if flip else c)
                slots = got[source, section : section + 1, :]
                energies = got[source, 4 + section : 5 + section, :]
                values = got[source, first : first + CAP, :]
            else:
                base = (c * 4 + p) * ROWS
                slots = labels[c * 4 + p, section : section + 1, :]
                energies = labels[c * 4 + p, 4 + section : 5 + section, :]
                values = send[pl.ds(pl.multiple_of(base + first, 8), CAP), :]
            match = slots_iota == slots
            chosen = jnp.where(match, 1.0, 0.0)
            hot[section, place_in * CAP : (place_in + 1) * CAP, :] = chosen.T[:CAP, :].astype(BF16)
            weight = weight + jnp.where(match, energies, 0.0)
            high, low = split(values)
            chosen = chosen.astype(BF16)
            lefts += [chosen, chosen]
            rights += [high, blank, low, blank]
        total = jnp.dot(
            jnp.concatenate(lefts, axis=1),
            jnp.concatenate(rights, axis=0),
            preferred_element_type=F32,
        )
        if section == 3:
            total = total + traces[...]
        high, low = split(weight)
        energy = lax.dot_general(ones, high, NT, preferred_element_type=F32) + lax.dot_general(
            ones, low, NT, preferred_element_type=F32
        )
        energy = jnp.where(top, energy[:, :128], energy[:, 128:])
        for sub in range(4):
            part[section, sub, :SUB, :] = total[sub * SUB : (sub + 1) * SUB, :]
            part[section, sub, SUB:, :] = energy
        tq = turn(q, TURNS[section])
        for dy in TURNS:
            ty = turn(y, dy)
            if section == 3 and dy == 0:
                own = pltpu.make_async_copy(part.at[section, y], parts.at[q, y], local.at[1])
                own.start()
            else:
                count = SUB if dy else PIECE
                start(
                    remote(
                        part.at[section, ty, pl.ds(0, count)], parts.at[q, y, pl.ds(0, count)],
                        s2.at[section * 4 + dy], r2.at[q * 4 + y], column(tq, ty),
                    )
                )
    own.wait()
    for dq in TURNS:
        for dy in TURNS:
            if dq or dy:
                fq, fy = turn(q, dq), turn(y, dy)
                count = SUB if dy else PIECE
                remote(
                    part.at[0, 0, pl.ds(0, count)], parts.at[fq, fy, pl.ds(0, count)], s2.at[0],
                    r2.at[fq * 4 + fy], column(fq, fy),
                ).wait_recv()
    energy = parts[0, y, SUB : SUB + 2, :]
    for other_q in range(1, 4):
        energy = energy + parts[other_q, y, SUB : SUB + 2, :]
    scale = 1.0 / (pick(energy, y) + 1.0)
    target = []
    for frame in range(4):
        total = parts[0, frame, :SUB, :]
        for other_q in range(1, 4):
            total = total + parts[other_q, frame, :SUB, :]
        target.append(total * scale)
    traced = sweeps(target, pick(slow[...], y), pick(fast[...], y))
    for frame in range(4):
        piece[frame] = traced[frame]

    for section in (3, 1, 2, 0):
        tq = turn(q, TURNS[section])
        for dy in TURNS:
            ty = turn(y, dy)
            if section == 3 and dy == 0:
                own = pltpu.make_async_copy(piece.at[y], whole.at[q, y], local.at[2])
                own.start()
            else:
                start(
                    remote(
                        piece.at[ty], whole.at[q, y], s3.at[section * 4 + dy], r3.at[q * 4 + y],
                        column(tq, ty),
                    )
                )
    own.wait()

    def answer(index, section):
        return back.at[pl.ds(pl.multiple_of(index * ROWS + 8 + CAP * section, 8), CAP), :]

    for section in (3, 1, 2, 0):
        fq = turn(q, TURNS[section])
        for dy in TURNS:
            if section != 3 or dy:
                fy = turn(y, dy)
                remote(
                    piece.at[0], whole.at[fq, fy], s3.at[0], r3.at[fq * 4 + fy], column(fq, fy)
                ).wait_recv()
        if section == 3:
            for sub in range(4):
                calcium[sub * SUB : (sub + 1) * SUB, :] = whole[q, sub]
        rows = whole[fq].reshape(OWN, FR).astype(BF16)
        reply[section] = jnp.dot(hot[section], rows, preferred_element_type=F32)
        for order in range(7, -1, -1):
            by, flip = sources[order]
            core = d if flip else c
            if by or flip:
                start(
                    remote(
                        reply.at[section, pl.ds(order * CAP, CAP)], answer(c * 4 + p, section),
                        s4.at[order * 4 + section], r4.at[(c * 4 + p) * 4 + section],
                        mine(turn(p, by), core),
                    )
                )
            else:
                own = pltpu.make_async_copy(
                    reply.at[section, pl.ds(order * CAP, CAP)], answer(c * 4 + p, section),
                    local.at[3 + section],
                )
                own.start()
                started.append(own)
    for section in (3, 1, 2, 0):
        for by in TURNS[::-1]:
            for core, pos in ((d, turn(q, by)), (c, turn(p, by))):
                if by == 0 and core is c:
                    continue
                index = core * 4 + pos
                remote(
                    reply.at[0, pl.ds(0, CAP)], answer(index, section), s4.at[0], r4.at[index * 4 + section],
                    other(q),
                ).wait_recv()
    for copy in started[14:]:
        if copy.is_remote:
            copy.wait_send()
        else:
            copy.wait()


def exchange(projected, labels, inverse, traces, slow_root, fast_root):
    dma = pltpu.SemaphoreType.DMA
    return pl.pallas_call(
        exchange_kernel,
        out_shape=(
            jax.ShapeDtypeStruct((8 * ROWS, FR), F32),
            jax.ShapeDtypeStruct((OWN, FR), F32),
        ),
        in_specs=[VMEM] * 6,
        out_specs=(VMEM, VMEM),
        scratch_shapes=[
            pltpu.SMEM((4, 8, 128), jnp.int32),
            pltpu.VMEM((8 * ROWS, FR), F32),
            pltpu.VMEM((8, ROWS, FR), F32),
            pltpu.VMEM((4, 8 * CAP, OWN), BF16),
            pltpu.VMEM((4, 4, PIECE, FR), F32),
            pltpu.VMEM((4, 4, PIECE, FR), F32),
            pltpu.VMEM((4, SUB, FR), F32),
            pltpu.VMEM((4, 4, SUB, FR), F32),
            pltpu.VMEM((4, 8 * CAP, FR), F32),
            dma((32,)), dma((32,)), dma((16,)), dma((16,)),
            dma((16,)), dma((16,)), dma((32,)), dma((32,)), dma((7,)),
        ],
        compiler_params=pltpu.CompilerParams(
            collective_id=1, has_side_effects=True, vmem_limit_bytes=48 << 20
        ),
        name="exchange",
    )(projected, labels, inverse, traces, slow_root.reshape(2, 128), fast_root.reshape(2, 128))


def rebuild_kernel(
    begins_v, places_v, back, foot, block, calcium, out_hbm, calcium_out,
    begins, places, rows, out, total, sem,
):
    to_smem = [
        pltpu.make_async_copy(source, target, sem.at[BLK // PART + number])
        for number, (source, target) in enumerate([(begins_v, begins), (places_v, places)])
    ]
    for copy in to_smem:
        copy.start()
    calcium_out[...] = calcium[...]
    rows[ENT:, :] = jnp.zeros((WINDOW, FR), F32)
    for copy in to_smem:
        copy.wait()

    def stage(group):
        if group is None:

            @pl.loop(0, ENT // 128)
            def _(line):
                for lane in range(128):
                    rows[pl.ds(line * 128 + lane, 1), :] = back[pl.ds(places[line, lane], 1), :]

        elif group % 2 == 0:
            number = group // 2
            for row in range(STAGES[number - 1] if number else 0, STAGES[number]):
                rows[row : row + 1, :] = back[pl.ds(places[row // 128, row % 128], 1), :]

    def term(chunk, first):
        span = pl.ds(pl.multiple_of(first, 8), WINDOW)
        values, which = rows[span, :], block[span, :]
        masked = jnp.concatenate(
            [
                jnp.where(which == jnp.asarray(chunk * 8 + n, F32), values, 0.0).astype(BF16)
                for n in range(8)
            ],
            axis=1,
        )
        left = foot[span, :].astype(BF16)
        return lax.dot_general(left, masked, TN, preferred_element_type=F32)

    def out_part(number):
        span = pl.ds(number * PART, PART)
        return pltpu.make_async_copy(out.at[span], out_hbm.at[span], sem.at[number])

    def product(chunk, begin, steps):
        result = term(chunk, begin)
        if not isinstance(steps, int):
            total[...] = result

            @pl.loop(1, steps)
            def _(step):
                total[...] += term(chunk, begin + step * WINDOW)

            result = total[...]
        for n in range(8):
            out[chunk * 8 + n] = result[:, n * FR : (n + 1) * FR].astype(BF16)

    windows(begins, product, stage, lambda group: out_part(group).start())

    @pl.loop(0, BLK // PART)
    def _(group):
        out_part(group).wait()


def rebuild(begins, places, back, foot, block, calcium):
    return pl.pallas_call(
        rebuild_kernel,
        out_shape=(
            jax.ShapeDtypeStruct((BLK, VOX, FR), BF16),
            jax.ShapeDtypeStruct((OWN, FR), F32),
        ),
        in_specs=[VMEM] * 6,
        out_specs=(pl.BlockSpec(memory_space=pl.ANY), VMEM),
        scratch_shapes=[
            pltpu.SMEM((8, 128), jnp.int32),
            pltpu.SMEM((8, 128), jnp.int32),
            pltpu.VMEM((ENT + WINDOW, FR), F32),
            pltpu.VMEM((BLK, VOX, FR), BF16),
            pltpu.VMEM((VOX, 8 * FR), F32),
            pltpu.SemaphoreType.DMA((BLK // PART + 2,)),
        ],
        compiler_params=pltpu.CompilerParams(vmem_limit_bytes=48 << 20),
        name="rebuild",
    )(begins, places, back, foot, block, calcium)


def shards(movie, footprint, entry_block, entry_owner, entry_slot, traces, slow_root, fast_root):
    projected, labels, inverse, begins, places, foot, block = gather(
        movie, footprint, entry_block, entry_owner, entry_slot
    )
    back, calcium = exchange(projected, labels, inverse, traces, slow_root, fast_root)
    return rebuild(begins, places, back, foot, block, calcium)


def solution(mesh):
    owners = ("tile", "plane")
    placed = (
        P(owners, None, "tm"),
        P(owners, None),
        P(owners),
        P(owners, None),
        P(owners),
        P(owners, "tm"),
        P(owners),
        P(owners),
    )
    return jax.shard_map(
        shards,
        mesh=mesh,
        in_specs=placed,
        out_specs=(P(owners, None, "tm"), P(owners, "tm")),
        check_vma=False,
    )
```

```python
import jax
import jax.numpy as jnp
from jax import lax
from jax.experimental import pallas as pl
from jax.experimental.pallas import tpu as pltpu
from jax.sharding import PartitionSpec as P

SWEEPS = 4
TURNS = (2, 1, 3, 0)
CAP = 96
OWN = 256
ENT = 1024
VOX = 128
FR = 128
BLK = 256
MSG = 4 * CAP
ROWS = MSG + 8
SUB = OWN // 4
PIECE = SUB + 8
WINDOW = 64
PART = 32
STAGES = (352, 640, 896, 1024)
MESH = pl.DeviceIdType.MESH
F32 = jnp.float32
BF16 = jnp.bfloat16
VMEM = pl.BlockSpec(memory_space=pltpu.VMEM)
NT = (((1,), (1,)), ((), ()))
TN = (((0,), (0,)), ((), ()))


def iota(shape, axis):
    return lax.broadcasted_iota(jnp.int32, shape, axis)


def split(value):
    high = value.astype(BF16)
    return high, (value - high.astype(F32)).astype(BF16)


def gather_kernel(
    movie_hbm, foot_hbm, block_hbm, owner_hbm, slot_hbm,
    projected, codes, energies, begins_out, foot_sorted, block_sorted,
    movie, foot, index, begins_s, sem,
):
    small = [
        pltpu.make_async_copy(source, target, sem.at[number])
        for number, (source, target) in enumerate(
            [(block_hbm, index.at[0]), (owner_hbm, index.at[1]), (slot_hbm, index.at[2]), (foot_hbm, foot)]
        )
    ]
    for copy in small:
        copy.start()

    load = pltpu.make_async_copy(movie_hbm, movie, sem.at[5])
    load.start()
    projected[...] = jnp.zeros_like(projected)
    foot_sorted[ENT:, :] = jnp.zeros((WINDOW, VOX), F32)
    block_sorted[ENT:, :] = jnp.full((WINDOW, 128), -1.0, F32)
    for copy in small[:3]:
        copy.wait()
    blk, own, slt = index[0], index[1], index[2]
    entry = iota((8, 128), 0) * 128 + iota((8, 128), 1)
    key = (blk * ENT + entry).astype(F32)
    ownf = own.astype(F32)
    key_col, own_col, blk_col = key.T, ownf.T, blk.astype(F32).T
    before = iota((128, 128), 0) < iota((128, 128), 1)
    lane8 = (iota((128, 128), 1) * 8).astype(F32)
    owner_rank, block_rank = [], []
    less = jnp.zeros((128, 128), F32)
    for row in range(8):
        key_row, own_row = key[row : row + 1, :], ownf[row : row + 1, :]
        count_o = jnp.zeros((128, 128), F32)
        count_k = jnp.zeros((128, 128), F32)
        for col in range(8):
            count_k += jnp.where(key_col[:, col : col + 1] < key_row, 1.0, 0.0)
            if col <= row:
                same = own_col[:, col : col + 1] == own_row
                if col == row:
                    same = same & before
                count_o += jnp.where(same, 1.0, 0.0)
        owner_rank.append(jnp.sum(count_o, axis=0, keepdims=True))
        block_rank.append(jnp.sum(count_k, axis=0, keepdims=True))
        less += jnp.where(blk_col[:, row : row + 1] < lane8, 1.0, 0.0)
    rank = jnp.concatenate(owner_rank, axis=0).astype(jnp.int32)
    order = jnp.concatenate(block_rank, axis=0).astype(jnp.int32)
    core, far, near = (own >> 2) & 1, own >> 3, own & 3
    message = jnp.where(core == 0, far, 4 + near)
    member = jnp.where(core == 0, near, far)
    tile, z = lax.axis_index("tile"), lax.axis_index("plane")
    turned = (member - jnp.where(core == 0, z, tile // 2) + 4) & 3
    section = jnp.where(turned == 0, 3, jnp.where(turned == 2, 0, jnp.where(turned == 1, 1, 2)))
    pos = message * ROWS + 8 + section * CAP + rank
    begins = jnp.broadcast_to(jnp.sum(less, axis=0, keepdims=True), (8, 128)).astype(jnp.int32)
    beyond = pltpu.roll(begins, 127, 1) - (begins >> 3) * 8 > WINDOW
    lane = iota((8, 128), 1)
    beyond = beyond & (lane < BLK // 8)
    for chunk, rows in zip((7, 15, 23), STAGES):
        beyond = beyond | ((lane == chunk) & ((begins >> 3) * 8 + WINDOW > rows))
    misfits = jnp.sum(jnp.where(beyond, 1.0, 0.0), axis=1, keepdims=True).astype(jnp.int32)
    begins_out[...] = jnp.where(lane == 127, misfits, begins)
    to_smem = pltpu.make_async_copy(begins_out, begins_s, sem.at[4])
    to_smem.start()

    small[3].wait()
    foot_values = foot[...].astype(F32)
    sq_high, sq_low = split(foot_values * foot_values)
    ones = jnp.ones((8, 128), BF16)
    energy = lax.dot_general(ones, sq_high, NT, preferred_element_type=F32) + lax.dot_general(
        ones, sq_low, NT, preferred_element_type=F32
    )
    for number, code in enumerate((message, section * 128 + rank, order, pos, slt)):
        codes[number] = code
    energies[...] = energy
    sorted_wide = jnp.zeros((ENT, 256), F32)
    for row in range(8):
        lanes = slice(row * 128, row * 128 + 128)
        permute = jnp.where(order[row : row + 1, :] == iota((ENT, 128), 0), 1.0, 0.0).astype(BF16)
        wide = jnp.concatenate(
            [
                foot[lanes, :],
                jnp.broadcast_to(blk_col[:, row : row + 1], (128, 128)).astype(BF16),
            ],
            axis=1,
        )
        sorted_wide += jnp.dot(permute, wide, preferred_element_type=F32)
    foot_sorted[:ENT, :] = sorted_wide[:, :128]
    block_sorted[:ENT, :] = sorted_wide[:, 128:]
    to_smem.wait()

    def product(chunk, begin, steps):
        right = movie[pl.ds(chunk * 8, 8)].reshape(8 * VOX, FR)

        def add(step):
            span = pl.ds(pl.multiple_of(begin + step * WINDOW, 8), WINDOW)
            values, which = foot_sorted[span, :], block_sorted[span, :]
            left = jnp.concatenate(
                [
                    jnp.where(which == jnp.asarray(chunk * 8 + n, F32), values, 0.0).astype(BF16)
                    for n in range(8)
                ],
                axis=1,
            )
            projected[span, :] += jnp.dot(left, right, preferred_element_type=F32)

        if isinstance(steps, int):
            add(0)
        else:
            pl.loop(0, steps)(add)

    load.wait()
    windows(begins_s, product)


def windows(begins, product, ahead=None, after=None):
    count = PART // 8
    misfits = begins[0, 127]

    @pl.when(misfits == 0)
    def _():
        for group in range(BLK // PART):
            if ahead is not None:
                ahead(group)
            for chunk in range(group * count, (group + 1) * count):
                product(chunk, (begins[0, chunk] // 8) * 8, 1)
            if after is not None:
                after(group)

    @pl.when(misfits != 0)
    def _():
        if ahead is not None:
            ahead(None)

        @pl.loop(0, BLK // PART)
        def _(group):
            @pl.loop(group * count, (group + 1) * count)
            def _(chunk):
                begin = (begins[0, chunk] // 8) * 8
                steps = (begins[0, chunk + 1] - begin + WINDOW - 1) // WINDOW
                product(chunk, begin, jnp.maximum(1, steps))

            if after is not None:
                after(group)


def gather(movie, footprint, entry_block, entry_owner, entry_slot):
    shape = jax.ShapeDtypeStruct
    in_place = pl.BlockSpec(memory_space=pltpu.HBM)
    return pl.pallas_call(
        gather_kernel,
        out_shape=(
            shape((ENT + WINDOW, FR), F32),
            shape((5, 8, 128), jnp.int32),
            shape((8, ENT), F32),
            shape((8, 128), jnp.int32),
            shape((ENT + WINDOW, VOX), F32),
            shape((ENT + WINDOW, 128), F32),
        ),
        in_specs=[in_place] * 5,
        out_specs=(VMEM,) * 6,
        scratch_shapes=[
            pltpu.VMEM((BLK, VOX, FR), BF16),
            pltpu.VMEM((ENT, VOX), BF16),
            pltpu.VMEM((3, 8, 128), jnp.int32),
            pltpu.SMEM((8, 128), jnp.int32),
            pltpu.SemaphoreType.DMA((6,)),
        ],
        compiler_params=pltpu.CompilerParams(vmem_limit_bytes=48 << 20),
        name="project",
    )(
        *(
            pltpu.with_memory_space_constraint(array, pltpu.HBM)
            for array in (
                movie, footprint, entry_block.reshape(8, 128),
                entry_owner.reshape(8, 128), entry_slot.reshape(8, 128),
            )
        )
    )


def pick(rows, sub):
    chosen = jnp.where(sub // 2 == 0, rows[0:1, :], rows[1:2, :])
    lane = iota((SUB, 128), 1) - lax.rem(sub, 2) * SUB
    column = jnp.sum(jnp.where(lane == iota((SUB, 128), 0), chosen, 0.0), axis=1, keepdims=True)
    return jnp.broadcast_to(column, (SUB, 128))


def delayed(parts, steps):
    if steps >= 128:
        hop = steps // 128
        return [None] * hop + parts[: len(parts) - hop]
    lane = iota((SUB, 128), 1)
    rolled = [pltpu.roll(part, steps, 1) for part in parts]
    out = [jnp.where(lane < steps, 0.0, rolled[0])]
    for index in range(1, len(parts)):
        out.append(jnp.where(lane < steps, rolled[index - 1], rolled[index]))
    return out


def first_order(parts, powers):
    for level, power in enumerate(powers):
        moved = delayed(parts, 1 << level)
        parts = [
            part if late is None else part + power * late for part, late in zip(parts, moved)
        ]
    return parts


def sweeps(target, slow, fast):
    lag_one, lag_two = slow + fast, -slow * fast
    slow_powers, fast_powers = [slow], [fast]
    for _ in range(8):
        slow_powers.append(slow_powers[-1] * slow_powers[-1])
        fast_powers.append(fast_powers[-1] * fast_powers[-1])
    slow_share = slow / (slow - fast)
    fast_share = fast / (slow - fast)
    estimate = target
    for sweep in range(SWEEPS):
        one, two = delayed(estimate, 1), delayed(estimate, 2)
        spikes = [
            jnp.maximum(now - lag_one * a - lag_two * b, 0.0)
            for now, a, b in zip(estimate, one, two)
        ]
        slow_part = first_order(spikes, slow_powers)
        fast_part = first_order(spikes, fast_powers)
        calcium = [slow_share * a - fast_share * b for a, b in zip(slow_part, fast_part)]
        if sweep + 1 < SWEEPS:
            estimate = [0.5 * (a + b) for a, b in zip(target, calcium)]
    return calcium


def exchange_kernel(
    projected, codes, energies, traces, slow, fast, back, calcium, places_out,
    labels, inverse_v, inverse, send, got, hot, part, parts, piece, whole, reply,
    s1, r1, s2, r2, s3, r3, s4, r4, local,
):
    tile, y, z = lax.axis_index("tile"), lax.axis_index("tm"), lax.axis_index("plane")
    x, c = tile // 2, lax.rem(tile, 2)
    d = 1 - c
    p = x * d + z * c
    q = z * d + x * c

    def turn(value, by):
        return lax.rem(value + by, 4)

    def mine(pos, core):
        return (d * (2 * pos + core) + c * (2 * x + core), y, d * z + c * pos)

    def other(pos):
        return (c * 2 * pos + d * (2 * x + 1), y, c * z + d * pos)

    def column(pos, frame):
        return (d * 2 * x + c * (2 * pos + 1), frame, d * pos + c * z)

    reach = TURNS[:3]
    barrier = pltpu.get_barrier_semaphore()
    met = [mine(turn(p, by), c) for by in reach]
    met += [mine(turn(p, by), d) for by in TURNS]
    met += [other(turn(q, by)) for by in reach]
    met += [column(turn(q, dq), turn(y, dy)) for dq in TURNS for dy in TURNS if dq or dy]
    for device in met:
        pl.semaphore_signal(barrier, inc=1, device_id=device, device_id_type=MESH)
    meta = jnp.zeros((40, 512), F32)
    for row in range(8):
        message_of, place_in, sorted_at, _, slots = [
            codes[number, row : row + 1, :] for number in range(5)
        ]
        chosen = message_of == iota((8, 128), 0)
        en_high, en_low = split(energies[:, row * 128 : row * 128 + 128])
        sorted_at = sorted_at + 1
        values = [
            jnp.where(chosen, value.astype(F32), 0.0)
            for value in (slots + 1, en_high, en_low, sorted_at >> 5, sorted_at & 31)
        ]
        spots = jnp.where(place_in == iota((512, 128), 0), 1.0, 0.0).astype(BF16)
        meta += lax.dot_general(
            jnp.concatenate(values, axis=0).astype(BF16), spots, NT, preferred_element_type=F32
        )
    place_of = (meta[24:32, :] * 32.0 + meta[32:40, :]).astype(jnp.int32)
    place_of = jnp.where(place_of == 0, ENT, jnp.clip(place_of - 1, 0, ENT))
    weights = meta[8:16, :] + meta[16:24, :]
    for i in range(4):
        lanes = slice(i * 128, i * 128 + 128)
        inverse_v[i] = place_of[:, lanes]
        labels[:, i, :] = meta[:8, lanes]
        labels[:, 4 + i, :] = weights[:, lanes]
    to_smem = pltpu.make_async_copy(inverse_v, inverse, local.at[0])
    to_smem.start()
    for index in range(8):
        send[index * ROWS : index * ROWS + 8, :] = labels[index]

    def place(section):
        @pl.loop(0, 8)
        def _(index):
            first = pl.multiple_of(index * ROWS + 8 + CAP * section, 8)
            for block in range(0, CAP, 8):
                rows = [
                    projected[pl.ds(inverse[section, index, block + row], 1), :] for row in range(8)
                ]
                send[pl.ds(first + block, 8), :] = jnp.concatenate(rows, axis=0)

    to_smem.wait()
    place(0)
    pl.semaphore_wait(barrier, len(met))

    def remote(source, target, sends, arrives, device):
        return pltpu.make_async_remote_copy(
            src_ref=source, dst_ref=target, send_sem=sends, recv_sem=arrives,
            device_id=device, device_id_type=MESH,
        )

    def rows_of(section):
        return (0, 8 + CAP) if section == 0 else (8 + CAP * section, CAP)

    def message(index, section):
        first, count = rows_of(section)
        return send.at[pl.ds(pl.multiple_of(index * ROWS + first, 8), count), :]

    def landing(index, section):
        first, count = rows_of(section)
        return got.at[index, pl.ds(first, count), :]

    started = []

    def start(copy):
        copy.start()
        started.append(copy)

    def send_section(section):
        for by in TURNS:
            if by:
                index = c * 4 + turn(p, by)
                start(
                    remote(
                        message(index, section), landing(p * 2 + c, section),
                        s1.at[index * 4 + section], r1.at[(p * 2 + c) * 4 + section],
                        mine(turn(p, by), c),
                    )
                )
            index = d * 4 + turn(q, by)
            start(
                remote(
                    message(index, section), landing(q * 2 + c, section),
                    s1.at[index * 4 + section], r1.at[(q * 2 + c) * 4 + section],
                    other(turn(q, by)),
                )
            )

    for section in range(4):
        if section:
            place(section)
        if section >= 2:
            for copy in started[(section - 2) * 7 : (section - 1) * 7]:
                copy.wait_send()
        send_section(section)

    slots_iota = (iota((OWN, 128), 0) + 1).astype(F32)
    ones = jnp.ones((8, 128), BF16)
    blank = jnp.zeros((128 - CAP, FR), BF16)
    top = iota((8, 128), 0) == 0
    sources = [(0, 0), (0, 1), (1, 0), (1, 1), (3, 0), (3, 1), (2, 0), (2, 1)]
    for section in range(4):
        weight = jnp.zeros((OWN, 128), F32)
        lefts, rights = [], []
        first = 8 + CAP * section
        for by, flip in sources[1:]:
            source = turn(p, by) * 2 + (d if flip else c)
            remote(
                message(0, section), landing(source, section), s1.at[0],
                r1.at[source * 4 + section], mine(turn(p, by), c),
            ).wait_recv()
        for place_in, (by, flip) in enumerate(sources):
            if by or flip:
                source = turn(p, by) * 2 + (d if flip else c)
                slots = got[source, section : section + 1, :]
                energies = got[source, 4 + section : 5 + section, :]
                values = got[source, first : first + CAP, :]
            else:
                base = (c * 4 + p) * ROWS
                slots = labels[c * 4 + p, section : section + 1, :]
                energies = labels[c * 4 + p, 4 + section : 5 + section, :]
                values = send[pl.ds(pl.multiple_of(base + first, 8), CAP), :]
            match = slots_iota == slots
            chosen = jnp.where(match, 1.0, 0.0)
            hot[section, place_in * CAP : (place_in + 1) * CAP, :] = chosen.T[:CAP, :].astype(BF16)
            weight = weight + jnp.where(match, energies, 0.0)
            high, low = split(values)
            chosen = chosen.astype(BF16)
            lefts += [chosen, chosen]
            rights += [high, blank, low, blank]
        total = jnp.dot(
            jnp.concatenate(lefts, axis=1),
            jnp.concatenate(rights, axis=0),
            preferred_element_type=F32,
        )
        if section == 3:
            total = total + traces[...]
        high, low = split(weight)
        energy = lax.dot_general(ones, high, NT, preferred_element_type=F32) + lax.dot_general(
            ones, low, NT, preferred_element_type=F32
        )
        energy = jnp.where(top, energy[:, :128], energy[:, 128:])
        for sub in range(4):
            part[section, sub, :SUB, :] = total[sub * SUB : (sub + 1) * SUB, :]
            part[section, sub, SUB:, :] = energy
        tq = turn(q, TURNS[section])
        for dy in TURNS:
            ty = turn(y, dy)
            if section == 3 and dy == 0:
                own = pltpu.make_async_copy(part.at[section, y], parts.at[q, y], local.at[1])
                own.start()
            else:
                count = SUB if dy else PIECE
                start(
                    remote(
                        part.at[section, ty, pl.ds(0, count)], parts.at[q, y, pl.ds(0, count)],
                        s2.at[section * 4 + dy], r2.at[q * 4 + y], column(tq, ty),
                    )
                )
    sorted_pos = jnp.zeros((16, ENT), F32)
    for row in range(8):
        sorted_at, pos = codes[2, row : row + 1, :], codes[3, row : row + 1, :]
        permute = jnp.where(sorted_at == iota((ENT, 128), 0), 1.0, 0.0).astype(BF16)
        halves = [
            jnp.broadcast_to(part_of, (8, 128)).astype(F32) for part_of in (pos >> 5, pos & 31)
        ]
        sorted_pos += lax.dot_general(
            jnp.concatenate(halves, axis=0).astype(BF16), permute, NT, preferred_element_type=F32
        )
    sorted_pos = (sorted_pos[:8, :] * 32.0 + sorted_pos[8:, :]).astype(jnp.int32)
    for row in range(8):
        places_out[row : row + 1, :] = sorted_pos[:1, row * 128 : (row + 1) * 128]
    own.wait()
    for dq in TURNS:
        for dy in TURNS:
            if dq or dy:
                fq, fy = turn(q, dq), turn(y, dy)
                count = SUB if dy else PIECE
                remote(
                    part.at[0, 0, pl.ds(0, count)], parts.at[fq, fy, pl.ds(0, count)], s2.at[0],
                    r2.at[fq * 4 + fy], column(fq, fy),
                ).wait_recv()
    energy = parts[0, y, SUB : SUB + 2, :]
    for other_q in range(1, 4):
        energy = energy + parts[other_q, y, SUB : SUB + 2, :]
    scale = 1.0 / (pick(energy, y) + 1.0)
    target = []
    for frame in range(4):
        total = parts[0, frame, :SUB, :]
        for other_q in range(1, 4):
            total = total + parts[other_q, frame, :SUB, :]
        target.append(total * scale)
    traced = sweeps(target, pick(slow[...], y), pick(fast[...], y))
    for frame in range(4):
        piece[frame] = traced[frame]

    for section in (3, 1, 2, 0):
        tq = turn(q, TURNS[section])
        for dy in TURNS:
            ty = turn(y, dy)
            if section == 3 and dy == 0:
                own = pltpu.make_async_copy(piece.at[y], whole.at[q, y], local.at[2])
                own.start()
            else:
                start(
                    remote(
                        piece.at[ty], whole.at[q, y], s3.at[section * 4 + dy], r3.at[q * 4 + y],
                        column(tq, ty),
                    )
                )
    own.wait()

    def answer(index, section):
        return back.at[pl.ds(pl.multiple_of(index * ROWS + 8 + CAP * section, 8), CAP), :]

    for section in (3, 1, 2, 0):
        fq = turn(q, TURNS[section])
        for dy in TURNS:
            if section != 3 or dy:
                fy = turn(y, dy)
                remote(
                    piece.at[0], whole.at[fq, fy], s3.at[0], r3.at[fq * 4 + fy], column(fq, fy)
                ).wait_recv()
        if section == 3:
            for sub in range(4):
                calcium[sub * SUB : (sub + 1) * SUB, :] = whole[q, sub]
        rows = whole[fq].reshape(OWN, FR).astype(BF16)
        reply[section] = jnp.dot(hot[section], rows, preferred_element_type=F32)
        for order in range(7, -1, -1):
            by, flip = sources[order]
            core = d if flip else c
            if by or flip:
                start(
                    remote(
                        reply.at[section, pl.ds(order * CAP, CAP)], answer(c * 4 + p, section),
                        s4.at[order * 4 + section], r4.at[(c * 4 + p) * 4 + section],
                        mine(turn(p, by), core),
                    )
                )
            else:
                own = pltpu.make_async_copy(
                    reply.at[section, pl.ds(order * CAP, CAP)], answer(c * 4 + p, section),
                    local.at[3 + section],
                )
                own.start()
                started.append(own)
    for section in (3, 1, 2, 0):
        for by in TURNS[::-1]:
            for core, pos in ((d, turn(q, by)), (c, turn(p, by))):
                if by == 0 and core is c:
                    continue
                index = core * 4 + pos
                remote(
                    reply.at[0, pl.ds(0, CAP)], answer(index, section), s4.at[0], r4.at[index * 4 + section],
                    other(q),
                ).wait_recv()
    for copy in started[14:]:
        if copy.is_remote:
            copy.wait_send()
        else:
            copy.wait()


def exchange(projected, codes, energies, traces, slow_root, fast_root):
    dma = pltpu.SemaphoreType.DMA
    return pl.pallas_call(
        exchange_kernel,
        out_shape=(
            jax.ShapeDtypeStruct((8 * ROWS, FR), F32),
            jax.ShapeDtypeStruct((OWN, FR), F32),
            jax.ShapeDtypeStruct((8, 128), jnp.int32),
        ),
        in_specs=[VMEM] * 6,
        out_specs=(VMEM, VMEM, VMEM),
        scratch_shapes=[
            pltpu.VMEM((8, 8, 128), F32),
            pltpu.VMEM((4, 8, 128), jnp.int32),
            pltpu.SMEM((4, 8, 128), jnp.int32),
            pltpu.VMEM((8 * ROWS, FR), F32),
            pltpu.VMEM((8, ROWS, FR), F32),
            pltpu.VMEM((4, 8 * CAP, OWN), BF16),
            pltpu.VMEM((4, 4, PIECE, FR), F32),
            pltpu.VMEM((4, 4, PIECE, FR), F32),
            pltpu.VMEM((4, SUB, FR), F32),
            pltpu.VMEM((4, 4, SUB, FR), F32),
            pltpu.VMEM((4, 8 * CAP, FR), F32),
            dma((32,)), dma((32,)), dma((16,)), dma((16,)),
            dma((16,)), dma((16,)), dma((32,)), dma((32,)), dma((7,)),
        ],
        compiler_params=pltpu.CompilerParams(
            collective_id=1, has_side_effects=True, vmem_limit_bytes=48 << 20
        ),
        name="exchange",
    )(projected, codes, energies, traces, slow_root.reshape(2, 128), fast_root.reshape(2, 128))


def rebuild_kernel(
    begins_v, places_v, back, foot, block, calcium, out_hbm, calcium_out,
    begins, places, rows, out, total, sem,
):
    to_smem = [
        pltpu.make_async_copy(source, target, sem.at[BLK // PART + number])
        for number, (source, target) in enumerate([(begins_v, begins), (places_v, places)])
    ]
    for copy in to_smem:
        copy.start()
    calcium_out[...] = calcium[...]
    rows[ENT:, :] = jnp.zeros((WINDOW, FR), F32)
    for copy in to_smem:
        copy.wait()

    def stage(group):
        if group is None:

            @pl.loop(0, ENT // 128)
            def _(line):
                for lane in range(128):
                    rows[pl.ds(line * 128 + lane, 1), :] = back[pl.ds(places[line, lane], 1), :]

        elif group % 2 == 0:
            number = group // 2
            for row in range(STAGES[number - 1] if number else 0, STAGES[number]):
                rows[row : row + 1, :] = back[pl.ds(places[row // 128, row % 128], 1), :]

    def term(chunk, first):
        span = pl.ds(pl.multiple_of(first, 8), WINDOW)
        values, which = rows[span, :], block[span, :]
        masked = jnp.concatenate(
            [
                jnp.where(which == jnp.asarray(chunk * 8 + n, F32), values, 0.0).astype(BF16)
                for n in range(8)
            ],
            axis=1,
        )
        left = foot[span, :].astype(BF16)
        return lax.dot_general(left, masked, TN, preferred_element_type=F32)

    def out_part(number):
        span = pl.ds(number * PART, PART)
        return pltpu.make_async_copy(out.at[span], out_hbm.at[span], sem.at[number])

    def product(chunk, begin, steps):
        result = term(chunk, begin)
        if not isinstance(steps, int):
            total[...] = result

            @pl.loop(1, steps)
            def _(step):
                total[...] += term(chunk, begin + step * WINDOW)

            result = total[...]
        for n in range(8):
            out[chunk * 8 + n] = result[:, n * FR : (n + 1) * FR].astype(BF16)

    windows(begins, product, stage, lambda group: out_part(group).start())

    @pl.loop(0, BLK // PART)
    def _(group):
        out_part(group).wait()


def rebuild(begins, places, back, foot, block, calcium):
    return pl.pallas_call(
        rebuild_kernel,
        out_shape=(
            jax.ShapeDtypeStruct((BLK, VOX, FR), BF16),
            jax.ShapeDtypeStruct((OWN, FR), F32),
        ),
        in_specs=[VMEM] * 6,
        out_specs=(pl.BlockSpec(memory_space=pl.ANY), VMEM),
        scratch_shapes=[
            pltpu.SMEM((8, 128), jnp.int32),
            pltpu.SMEM((8, 128), jnp.int32),
            pltpu.VMEM((ENT + WINDOW, FR), F32),
            pltpu.VMEM((BLK, VOX, FR), BF16),
            pltpu.VMEM((VOX, 8 * FR), F32),
            pltpu.SemaphoreType.DMA((BLK // PART + 2,)),
        ],
        compiler_params=pltpu.CompilerParams(vmem_limit_bytes=48 << 20),
        name="rebuild",
    )(begins, places, back, foot, block, calcium)


def shards(movie, footprint, entry_block, entry_owner, entry_slot, traces, slow_root, fast_root):
    projected, codes, energies, begins, foot, block = gather(
        movie, footprint, entry_block, entry_owner, entry_slot
    )
    back, calcium, places = exchange(projected, codes, energies, traces, slow_root, fast_root)
    return rebuild(begins, places, back, foot, block, calcium)


def solution(mesh):
    owners = ("tile", "plane")
    placed = (
        P(owners, None, "tm"),
        P(owners, None),
        P(owners),
        P(owners, None),
        P(owners),
        P(owners, "tm"),
        P(owners),
        P(owners),
    )
    return jax.shard_map(
        shards,
        mesh=mesh,
        in_specs=placed,
        out_specs=(P(owners, None, "tm"), P(owners, "tm")),
        check_vma=False,
    )
```

```python
import jax
import jax.numpy as jnp
from jax import lax
from jax.experimental import pallas as pl
from jax.experimental.pallas import tpu as pltpu
from jax.sharding import PartitionSpec as P

SWEEPS = 4
TURNS = (2, 1, 3, 0)
FAST_BLOCK = 32
CAP = 96
OWN = 256
ENT = 1024
VOX = 128
FR = 128
BLK = 256
MSG = 4 * CAP
ROWS = MSG + 8
SUB = OWN // 4
PIECE = SUB + 8
WINDOW = 64
PART = 32
STAGES = (352, 640, 896, 1024)
MESH = pl.DeviceIdType.MESH
F32 = jnp.float32
BF16 = jnp.bfloat16
VMEM = pl.BlockSpec(memory_space=pltpu.VMEM)
NT = (((1,), (1,)), ((), ()))
TN = (((0,), (0,)), ((), ()))


def iota(shape, axis):
    return lax.broadcasted_iota(jnp.int32, shape, axis)


def split(value):
    high = value.astype(BF16)
    return high, (value - high.astype(F32)).astype(BF16)


def gather_kernel(
    movie_hbm, foot_hbm, block_hbm, owner_hbm, slot_hbm,
    projected, codes, energies, begins_out, foot_sorted, block_sorted,
    movie, foot, index, begins_s, sem,
):
    small = [
        pltpu.make_async_copy(source, target, sem.at[number])
        for number, (source, target) in enumerate(
            [(block_hbm, index.at[0]), (owner_hbm, index.at[1]), (slot_hbm, index.at[2]), (foot_hbm, foot)]
        )
    ]
    for copy in small:
        copy.start()

    load = pltpu.make_async_copy(movie_hbm, movie, sem.at[5])
    load.start()
    projected[...] = jnp.zeros_like(projected)
    foot_sorted[ENT:, :] = jnp.zeros((WINDOW, VOX), F32)
    block_sorted[ENT:, :] = jnp.full((WINDOW, 128), -1.0, F32)
    for copy in small[:3]:
        copy.wait()
    blk, own, slt = index[0], index[1], index[2]
    entry = iota((8, 128), 0) * 128 + iota((8, 128), 1)
    key = (blk * ENT + entry).astype(F32)
    ownf = own.astype(F32)
    key_col, own_col, blk_col = key.T, ownf.T, blk.astype(F32).T
    before = iota((128, 128), 0) < iota((128, 128), 1)
    lane8 = (iota((128, 128), 1) * 8).astype(F32)
    owner_rank, block_rank = [], []
    less = jnp.zeros((128, 128), F32)
    for row in range(8):
        key_row, own_row = key[row : row + 1, :], ownf[row : row + 1, :]
        count_o = jnp.zeros((128, 128), F32)
        count_k = jnp.zeros((128, 128), F32)
        for col in range(8):
            count_k += jnp.where(key_col[:, col : col + 1] < key_row, 1.0, 0.0)
            if col <= row:
                same = own_col[:, col : col + 1] == own_row
                if col == row:
                    same = same & before
                count_o += jnp.where(same, 1.0, 0.0)
        owner_rank.append(jnp.sum(count_o, axis=0, keepdims=True))
        block_rank.append(jnp.sum(count_k, axis=0, keepdims=True))
        less += jnp.where(blk_col[:, row : row + 1] < lane8, 1.0, 0.0)
    rank = jnp.concatenate(owner_rank, axis=0).astype(jnp.int32)
    order = jnp.concatenate(block_rank, axis=0).astype(jnp.int32)
    core, far, near = (own >> 2) & 1, own >> 3, own & 3
    message = jnp.where(core == 0, far, 4 + near)
    member = jnp.where(core == 0, near, far)
    tile, z = lax.axis_index("tile"), lax.axis_index("plane")
    turned = (member - jnp.where(core == 0, z, tile // 2) + 4) & 3
    section = jnp.where(turned == 0, 3, jnp.where(turned == 2, 0, jnp.where(turned == 1, 1, 2)))
    pos = message * ROWS + 8 + section * CAP + rank
    begins = jnp.broadcast_to(jnp.sum(less, axis=0, keepdims=True), (8, 128)).astype(jnp.int32)
    beyond = pltpu.roll(begins, 127, 1) - (begins >> 3) * 8 > WINDOW
    lane = iota((8, 128), 1)
    beyond = beyond & (lane < BLK // 8)
    for chunk, rows in zip((7, 15, 23), STAGES):
        beyond = beyond | ((lane == chunk) & ((begins >> 3) * 8 + WINDOW > rows))
    misfits = jnp.sum(jnp.where(beyond, 1.0, 0.0), axis=1, keepdims=True).astype(jnp.int32)
    begins_out[...] = jnp.where(lane == 127, misfits, begins)
    to_smem = pltpu.make_async_copy(begins_out, begins_s, sem.at[4])
    to_smem.start()

    small[3].wait()
    foot_values = foot[...].astype(F32)
    sq_high, sq_low = split(foot_values * foot_values)
    ones = jnp.ones((8, 128), BF16)
    energy = lax.dot_general(ones, sq_high, NT, preferred_element_type=F32) + lax.dot_general(
        ones, sq_low, NT, preferred_element_type=F32
    )
    for number, code in enumerate((message, section * 128 + rank, order, pos, slt)):
        codes[number] = code
    energies[...] = energy
    sorted_wide = jnp.zeros((ENT, 256), F32)
    for row in range(8):
        lanes = slice(row * 128, row * 128 + 128)
        permute = jnp.where(order[row : row + 1, :] == iota((ENT, 128), 0), 1.0, 0.0).astype(BF16)
        wide = jnp.concatenate(
            [
                foot[lanes, :],
                jnp.broadcast_to(blk_col[:, row : row + 1], (128, 128)).astype(BF16),
            ],
            axis=1,
        )
        sorted_wide += jnp.dot(permute, wide, preferred_element_type=F32)
    foot_sorted[:ENT, :] = sorted_wide[:, :128]
    block_sorted[:ENT, :] = sorted_wide[:, 128:]
    to_smem.wait()

    def product(chunk, begin, steps):
        right = movie[pl.ds(chunk * 8, 8)].reshape(8 * VOX, FR)

        def add(step):
            span = pl.ds(pl.multiple_of(begin + step * WINDOW, 8), WINDOW)
            values, which = foot_sorted[span, :], block_sorted[span, :]
            left = jnp.concatenate(
                [
                    jnp.where(which == jnp.asarray(chunk * 8 + n, F32), values, 0.0).astype(BF16)
                    for n in range(8)
                ],
                axis=1,
            )
            projected[span, :] += jnp.dot(left, right, preferred_element_type=F32)

        if isinstance(steps, int):
            add(0)
        else:
            pl.loop(0, steps)(add)

    load.wait()
    windows(begins_s, product)


def windows(begins, product, ahead=None, after=None):
    count = PART // 8
    misfits = begins[0, 127]

    @pl.when(misfits == 0)
    def _():
        for group in range(BLK // PART):
            if ahead is not None:
                ahead(group)
            for chunk in range(group * count, (group + 1) * count):
                product(chunk, (begins[0, chunk] // 8) * 8, 1)
            if after is not None:
                after(group)

    @pl.when(misfits != 0)
    def _():
        if ahead is not None:
            ahead(None)

        @pl.loop(0, BLK // PART)
        def _(group):
            @pl.loop(group * count, (group + 1) * count)
            def _(chunk):
                begin = (begins[0, chunk] // 8) * 8
                steps = (begins[0, chunk + 1] - begin + WINDOW - 1) // WINDOW
                product(chunk, begin, jnp.maximum(1, steps))

            if after is not None:
                after(group)


def gather(movie, footprint, entry_block, entry_owner, entry_slot):
    shape = jax.ShapeDtypeStruct
    in_place = pl.BlockSpec(memory_space=pltpu.HBM)
    return pl.pallas_call(
        gather_kernel,
        out_shape=(
            shape((ENT + WINDOW, FR), F32),
            shape((5, 8, 128), jnp.int32),
            shape((8, ENT), F32),
            shape((8, 128), jnp.int32),
            shape((ENT + WINDOW, VOX), F32),
            shape((ENT + WINDOW, 128), F32),
        ),
        in_specs=[in_place] * 5,
        out_specs=(VMEM,) * 6,
        scratch_shapes=[
            pltpu.VMEM((BLK, VOX, FR), BF16),
            pltpu.VMEM((ENT, VOX), BF16),
            pltpu.VMEM((3, 8, 128), jnp.int32),
            pltpu.SMEM((8, 128), jnp.int32),
            pltpu.SemaphoreType.DMA((6,)),
        ],
        compiler_params=pltpu.CompilerParams(vmem_limit_bytes=48 << 20),
        name="project",
    )(
        *(
            pltpu.with_memory_space_constraint(array, pltpu.HBM)
            for array in (
                movie, footprint, entry_block.reshape(8, 128),
                entry_owner.reshape(8, 128), entry_slot.reshape(8, 128),
            )
        )
    )


def pick(rows, sub):
    chosen = jnp.where(sub // 2 == 0, rows[0:1, :], rows[1:2, :])
    lane = iota((SUB, 128), 1) - lax.rem(sub, 2) * SUB
    column = jnp.sum(jnp.where(lane == iota((SUB, 128), 0), chosen, 0.0), axis=1, keepdims=True)
    return jnp.broadcast_to(column, (SUB, 128))


def delayed(parts, steps):
    if steps >= 128:
        hop = steps // 128
        return [None] * hop + parts[: len(parts) - hop]
    lane = iota((SUB, 128), 1)
    rolled = [pltpu.roll(part, steps, 1) for part in parts]
    out = [jnp.where(lane < steps, 0.0, rolled[0])]
    for index in range(1, len(parts)):
        out.append(jnp.where(lane < steps, rolled[index - 1], rolled[index]))
    return out


def raised(root, count):
    lane = iota(root.shape, 1)
    value, power = jnp.ones_like(root), root
    for level in range(count.bit_length() - 1):
        value = jnp.where((lane >> level) & 1 == 1, value * power, value)
        power = power * power
    return value, power


def running(count):
    row, lane = iota((128, 128), 0), iota((128, 128), 1)
    block = row // count == lane // count
    sums = [jnp.where(block & (row <= lane), 1.0, 0.0), jnp.where(block, 1.0, 0.0)]
    sums = jnp.concatenate(sums, axis=1).astype(BF16)
    return jnp.concatenate([sums] * 3, axis=0)


def first_order(parts, count, sums, value, inverse, power, root):
    rows = parts[0].shape[0]
    last = power / root
    scaled = jnp.concatenate([part * inverse for part in parts], axis=0)
    high = scaled.astype(BF16)
    rest = scaled - high.astype(F32)
    middle = rest.astype(BF16)
    low = (rest - middle.astype(F32)).astype(BF16)
    both = jnp.dot(
        jnp.concatenate([high, middle, low], axis=1), sums, preferred_element_type=F32
    )
    cut = [both[index * rows : (index + 1) * rows] for index in range(len(parts))]
    ends = [piece[:, 128:] * last for piece in cut]
    if count == 128:
        carry = [None, ends[0]]
        for end in ends[1:-1]:
            carry.append(end + power * carry[-1])
    else:
        carry, step = delayed(ends, count), count
        while step < 512:
            moved = delayed(carry, step)
            carry = [
                now if late is None else now + power * late for now, late in zip(carry, moved)
            ]
            step, power = 2 * step, power * power
    after = value * root
    return [
        piece[:, :128] * value if late is None else piece[:, :128] * value + after * late
        for piece, late in zip(cut, carry)
    ]


def sweeps(target, slow, fast):
    lag_one, lag_two = slow + fast, -slow * fast
    settings = []
    for root, count in ((slow, 128), (fast, FAST_BLOCK)):
        value, power = raised(root, count)
        settings.append((count, running(count), value, 1.0 / value, power, root))
    slow_share = slow / (slow - fast)
    fast_share = fast / (slow - fast)
    estimate = target
    for sweep in range(SWEEPS):
        one, two = delayed(estimate, 1), delayed(estimate, 2)
        spikes = [
            jnp.maximum(now - lag_one * a - lag_two * b, 0.0)
            for now, a, b in zip(estimate, one, two)
        ]
        slow_part = first_order(spikes, *settings[0])
        fast_part = first_order(spikes, *settings[1])
        calcium = [slow_share * a - fast_share * b for a, b in zip(slow_part, fast_part)]
        if sweep + 1 < SWEEPS:
            estimate = [0.5 * (a + b) for a, b in zip(target, calcium)]
    return calcium


def exchange_kernel(
    projected, codes, energies, traces, slow, fast, back, calcium, places_out,
    labels, inverse_v, inverse, send, got, hot, part, parts, piece, whole, reply,
    s1, r1, s2, r2, s3, r3, s4, r4, local,
):
    tile, y, z = lax.axis_index("tile"), lax.axis_index("tm"), lax.axis_index("plane")
    x, c = tile // 2, lax.rem(tile, 2)
    d = 1 - c
    p = x * d + z * c
    q = z * d + x * c

    def turn(value, by):
        return lax.rem(value + by, 4)

    def mine(pos, core):
        return (d * (2 * pos + core) + c * (2 * x + core), y, d * z + c * pos)

    def other(pos):
        return (c * 2 * pos + d * (2 * x + 1), y, c * z + d * pos)

    def column(pos, frame):
        return (d * 2 * x + c * (2 * pos + 1), frame, d * pos + c * z)

    reach = TURNS[:3]
    barrier = pltpu.get_barrier_semaphore()
    met = [mine(turn(p, by), c) for by in reach]
    met += [mine(turn(p, by), d) for by in TURNS]
    met += [other(turn(q, by)) for by in reach]
    met += [column(turn(q, dq), turn(y, dy)) for dq in TURNS for dy in TURNS if dq or dy]
    for device in met:
        pl.semaphore_signal(barrier, inc=1, device_id=device, device_id_type=MESH)
    meta = jnp.zeros((40, 512), F32)
    for row in range(8):
        message_of, place_in, sorted_at, _, slots = [
            codes[number, row : row + 1, :] for number in range(5)
        ]
        chosen = message_of == iota((8, 128), 0)
        en_high, en_low = split(energies[:, row * 128 : row * 128 + 128])
        sorted_at = sorted_at + 1
        values = [
            jnp.where(chosen, value.astype(F32), 0.0)
            for value in (slots + 1, en_high, en_low, sorted_at >> 5, sorted_at & 31)
        ]
        spots = jnp.where(place_in == iota((512, 128), 0), 1.0, 0.0).astype(BF16)
        meta += lax.dot_general(
            jnp.concatenate(values, axis=0).astype(BF16), spots, NT, preferred_element_type=F32
        )
    place_of = (meta[24:32, :] * 32.0 + meta[32:40, :]).astype(jnp.int32)
    place_of = jnp.where(place_of == 0, ENT, jnp.clip(place_of - 1, 0, ENT))
    weights = meta[8:16, :] + meta[16:24, :]
    for i in range(4):
        lanes = slice(i * 128, i * 128 + 128)
        inverse_v[i] = place_of[:, lanes]
        labels[:, i, :] = meta[:8, lanes]
        labels[:, 4 + i, :] = weights[:, lanes]
    to_smem = pltpu.make_async_copy(inverse_v, inverse, local.at[0])
    to_smem.start()
    for index in range(8):
        send[index * ROWS : index * ROWS + 8, :] = labels[index]

    def place(section):
        @pl.loop(0, 8)
        def _(index):
            first = pl.multiple_of(index * ROWS + 8 + CAP * section, 8)
            for block in range(0, CAP, 8):
                rows = [
                    projected[pl.ds(inverse[section, index, block + row], 1), :] for row in range(8)
                ]
                send[pl.ds(first + block, 8), :] = jnp.concatenate(rows, axis=0)

    to_smem.wait()
    place(0)
    pl.semaphore_wait(barrier, len(met))

    def remote(source, target, sends, arrives, device):
        return pltpu.make_async_remote_copy(
            src_ref=source, dst_ref=target, send_sem=sends, recv_sem=arrives,
            device_id=device, device_id_type=MESH,
        )

    def rows_of(section):
        return (0, 8 + CAP) if section == 0 else (8 + CAP * section, CAP)

    def message(index, section):
        first, count = rows_of(section)
        return send.at[pl.ds(pl.multiple_of(index * ROWS + first, 8), count), :]

    def landing(index, section):
        first, count = rows_of(section)
        return got.at[index, pl.ds(first, count), :]

    started = []

    def start(copy):
        copy.start()
        started.append(copy)

    def send_section(section):
        for by in TURNS:
            if by:
                index = c * 4 + turn(p, by)
                start(
                    remote(
                        message(index, section), landing(p * 2 + c, section),
                        s1.at[index * 4 + section], r1.at[(p * 2 + c) * 4 + section],
                        mine(turn(p, by), c),
                    )
                )
            index = d * 4 + turn(q, by)
            start(
                remote(
                    message(index, section), landing(q * 2 + c, section),
                    s1.at[index * 4 + section], r1.at[(q * 2 + c) * 4 + section],
                    other(turn(q, by)),
                )
            )

    for section in range(4):
        if section:
            place(section)
        if section >= 2:
            for copy in started[(section - 2) * 7 : (section - 1) * 7]:
                copy.wait_send()
        send_section(section)

    slots_iota = (iota((OWN, 128), 0) + 1).astype(F32)
    ones = jnp.ones((8, 128), BF16)
    blank = jnp.zeros((128 - CAP, FR), BF16)
    top = iota((8, 128), 0) == 0
    sources = [(0, 0), (0, 1), (1, 0), (1, 1), (3, 0), (3, 1), (2, 0), (2, 1)]
    for section in range(4):
        weight = jnp.zeros((OWN, 128), F32)
        lefts, rights = [], []
        first = 8 + CAP * section
        for by, flip in sources[1:]:
            source = turn(p, by) * 2 + (d if flip else c)
            remote(
                message(0, section), landing(source, section), s1.at[0],
                r1.at[source * 4 + section], mine(turn(p, by), c),
            ).wait_recv()
        for place_in, (by, flip) in enumerate(sources):
            if by or flip:
                source = turn(p, by) * 2 + (d if flip else c)
                slots = got[source, section : section + 1, :]
                energies = got[source, 4 + section : 5 + section, :]
                values = got[source, first : first + CAP, :]
            else:
                base = (c * 4 + p) * ROWS
                slots = labels[c * 4 + p, section : section + 1, :]
                energies = labels[c * 4 + p, 4 + section : 5 + section, :]
                values = send[pl.ds(pl.multiple_of(base + first, 8), CAP), :]
            match = slots_iota == slots
            chosen = jnp.where(match, 1.0, 0.0)
            hot[section, place_in * CAP : (place_in + 1) * CAP, :] = chosen.T[:CAP, :].astype(BF16)
            weight = weight + jnp.where(match, energies, 0.0)
            high, low = split(values)
            chosen = chosen.astype(BF16)
            lefts += [chosen, chosen]
            rights += [high, blank, low, blank]
        total = jnp.dot(
            jnp.concatenate(lefts, axis=1),
            jnp.concatenate(rights, axis=0),
            preferred_element_type=F32,
        )
        if section == 3:
            total = total + traces[...]
        high, low = split(weight)
        energy = lax.dot_general(ones, high, NT, preferred_element_type=F32) + lax.dot_general(
            ones, low, NT, preferred_element_type=F32
        )
        energy = jnp.where(top, energy[:, :128], energy[:, 128:])
        for sub in range(4):
            part[section, sub, :SUB, :] = total[sub * SUB : (sub + 1) * SUB, :]
            part[section, sub, SUB:, :] = energy
        tq = turn(q, TURNS[section])
        for dy in TURNS:
            ty = turn(y, dy)
            if section == 3 and dy == 0:
                own = pltpu.make_async_copy(part.at[section, y], parts.at[q, y], local.at[1])
                own.start()
            else:
                count = SUB if dy else PIECE
                start(
                    remote(
                        part.at[section, ty, pl.ds(0, count)], parts.at[q, y, pl.ds(0, count)],
                        s2.at[section * 4 + dy], r2.at[q * 4 + y], column(tq, ty),
                    )
                )
    sorted_pos = jnp.zeros((16, ENT), F32)
    for row in range(8):
        sorted_at, pos = codes[2, row : row + 1, :], codes[3, row : row + 1, :]
        permute = jnp.where(sorted_at == iota((ENT, 128), 0), 1.0, 0.0).astype(BF16)
        halves = [
            jnp.broadcast_to(part_of, (8, 128)).astype(F32) for part_of in (pos >> 5, pos & 31)
        ]
        sorted_pos += lax.dot_general(
            jnp.concatenate(halves, axis=0).astype(BF16), permute, NT, preferred_element_type=F32
        )
    sorted_pos = (sorted_pos[:8, :] * 32.0 + sorted_pos[8:, :]).astype(jnp.int32)
    for row in range(8):
        places_out[row : row + 1, :] = sorted_pos[:1, row * 128 : (row + 1) * 128]
    own.wait()
    for dq in TURNS:
        for dy in TURNS:
            if dq or dy:
                fq, fy = turn(q, dq), turn(y, dy)
                count = SUB if dy else PIECE
                remote(
                    part.at[0, 0, pl.ds(0, count)], parts.at[fq, fy, pl.ds(0, count)], s2.at[0],
                    r2.at[fq * 4 + fy], column(fq, fy),
                ).wait_recv()
    energy = parts[0, y, SUB : SUB + 2, :]
    for other_q in range(1, 4):
        energy = energy + parts[other_q, y, SUB : SUB + 2, :]
    scale = 1.0 / (pick(energy, y) + 1.0)
    target = []
    for frame in range(4):
        total = parts[0, frame, :SUB, :]
        for other_q in range(1, 4):
            total = total + parts[other_q, frame, :SUB, :]
        target.append(total * scale)
    traced = sweeps(target, pick(slow[...], y), pick(fast[...], y))
    for frame in range(4):
        piece[frame] = traced[frame]

    for section in (3, 1, 2, 0):
        tq = turn(q, TURNS[section])
        for dy in TURNS:
            ty = turn(y, dy)
            if section == 3 and dy == 0:
                own = pltpu.make_async_copy(piece.at[y], whole.at[q, y], local.at[2])
                own.start()
            else:
                start(
                    remote(
                        piece.at[ty], whole.at[q, y], s3.at[section * 4 + dy], r3.at[q * 4 + y],
                        column(tq, ty),
                    )
                )
    own.wait()

    def answer(index, section):
        return back.at[pl.ds(pl.multiple_of(index * ROWS + 8 + CAP * section, 8), CAP), :]

    for section in (3, 1, 2, 0):
        fq = turn(q, TURNS[section])
        for dy in TURNS:
            if section != 3 or dy:
                fy = turn(y, dy)
                remote(
                    piece.at[0], whole.at[fq, fy], s3.at[0], r3.at[fq * 4 + fy], column(fq, fy)
                ).wait_recv()
        if section == 3:
            for sub in range(4):
                calcium[sub * SUB : (sub + 1) * SUB, :] = whole[q, sub]
        rows = whole[fq].reshape(OWN, FR).astype(BF16)
        reply[section] = jnp.dot(hot[section], rows, preferred_element_type=F32)
        for order in range(7, -1, -1):
            by, flip = sources[order]
            core = d if flip else c
            if by or flip:
                start(
                    remote(
                        reply.at[section, pl.ds(order * CAP, CAP)], answer(c * 4 + p, section),
                        s4.at[order * 4 + section], r4.at[(c * 4 + p) * 4 + section],
                        mine(turn(p, by), core),
                    )
                )
            else:
                own = pltpu.make_async_copy(
                    reply.at[section, pl.ds(order * CAP, CAP)], answer(c * 4 + p, section),
                    local.at[3 + section],
                )
                own.start()
                started.append(own)
    for section in (3, 1, 2, 0):
        for by in TURNS[::-1]:
            for core, pos in ((d, turn(q, by)), (c, turn(p, by))):
                if by == 0 and core is c:
                    continue
                index = core * 4 + pos
                remote(
                    reply.at[0, pl.ds(0, CAP)], answer(index, section), s4.at[0], r4.at[index * 4 + section],
                    other(q),
                ).wait_recv()
    for copy in started[14:]:
        if copy.is_remote:
            copy.wait_send()
        else:
            copy.wait()


def exchange(projected, codes, energies, traces, slow_root, fast_root):
    dma = pltpu.SemaphoreType.DMA
    return pl.pallas_call(
        exchange_kernel,
        out_shape=(
            jax.ShapeDtypeStruct((8 * ROWS, FR), F32),
            jax.ShapeDtypeStruct((OWN, FR), F32),
            jax.ShapeDtypeStruct((8, 128), jnp.int32),
        ),
        in_specs=[VMEM] * 6,
        out_specs=(VMEM, VMEM, VMEM),
        scratch_shapes=[
            pltpu.VMEM((8, 8, 128), F32),
            pltpu.VMEM((4, 8, 128), jnp.int32),
            pltpu.SMEM((4, 8, 128), jnp.int32),
            pltpu.VMEM((8 * ROWS, FR), F32),
            pltpu.VMEM((8, ROWS, FR), F32),
            pltpu.VMEM((4, 8 * CAP, OWN), BF16),
            pltpu.VMEM((4, 4, PIECE, FR), F32),
            pltpu.VMEM((4, 4, PIECE, FR), F32),
            pltpu.VMEM((4, SUB, FR), F32),
            pltpu.VMEM((4, 4, SUB, FR), F32),
            pltpu.VMEM((4, 8 * CAP, FR), F32),
            dma((32,)), dma((32,)), dma((16,)), dma((16,)),
            dma((16,)), dma((16,)), dma((32,)), dma((32,)), dma((7,)),
        ],
        compiler_params=pltpu.CompilerParams(
            collective_id=1, has_side_effects=True, vmem_limit_bytes=48 << 20
        ),
        name="exchange",
    )(projected, codes, energies, traces, slow_root.reshape(2, 128), fast_root.reshape(2, 128))


def rebuild_kernel(
    begins_v, places_v, back, foot, block, calcium, out_hbm, calcium_out,
    begins, places, rows, out, total, sem,
):
    to_smem = [
        pltpu.make_async_copy(source, target, sem.at[BLK // PART + number])
        for number, (source, target) in enumerate([(begins_v, begins), (places_v, places)])
    ]
    for copy in to_smem:
        copy.start()
    calcium_out[...] = calcium[...]
    rows[ENT:, :] = jnp.zeros((WINDOW, FR), F32)
    for copy in to_smem:
        copy.wait()

    def stage(group):
        if group is None:

            @pl.loop(0, ENT // 128)
            def _(line):
                for lane in range(128):
                    rows[pl.ds(line * 128 + lane, 1), :] = back[pl.ds(places[line, lane], 1), :]

        elif group % 2 == 0:
            number = group // 2
            for row in range(STAGES[number - 1] if number else 0, STAGES[number]):
                rows[row : row + 1, :] = back[pl.ds(places[row // 128, row % 128], 1), :]

    def term(chunk, first):
        span = pl.ds(pl.multiple_of(first, 8), WINDOW)
        values, which = rows[span, :], block[span, :]
        masked = jnp.concatenate(
            [
                jnp.where(which == jnp.asarray(chunk * 8 + n, F32), values, 0.0).astype(BF16)
                for n in range(8)
            ],
            axis=1,
        )
        left = foot[span, :].astype(BF16)
        return lax.dot_general(left, masked, TN, preferred_element_type=F32)

    def out_part(number):
        span = pl.ds(number * PART, PART)
        return pltpu.make_async_copy(out.at[span], out_hbm.at[span], sem.at[number])

    def product(chunk, begin, steps):
        result = term(chunk, begin)
        if not isinstance(steps, int):
            total[...] = result

            @pl.loop(1, steps)
            def _(step):
                total[...] += term(chunk, begin + step * WINDOW)

            result = total[...]
        for n in range(8):
            out[chunk * 8 + n] = result[:, n * FR : (n + 1) * FR].astype(BF16)

    windows(begins, product, stage, lambda group: out_part(group).start())

    @pl.loop(0, BLK // PART)
    def _(group):
        out_part(group).wait()


def rebuild(begins, places, back, foot, block, calcium):
    return pl.pallas_call(
        rebuild_kernel,
        out_shape=(
            jax.ShapeDtypeStruct((BLK, VOX, FR), BF16),
            jax.ShapeDtypeStruct((OWN, FR), F32),
        ),
        in_specs=[VMEM] * 6,
        out_specs=(pl.BlockSpec(memory_space=pl.ANY), VMEM),
        scratch_shapes=[
            pltpu.SMEM((8, 128), jnp.int32),
            pltpu.SMEM((8, 128), jnp.int32),
            pltpu.VMEM((ENT + WINDOW, FR), F32),
            pltpu.VMEM((BLK, VOX, FR), BF16),
            pltpu.VMEM((VOX, 8 * FR), F32),
            pltpu.SemaphoreType.DMA((BLK // PART + 2,)),
        ],
        compiler_params=pltpu.CompilerParams(vmem_limit_bytes=48 << 20),
        name="rebuild",
    )(begins, places, back, foot, block, calcium)


def shards(movie, footprint, entry_block, entry_owner, entry_slot, traces, slow_root, fast_root):
    projected, codes, energies, begins, foot, block = gather(
        movie, footprint, entry_block, entry_owner, entry_slot
    )
    back, calcium, places = exchange(projected, codes, energies, traces, slow_root, fast_root)
    return rebuild(begins, places, back, foot, block, calcium)


def solution(mesh):
    owners = ("tile", "plane")
    placed = (
        P(owners, None, "tm"),
        P(owners, None),
        P(owners),
        P(owners, None),
        P(owners),
        P(owners, "tm"),
        P(owners),
        P(owners),
    )
    return jax.shard_map(
        shards,
        mesh=mesh,
        in_specs=placed,
        out_specs=(P(owners, None, "tm"), P(owners, "tm")),
        check_vma=False,
    )
```
